512 devices in a mesh: gx: 32 (over y_hi, x, core), gy: 16 (over y_lo, z).
Axes of the slice: x: 4, y: 8 (y_hi: 4, y_lo: 2; y = y_hi * 2 + y_lo), z: 8, core: 2. Of those that a mesh axis runs over, the one named last changes fastest.
Arguments:
- source: float32 [4, 512, 512, 128], P(None, 'gx', 'gy'), may hold values from -6 to 6
- conduct_fine: float32 [512, 512, 128], P('gx', 'gy'), may hold values from 0.05 to 0.3
- conduct_second: float32 [256, 256, 64], P('gx', 'gy'), may hold values from 0.05 to 0.3
- conduct_third: float32 [128, 128, 32], P('gx', 'gy'), may hold values from 0.05 to 0.3
- conduct_coarse: float32 [64, 64, 16], P('gx', 'gy'), may hold values from 0.05 to 0.3
- mixers: float32 [4, 4, 4], replicated, may hold values from -1.5 to 1.5
- smoothers: float32 [4, 4, 4], replicated, may hold values from -0.75 to 0.75
Outputs:
- solution: float32 [4, 512, 512, 128], P(None, 'gx', 'gy')
The draws below stay inside these ranges and needn't reach their ends.
All inputs are finite; a program needn't handle non-finite values.
Results may differ from the reference program's by a relative error of at most 0.00011.
Values sent between devices are 32-bit elements; how exact they have to be, the bound alone decides.
A program may use at most 128 MiB of HBM per device.

```python
import math
import jax
import jax.numpy as jnp
from jax import lax

CHANNELS = 4
LEVELS = 4
SWEEPS = 3
NZ = 128
NX = 512
NY = 512


def block_scale(rng, dims, split, smallest, largest):
    loudness = 1.0
    for position, shards_of in split:
        steps = jax.random.uniform(jax.random.fold_in(jax.random.fold_in(rng, 6), position), (shards_of,), jnp.float32, smallest / len(split), largest / len(split))
        loudness = loudness * jnp.repeat(jnp.exp(steps), dims[position] // shards_of).reshape((-1,) + (1,) * (len(dims) - 1 - position))
    return loudness


def scatter_about(own_key, extent, scale, most, cuts=(), kind=jnp.bfloat16):
    result = scale * jax.random.normal(own_key, extent, jnp.float32)
    if cuts:
        result = result * block_scale(own_key, extent, cuts, -0.22, 0.18)
    return jnp.clip(result, -most, most).astype(kind)


def setup_inputs(seed: int = 0) -> dict:
    key_list = jax.random.split(jax.random.key(seed), 8)
    return {
        "source": scatter_about(key_list[0], (CHANNELS, NX, NY, NZ), 1.0, 6.0, ((1, 32), (2, 16)), jnp.float32),
        "conduct_fine": jnp.clip(jnp.exp(math.log(0.3) - 1.7917595 * jax.random.uniform(key_list[1], (NX, NY, NZ), jnp.float32) ** block_scale(key_list[1], (NX, NY, NZ), ((0, 32), (1, 16)), -0.2, 0.2)), 0.05, 0.3),
        "conduct_second": jnp.clip(jnp.exp(math.log(0.3) - 1.7917595 * jax.random.uniform(key_list[2], (NX // 2, NY // 2, NZ // 2), jnp.float32) ** block_scale(key_list[2], (NX // 2, NY // 2, NZ // 2), ((0, 32), (1, 16)), -0.2, 0.2)), 0.05, 0.3),
        "conduct_third": jnp.clip(jnp.exp(math.log(0.3) - 1.7917595 * jax.random.uniform(key_list[3], (NX // 4, NY // 4, NZ // 4), jnp.float32) ** block_scale(key_list[3], (NX // 4, NY // 4, NZ // 4), ((0, 32), (1, 16)), -0.2, 0.2)), 0.05, 0.3),
        "conduct_coarse": jnp.clip(jnp.exp(math.log(0.3) - 1.7917595 * jax.random.uniform(key_list[4], (NX // 8, NY // 8, NZ // 8), jnp.float32) ** block_scale(key_list[4], (NX // 8, NY // 8, NZ // 8), ((0, 32), (1, 16)), -0.2, 0.2)), 0.05, 0.3),
        "mixers": scatter_about(key_list[5], (LEVELS, CHANNELS, CHANNELS), 16 ** -0.5, 1.5, (), jnp.float32),
        "smoothers": scatter_about(key_list[6], (LEVELS, CHANNELS, CHANNELS), 64 ** -0.5, 0.75, (), jnp.float32),
    }


def mixing(matrix, field):
    return jnp.einsum('ij,jxyz->ixyz', matrix, field, precision=lax.Precision.HIGHEST)

def stencil(padded, coefficient):
    center = padded[:, 1:-1, 1:-1, 1:-1]
    beside_all = padded[:, 2:, 1:-1, 1:-1] + padded[:, :-2, 1:-1, 1:-1]
    beside_all = beside_all + padded[:, 1:-1, 2:, 1:-1] + padded[:, 1:-1, :-2, 1:-1]
    beside_all = beside_all + padded[:, 1:-1, 1:-1, 2:] + padded[:, 1:-1, 1:-1, :-2]
    return coefficient * (6.0 * center - beside_all) + center

def operate(field, coefficient, mixer):
    padded = jnp.pad(field, ((0, 0), (1, 1), (1, 1), (1, 1)))
    identity = jnp.eye(field.shape[0], dtype=jnp.float32)
    return mixing(identity + mixer, stencil(padded, coefficient))

def restrict(field):
    channels, extent_x, extent_y, extent_z = field.shape
    blocks = field.reshape(channels, extent_x // 2, 2, extent_y // 2, 2, extent_z // 2, 2)
    return blocks.mean(axis=(2, 4, 6))

def prolong(field):
    return jnp.repeat(jnp.repeat(jnp.repeat(field, 2, 1), 2, 2), 2, 3)

def line_term(field):
    return field + 4.0 / math.sqrt(field.shape[2]) * lax.optimization_barrier(jnp.sum(field, axis=2, keepdims=True))

def reference(source, conduct_fine, conduct_second, conduct_third, conduct_coarse, mixers, smoothers):
    identity = jnp.eye(source.shape[0], dtype=jnp.float32)
    coefficients = [conduct_fine, conduct_second, conduct_third, conduct_coarse]
    sources = [source]
    smoothed = []
    for level_index in range(LEVELS - 1):
        smoother = 0.25 * identity + smoothers[level_index]
        forcing = sources[level_index]
        coefficient = coefficients[level_index]
        mixer = mixers[level_index]
        field = mixing(smoother, forcing)
        field = field + mixing(smoother, forcing - operate(field, coefficient, mixer))
        sources.append(restrict(forcing - operate(field, coefficient, mixer)))
        smoothed.append(field)
    smoother = 0.25 * identity + smoothers[LEVELS - 1]
    forcing = sources[LEVELS - 1]
    field = line_term(mixing(smoother, forcing))
    for sweep_index in range(SWEEPS):
        field = field + mixing(smoother, forcing - operate(field, conduct_coarse, mixers[LEVELS - 1]))
    for level_index in range(LEVELS - 2, -1, -1):
        smoother = 0.25 * identity + smoothers[level_index]
        update = smoothed[level_index] + prolong(field)
        field = update + mixing(smoother, sources[level_index] - operate(update, coefficients[level_index], mixers[level_index]))
    return field
```

```python
import functools
import math

import jax
import jax.numpy as jnp
from jax import lax
from jax.experimental import pallas as pl
from jax.experimental.pallas import tpu as pltpu
from jax.sharding import PartitionSpec as P

MESH = pl.DeviceIdType.MESH
F32 = jnp.float32
BF16 = jnp.bfloat16
LANES = 128
PAD = 8


def spread(field, matrix):
    high = field.astype(BF16)
    low = (field - high.astype(F32)).astype(BF16)
    return jnp.dot(high, matrix, preferred_element_type=F32) + jnp.dot(
        low, matrix, preferred_element_type=F32
    )


def lane_index(shape):
    return lax.broadcasted_iota(jnp.int32, shape, len(shape) - 1)


def beside_z(field, segment):
    lane = lane_index((1, LANES)) % segment
    axis = field.ndim - 1
    before = jnp.where(lane == 0, 0.0, pltpu.roll(field, 1, axis))
    after = jnp.where(lane == segment - 1, 0.0, pltpu.roll(field, LANES - 1, axis))
    return before + after


def stencil(center, beside, coefficient, segment):
    total = beside + beside_z(center, segment)
    return coefficient * (6.0 * center - total) + center


def kernel(
    nx, ny,
    source, fine, second, third, coarse, mixers, smoothers, out,
    f0, g0, v0, r0, q0, s0, p0, c0,
    a1, f1, g1, v1, r1, q1, w1, s1, p1, c1,
    a2, f2, g2, v2, r2, q2, w2, s2, p2, c2,
    a3, r3, g3, w3, b3, s3, p3, line, lines,
    table, down, up, last_down, last_up,
    send_sem, recv_sem, local_sem, out_sem,
):
    mx, my = lax.axis_index("gx"), lax.axis_index("gy")

    def device(dx, dy):
        return (lax.rem(mx + (dx + nx), nx), lax.rem(my + (dy + ny), ny))

    barrier = pltpu.get_barrier_semaphore()
    peers = [(0, k) for k in range(1, ny)]
    peers += [(dx, dy) for dx in (-1, 1) for dy in (-1, 0, 1)] + [(-2, 0), (2, 0)]
    for dx, dy in peers:
        pl.semaphore_signal(barrier, inc=1, device_id=device(dx, dy), device_id_type=MESH)

    x0, y0 = f0.shape[1:3]
    x1, y1 = f1.shape[1:3]
    x2, y2 = f2.shape[:2]
    x3, y3 = a3.shape[:2]
    loads = [
        pltpu.make_async_copy(source, f0, local_sem.at[0]),
        pltpu.make_async_copy(fine, g0.at[4, pl.ds(2, x0), pl.ds(PAD, y0)], local_sem.at[1]),
        pltpu.make_async_copy(second, a1, local_sem.at[2]),
        pltpu.make_async_copy(third, a2, local_sem.at[3]),
        pltpu.make_async_copy(coarse, a3, local_sem.at[4]),
    ]
    for load in loads:
        load.start()

    def smooth_matrix(level):
        return [
            [smoothers[level, i, j] + (0.25 if i == j else 0.0) for j in range(4)]
            for i in range(4)
        ]

    def mix_matrix(level):
        return [
            [mixers[level, i, j] + (1.0 if i == j else 0.0) for j in range(4)] for i in range(4)
        ]

    def product(left, right):
        return [
            [sum(left[i][k] * right[k][j] for k in range(4)) for j in range(4)] for i in range(4)
        ]

    lane = lane_index((1, LANES))
    rows_used = [0]

    def keep(vector):
        row = rows_used[0]
        rows_used[0] += 1
        table[row : row + 1, :] = vector
        return row

    def pair_rows(matrix):
        return [
            [
                [
                    keep(
                        jnp.where(
                            lane < 64,
                            matrix[2 * g][2 * h + s],
                            matrix[2 * g + 1][2 * h + 1 - s],
                        )
                    )
                    for s in range(2)
                ]
                for h in range(2)
            ]
            for g in range(2)
        ]

    def quad_rows(matrix, segment):
        channel = (lane // segment) % 4
        rows = []
        for k in range(4):
            vector = jnp.zeros((1, LANES), F32)
            for i in range(4):
                vector = jnp.where(channel == i, matrix[i][(i - k) % 4], vector)
            rows.append(keep(vector))
        return rows

    S0, B0 = smooth_matrix(0), mix_matrix(0)
    T0 = product(S0, B0)
    smooth1, mixer1 = smooth_matrix(1), mix_matrix(1)
    S1, B1, T1 = pair_rows(smooth1), pair_rows(mixer1), pair_rows(product(smooth1, mixer1))
    smooth2, mixer2 = smooth_matrix(2), mix_matrix(2)
    S2, B2 = quad_rows(smooth2, 32), quad_rows(mixer2, 32)
    T2 = quad_rows(product(smooth2, mixer2), 32)
    smooth3, mixer3 = smooth_matrix(3), mix_matrix(3)
    S3, T3 = quad_rows(smooth3, 16), quad_rows(product(smooth3, mixer3), 16)

    def mixed4(matrix, fields):
        return [
            matrix[i][0] * fields[0]
            + matrix[i][1] * fields[1]
            + (matrix[i][2] * fields[2] + matrix[i][3] * fields[3])
            for i in range(4)
        ]

    def vector_of(row):
        return table[row : row + 1, :]

    def mixed2(rows, fields):
        turned = [pltpu.roll(field, 64, field.ndim - 1) for field in fields]
        return [
            vector_of(rows[g][0][0]) * fields[0]
            + vector_of(rows[g][0][1]) * turned[0]
            + (vector_of(rows[g][1][0]) * fields[1] + vector_of(rows[g][1][1]) * turned[1])
            for g in range(2)
        ]

    def mixed1(rows, field, segment):
        total = vector_of(rows[0]) * field
        for k in range(1, 4):
            total += vector_of(rows[k]) * pltpu.roll(field, k * segment, field.ndim - 1)
        return total

    wide, narrow = (2 * LANES, LANES), (LANES, LANES)

    def row_index(shape):
        return lax.broadcasted_iota(jnp.int32, shape, 0)

    down[...] = jnp.where(row_index(wide) // 2 == lane_index(wide), 0.125, 0.0).astype(BF16)
    up[...] = jnp.where(
        lane_index((LANES, 2 * LANES)) // 2 == row_index((LANES, 2 * LANES)), 1.0, 0.0
    ).astype(BF16)
    last_down[...] = jnp.where(
        row_index(narrow) // 2 == lane_index(narrow) % 64, 0.125, 0.0
    ).astype(BF16)
    last_up[...] = jnp.where(lane_index(narrow) // 2 == row_index(narrow), 1.0, 0.0).astype(BF16)

    started = []

    def send(src, dst, place):
        number = len(started)
        copy = pltpu.make_async_remote_copy(
            src_ref=src, dst_ref=dst, send_sem=send_sem.at[number], recv_sem=recv_sem.at[number],
            device_id=device(*place), device_id_type=MESH,
        )
        copy.start()
        started.append(copy)
        return copy

    def pack(g, s, planes, h, xs, ys):
        for p, (k, c) in enumerate(planes):
            s[0, p, 0:xs, :] = g[c, h : h + xs, PAD + k, :]
            s[1, p, 0:xs, :] = g[c, h : h + xs, PAD + ys - 1 - k, :]

    def exchange(g, s, p, corner, h, xs, ys, near):
        own = pl.ds(PAD, ys)
        copies = [
            send(g.at[:, pl.ds(xs, h), own], g.at[:, pl.ds(0, h), own], (1, 0)),
            send(g.at[:, pl.ds(h, h), own], g.at[:, pl.ds(xs + h, h), own], (-1, 0)),
            send(s.at[1], p.at[0], (0, 1)),
            send(s.at[0], p.at[1], (0, -1)),
        ]
        first, last = pl.ds(0, 8), pl.ds(max(xs - 8, 0), 8)
        for side, dy in ((1, 1), (0, -1)):
            for end, dx in ((last, 1), (first, -1)):
                copies.append(
                    send(
                        s.at[side, pl.ds(0, near), end],
                        corner.at[(0 if dx > 0 else 1) * 2 + (0 if dy > 0 else 1)],
                        (dx, dy),
                    )
                )
        return copies

    def unpack(copies, g, p, corner, planes, h, xs, ys, near, reach, a_reach):
        for copy in copies:
            copy.wait_recv()
        groups = g.shape[0]
        for n, (k, c) in enumerate(planes):
            g[c, h : h + xs, PAD - 1 - k, :] = p[0, n, 0:xs, :]
            g[c, h : h + xs, PAD + ys + k, :] = p[1, n, 0:xs, :]
        top = min(xs, 8) - 1
        for n, (k, c) in enumerate(planes[:near]):
            for i in range((a_reach if c == groups - 1 else reach) - 1 - k):
                for from_dy in range(2):
                    row = PAD - 1 - k if from_dy == 0 else PAD + ys + k
                    g[c, h - 1 - i, row : row + 1, :] = corner[from_dy, n, top - i : top - i + 1, :]
                    g[c, h + xs + i, row : row + 1, :] = corner[2 + from_dy, n, i : i + 1, :]

        @pl.when(mx == 0)
        def _():
            g[:, 0:h] = jnp.zeros((groups, h) + g.shape[2:], F32)

        @pl.when(mx == nx - 1)
        def _():
            g[:, h + xs :] = jnp.zeros((groups, h) + g.shape[2:], F32)

        @pl.when(my == 0)
        def _():
            g[:, :, 0:PAD] = jnp.zeros(g.shape[:2] + (PAD, LANES), F32)

        @pl.when(my == ny - 1)
        def _():
            g[:, :, PAD + ys :] = jnp.zeros(g.shape[:2] + (PAD, LANES), F32)

    def steps(count, body):
        def step(i, carry):
            body(i)
            return carry

        lax.fori_loop(0, count, step, 0)

    def stencil_of(field, coefficient, c, x, row, rows, segment):
        center = field[c, x, row : row + rows, :]
        beside = field[c, x - 1, row : row + rows, :] + field[c, x + 1, row : row + rows, :]
        beside += field[c, x, row - 1 : row - 1 + rows, :]
        beside += field[c, x, row + 1 : row + 1 + rows, :]
        return stencil(center, beside, coefficient, segment)

    for load in loads:
        load.wait()

    def smooth_fine(x):
        fields = mixed4(S0, [f0[c, x] for c in range(4)])
        for c in range(4):
            g0[c, x + 2, PAD : PAD + y0, :] = fields[c]

    steps(x0, smooth_fine)
    planes0 = [(0, 0), (0, 1), (0, 2), (0, 3), (0, 4), (1, 0), (1, 1), (1, 2), (1, 3)]
    pack(g0, s0, planes0, 2, x0, y0)
    pl.semaphore_wait(barrier, len(peers))
    copies = exchange(g0, s0, p0, c0, 2, x0, y0, 4)

    g1[2, 3 : 3 + x1, PAD : PAD + y1, :] = jnp.concatenate([a1[...]] * 2, axis=-1)
    g2[1, 3 : 3 + x2, PAD : PAD + y2, :] = jnp.concatenate([a2[...]] * 4, axis=-1)
    g3[1, 4 : 4 + x3, PAD : PAD + y3, :] = jnp.concatenate([a3[...]] * 8, axis=-1)
    unpack(copies, g0, p0, c0, planes0, 2, x0, y0, 4, 2, 1)

    def relax_fine(step):
        x = step + 1
        row, rows = PAD - 1, y0 + 2
        coefficient = g0[4, x, row : row + rows, :]
        change = mixed4(T0, [stencil_of(g0, coefficient, c, x, row, rows, LANES) for c in range(4)])
        for c in range(4):
            v0[c, x, row : row + rows, :] = 2.0 * g0[c, x, row : row + rows, :] - change[c]

    steps(x0 + 2, relax_fine)

    def residual_fine(i):
        total = [None] * 4
        for s in range(2):
            x = 2 * i + s
            coefficient = g0[4, x + 2, PAD : PAD + y0, :]
            applied = mixed4(
                B0, [stencil_of(v0, coefficient, c, x + 2, PAD, y0, LANES) for c in range(4)]
            )
            for c in range(4):
                rest = f0[c, x] - applied[c]
                total[c] = rest if s == 0 else total[c] + rest
        for c in range(4):
            r0[c, i] = total[c]

    steps(x1, residual_fine)

    for g in range(2):
        pieces = [
            r0[c, :, pl.ds(0, y1, stride=2), :] + r0[c, :, pl.ds(1, y1, stride=2), :]
            for c in (2 * g, 2 * g + 1)
        ]
        joined = jnp.concatenate([piece.reshape(x1 * y1, LANES) for piece in pieces], axis=-1)
        f1[g] = spread(joined, down[...]).reshape(x1, y1, LANES)
    fields = mixed2(S1, [f1[g] for g in range(2)])
    for g in range(2):
        g1[g, 3 : 3 + x1, PAD : PAD + y1, :] = fields[g]
    planes1 = [(0, 0), (0, 1), (0, 2), (1, 0), (1, 1), (1, 2), (2, 0), (2, 1)]
    pack(g1, s1, planes1, 3, x1, y1)
    copies = exchange(g1, s1, p1, c1, 3, x1, y1, 5)
    unpack(copies, g1, p1, c1, planes1, 3, x1, y1, 5, 3, 2)

    def relax_second(step):
        x = step + 1
        row, rows = PAD - 2, y1 + 4
        coefficient = g1[2, x, row : row + rows, :]
        change = mixed2(T1, [stencil_of(g1, coefficient, c, x, row, rows, 64) for c in range(2)])
        for c in range(2):
            v1[c, x, row : row + rows, :] = 2.0 * g1[c, x, row : row + rows, :] - change[c]

    steps(x1 + 4, relax_second)

    def residual_second(i):
        total = [None] * 2
        for s in range(2):
            x = 2 * i + s
            coefficient = g1[2, x + 3, PAD : PAD + y1, :]
            applied = mixed2(
                B1, [stencil_of(v1, coefficient, c, x + 3, PAD, y1, 64) for c in range(2)]
            )
            for c in range(2):
                rest = f1[c, x] - applied[c]
                total[c] = rest if s == 0 else total[c] + rest
        for c in range(2):
            r1[c, i] = total[c]

    steps(x2, residual_second)

    pieces = [
        r1[c, :, pl.ds(0, y2, stride=2), :] + r1[c, :, pl.ds(1, y2, stride=2), :] for c in range(2)
    ]
    joined = jnp.concatenate([piece.reshape(x2 * y2, LANES) for piece in pieces], axis=-1)
    f2[...] = spread(joined, down[...]).reshape(x2, y2, LANES)
    g2[0, 3 : 3 + x2, PAD : PAD + y2, :] = mixed1(S2, f2[...], 32)
    planes2 = [(0, 0), (0, 1), (1, 0), (1, 1), (2, 0)]
    pack(g2, s2, planes2, 3, x2, y2)
    copies = exchange(g2, s2, p2, c2, 3, x2, y2, 5)
    unpack(copies, g2, p2, c2, planes2, 3, x2, y2, 5, 4, 3)

    def block_stencil(load, coefficient, x, xs, row, rows, segment):
        center = load(x, xs, row, rows)
        beside = load(x - 1, xs, row, rows) + load(x + 1, xs, row, rows)
        beside += load(x, xs, row - 1, rows) + load(x, xs, row + 1, rows)
        return center, stencil(center, beside, coefficient, segment)

    def from_g2(x, xs, row, rows):
        return g2[0, x : x + xs, row : row + rows, :]

    def from_v2(x, xs, row, rows):
        return v2[x : x + xs, row : row + rows, :]

    row, rows = PAD - 2, y2 + 4
    center, applied = block_stencil(
        from_g2, g2[1, 1 : x2 + 5, row : row + rows, :], 1, x2 + 4, row, rows, 32
    )
    v2[1 : x2 + 5, row : row + rows, :] = 2.0 * center - mixed1(T2, applied, 32)
    _, applied = block_stencil(
        from_v2, g2[1, 3 : 3 + x2, PAD : PAD + y2, :], 3, x2, PAD, y2, 32
    )
    rest = f2[...] - mixed1(B2, applied, 32)
    pairs = jnp.concatenate([rest[2 * i] + rest[2 * i + 1] for i in range(x3)], axis=0)
    r3[...] = spread(pairs, last_down[...]).reshape(x3, y2, LANES)

    forcing = r3[:, pl.ds(0, y3, stride=2), :] + r3[:, pl.ds(1, y3, stride=2), :]
    smoothed = mixed1(S3, forcing, 16)
    g3[0, 4 : 4 + x3, PAD : PAD + y3, :] = smoothed
    s3[:, 0:y3, :] = smoothed
    s3[:, y3 : 2 * y3, :] = g3[1, 4 : 4 + x3, PAD : PAD + y3, :]
    for x in range(x3):
        line[x : x + 1, :] = jnp.sum(smoothed[x], axis=0, keepdims=True)
    copies = [send(s3, p3.at[0], (0, 1)), send(s3, p3.at[1], (0, -1))]
    copies += [send(line, lines.at[k - 1], (0, k)) for k in range(1, ny)]
    for copy in copies:
        copy.wait_recv()
    total = line[...]
    for k in range(1, ny):
        total += lines[k - 1]
    total *= 4.0 / math.sqrt(ny * y3)
    for x in range(x3):
        g3[0, 4 + x, 0:1, :] = total[x : x + 1, :]
    for side, row in ((0, PAD - y3), (1, PAD + y3)):
        inside = (my > 0) if side == 0 else (my < ny - 1)
        for c in range(2):
            g3[c, 4 : 4 + x3, row : row + y3, :] = jnp.where(
                inside, p3[side, :, c * y3 : (c + 1) * y3, :], 0.0
            )
    block = pl.ds(4, x3)
    used = pl.ds(0, 2 * PAD)
    copies = [
        send(g3.at[:, block, used], g3.at[:, pl.ds(4 - dx * x3, x3), used], (dx, 0))
        for dx in (1, -1, 2, -2)
    ]
    for copy in copies:
        copy.wait_recv()
    for dx in (1, -1, 2, -2):
        outside = (mx < dx) if dx > 0 else (mx >= nx + dx)

        @pl.when(outside)
        def _(dx=dx):
            g3[:, 4 - dx * x3 : 4 - dx * x3 + x3] = jnp.zeros((2, x3) + g3.shape[2:], F32)

    low, high = PAD - y3, PAD + 2 * y3
    cell = lax.broadcasted_iota(jnp.int32, (1, 3 * y3, LANES), 1) + (my - 1) * y3
    inside = (cell >= 0) & (cell < ny * y3)
    w3[:, low:high, :] = g3[0, :, low:high, :] + jnp.where(inside, g3[0, :, 0:1, :], 0.0)

    def from_w3(x, xs, row, rows):
        return w3[x : x + xs, row : row + rows, :]

    for sweep in range(1, 4):
        x, xs = sweep, 8 + x3 - 2 * sweep
        row, rows = low + sweep, high - low - 2 * sweep
        center, applied = block_stencil(
            from_w3, g3[1, x : x + xs, row : row + rows, :], x, xs, row, rows, 16
        )
        value = center + g3[0, x : x + xs, row : row + rows, :] - mixed1(T3, applied, 16)
        if sweep < 3:
            w3[x : x + xs, row : row + rows, :] = value
        else:
            b3[:, 0:rows, :] = value

    xs, rows = x3 + 2, y3 + 2
    children = spread(b3[...].reshape(xs * 8, LANES), last_up[...]).reshape(xs, 8, LANES)
    for i in range(xs):
        for s in range(2):
            q2[i, pl.ds(PAD - 2 + s, rows, stride=2), :] = children[i, 0:rows, :]
    row, rows = PAD - 2, y2 + 4
    for i in range(xs):
        for s in range(2):
            v2[1 + 2 * i + s, row : row + rows, :] += q2[i, row : row + rows, :]
    row, rows = PAD - 1, y2 + 2
    center, applied = block_stencil(
        from_v2, g2[1, 2 : x2 + 4, row : row + rows, :], 2, x2 + 2, row, rows, 32
    )
    w2[:, 0:rows, :] = center + g2[0, 2 : x2 + 4, row : row + rows, :] - mixed1(T2, applied, 32)

    xs = x2 + 2
    children = spread(w2[...].reshape(xs * 16, LANES), up[...]).reshape(xs, 16, 2 * LANES)
    for g in range(2):
        for i in range(xs):
            for s in range(2):
                q1[g, i, pl.ds(PAD - 2 + s, rows, stride=2), :] = children[
                    i, 0:rows, g * LANES : (g + 1) * LANES
                ]

    def lift_second(step):
        row, rows = PAD - 2, y1 + 4
        for g in range(2):
            part = q1[g, step // 2, row : row + rows, :]
            v1[g, step + 1, row : row + rows, :] += part

    steps(x1 + 4, lift_second)

    def finish_second(step):
        x = step + 2
        row, rows = PAD - 1, y1 + 2
        coefficient = g1[2, x, row : row + rows, :]
        change = mixed2(T1, [stencil_of(v1, coefficient, c, x, row, rows, 64) for c in range(2)])
        for c in range(2):
            value = v1[c, x, row : row + rows, :] + g1[c, x, row : row + rows, :] - change[c]
            w1[c, step, 0:rows, :] = value

    steps(x1 + 2, finish_second)

    def spread_fine(i):
        rows = y1 + 2
        for g in range(2):
            children = spread(w1[g, i], up[...])
            for c in range(2):
                for s in range(2):
                    q0[2 * g + c, i, pl.ds(PAD - 2 + s, rows, stride=2), :] = children[
                        0:rows, c * LANES : (c + 1) * LANES
                    ]

    steps(x1 + 2, spread_fine)

    def lift_fine(step):
        row, rows = PAD - 1, y0 + 2
        for c in range(4):
            part = q0[c, (step + 1) // 2, row : row + rows, :]
            v0[c, step + 1, row : row + rows, :] += part

    steps(x0 + 2, lift_fine)

    def finish_fine(x):
        coefficient = g0[4, x + 2, PAD : PAD + y0, :]
        change = mixed4(
            T0, [stencil_of(v0, coefficient, c, x + 2, PAD, y0, LANES) for c in range(4)]
        )
        for c in range(4):
            value = v0[c, x + 2, PAD : PAD + y0, :] + g0[c, x + 2, PAD : PAD + y0, :]
            f0[c, x] = value - change[c]

    quarter = x0 // 4
    stores = []
    for q in range(4):
        steps(quarter, lambda i, q=q: finish_fine(i + q * quarter))
        part = pl.ds(q * quarter, quarter)
        store = pltpu.make_async_copy(f0.at[:, part], out.at[:, part], out_sem.at[q])
        store.start()
        stores.append(store)
    for copy in started:
        copy.wait_send()
    for store in stores:
        store.wait()


def per_device(nx, ny, source, fine, second, third, coarse, mixers, smoothers):
    x0, y0 = source.shape[1:3]
    x1, y1 = second.shape[:2]
    x2, y2 = third.shape[:2]
    x3, y3 = coarse.shape[:2]

    def padded(groups, xs, ys, h):
        return pltpu.VMEM((groups, xs + 2 * h, ys + 2 * PAD, LANES), F32)

    def vmem(*shape):
        return pltpu.VMEM(shape, F32)

    def faces(planes, near, xs):
        rows = max(xs, 8)
        return [
            vmem(2, planes, rows, LANES),
            vmem(2, planes, rows, LANES),
            vmem(4, near, 8, LANES),
        ]

    scratch = (
        [vmem(4, x0, y0, LANES), padded(5, x0, y0, 2), padded(4, x0, y0, 2)]
        + [vmem(4, x1, y0, LANES), vmem(4, x1 + 2, y0 + 2 * PAD, LANES)]
        + faces(9, 4, x0)
        + [vmem(*second.shape), vmem(2, x1, y1, LANES), padded(3, x1, y1, 3), padded(2, x1, y1, 3)]
        + [vmem(2, x2, y1, LANES), vmem(2, x2 + 2, y1 + 2 * PAD, LANES)]
        + [vmem(2, x1 + 2, y1 + 8, LANES)]
        + faces(8, 5, x1)
        + [vmem(*third.shape), vmem(x2, y2, LANES), padded(2, x2, y2, 3)]
        + [vmem(x2 + 6, y2 + 2 * PAD, LANES), vmem(x3, y2, LANES)]
        + [vmem(x3 + 2, y2 + 2 * PAD, LANES), vmem(x2 + 2, 16, LANES)]
        + faces(5, 5, x2)
        + [vmem(*coarse.shape), vmem(x3, y2, LANES), vmem(2, x3 + 8, 24, LANES)]
        + [vmem(x3 + 8, 24, LANES), vmem(x3 + 2, 8, LANES)]
        + [vmem(x3, 2 * y3, LANES), vmem(2, x3, 2 * y3, LANES)]
        + [vmem(x3, LANES), vmem(ny - 1, x3, LANES)]
        + [vmem(48, LANES)]
        + [pltpu.VMEM((2 * LANES, LANES), BF16), pltpu.VMEM((LANES, 2 * LANES), BF16)]
        + [pltpu.VMEM((LANES, LANES), BF16), pltpu.VMEM((LANES, LANES), BF16)]
    )
    copies = 8 * 3 + 2 + (ny - 1) + 4
    scratch += [
        pltpu.SemaphoreType.DMA((copies,)),
        pltpu.SemaphoreType.DMA((copies,)),
        pltpu.SemaphoreType.DMA((5,)),
        pltpu.SemaphoreType.DMA((4,)),
    ]
    anywhere = pl.BlockSpec(memory_space=pl.ANY)
    scalars = pl.BlockSpec(memory_space=pltpu.SMEM)
    return pl.pallas_call(
        functools.partial(kernel, nx, ny),
        out_shape=jax.ShapeDtypeStruct(source.shape, F32),
        in_specs=[anywhere] * 5 + [scalars] * 2,
        out_specs=anywhere,
        scratch_shapes=scratch,
        compiler_params=pltpu.CompilerParams(
            collective_id=0, has_side_effects=True, vmem_limit_bytes=40 * 1024 * 1024
        ),
    )(source, fine, second, third, coarse, mixers, smoothers)


def solution(mesh):
    field, cells = P(None, "gx", "gy", None), P("gx", "gy", None)
    return jax.shard_map(
        functools.partial(per_device, mesh.shape["gx"], mesh.shape["gy"]),
        mesh=mesh,
        in_specs=(field, cells, cells, cells, cells, P(), P()),
        out_specs=field,
        check_vma=False,
    )
```

```python
import functools
import math

import jax
import jax.numpy as jnp
from jax import lax
from jax.experimental import pallas as pl
from jax.experimental.pallas import tpu as pltpu
from jax.sharding import PartitionSpec as P

MESH = pl.DeviceIdType.MESH
F32 = jnp.float32
BF16 = jnp.bfloat16
LANES = 128
PAD = 8


def spread(field, matrix):
    high = field.astype(BF16)
    low = (field - high.astype(F32)).astype(BF16)
    return jnp.dot(high, matrix, preferred_element_type=F32) + jnp.dot(
        low, matrix, preferred_element_type=F32
    )


def spread_stacked(field, matrix):
    high = field.astype(BF16)
    low = (field - high.astype(F32)).astype(BF16)
    return jnp.dot(jnp.concatenate([high, low], axis=-1), matrix, preferred_element_type=F32)


def lane_index(shape):
    return lax.broadcasted_iota(jnp.int32, shape, len(shape) - 1)


def beside_z(field, segment):
    lane = lane_index((1, LANES)) % segment
    axis = field.ndim - 1
    before = jnp.where(lane == 0, 0.0, pltpu.roll(field, 1, axis))
    after = jnp.where(lane == segment - 1, 0.0, pltpu.roll(field, LANES - 1, axis))
    return before + after


def stencil(center, beside, coefficient, segment):
    total = beside + beside_z(center, segment)
    return coefficient * (6.0 * center - total) + center


def kernel(
    nx, ny,
    source, fine, second, third, coarse, mixers, smoothers, out,
    f0, a0, g0, v0, h0, r0, e0, m0, q0, s0, p0, c0,
    a1, f1, g1, v1, r1, x1_part, e1, m1, q1, w1, s1, p1, c1,
    a2, f2, g2, v2, r2, x2_part, e2, m2, q2, w2, s2, p2, c2,
    a3, r3, g3, k3, w3, b3, s3, p3, t3, u3, line, lines,
    table, down, up, rise_fine, rise_second, last_down, last_up, last_rise,
    send_sem, recv_sem, local_sem, out_sem,
):
    mx, my = lax.axis_index("gx"), lax.axis_index("gy")

    def device(dx, dy):
        return (lax.rem(mx + (dx + nx), nx), lax.rem(my + (dy + ny), ny))

    barrier = pltpu.get_barrier_semaphore()
    peers = [(0, k) for k in range(1, ny)]
    peers += [(dx, dy) for dx in (-1, 1) for dy in (-1, 0, 1)] + [(-2, 0), (2, 0)]
    for dx, dy in peers:
        pl.semaphore_signal(barrier, inc=1, device_id=device(dx, dy), device_id_type=MESH)

    x0, y0 = f0.shape[1:3]
    x1, y1 = f1.shape[1:3]
    x2, y2 = f2.shape[:2]
    x3, y3 = a3.shape[:2]
    first_rows = min(4, x0 // 4)
    parts = [(0, first_rows), (x0 - first_rows, first_rows), (first_rows, x0 - 2 * first_rows)]
    load_fine = pltpu.make_async_copy(fine, a0.at[pl.ds(1, x0)], local_sem.at[0])
    load_parts = [
        pltpu.make_async_copy(
            source.at[:, pl.ds(x, xs)], f0.at[:, pl.ds(x, xs)], local_sem.at[4 + n]
        )
        for n, (x, xs) in enumerate(parts)
    ]
    load_coarser = [
        pltpu.make_async_copy(second, a1, local_sem.at[1]),
        pltpu.make_async_copy(third, a2, local_sem.at[2]),
        pltpu.make_async_copy(coarse, a3, local_sem.at[3]),
    ]
    for load in load_parts + [load_fine] + load_coarser:
        load.start()

    def smooth_matrix(level):
        return [
            [smoothers[level, i, j] + (0.25 if i == j else 0.0) for j in range(4)]
            for i in range(4)
        ]

    def mix_matrix(level):
        return [
            [mixers[level, i, j] + (1.0 if i == j else 0.0) for j in range(4)] for i in range(4)
        ]

    def product(left, right):
        return [
            [sum(left[i][k] * right[k][j] for k in range(4)) for j in range(4)] for i in range(4)
        ]

    lane = lane_index((1, LANES))
    rows_used = [0]

    def keep(vector):
        row = rows_used[0]
        rows_used[0] += 1
        table[row : row + 1, :] = vector
        return row

    def pair_rows(matrix):
        return [
            [
                [
                    keep(
                        jnp.where(
                            lane < 64,
                            matrix[2 * g][2 * h + s],
                            matrix[2 * g + 1][2 * h + 1 - s],
                        )
                    )
                    for s in range(2)
                ]
                for h in range(2)
            ]
            for g in range(2)
        ]

    def quad_rows(matrix, segment):
        channel = (lane // segment) % 4
        rows = []
        for k in range(4):
            vector = jnp.zeros((1, LANES), F32)
            for i in range(4):
                vector = jnp.where(channel == i, matrix[i][(i - k) % 4], vector)
            rows.append(keep(vector))
        return rows

    S0 = smooth_matrix(0)

    def mixed4(matrix, fields):
        return [
            matrix[i][0] * fields[0]
            + matrix[i][1] * fields[1]
            + (matrix[i][2] * fields[2] + matrix[i][3] * fields[3])
            for i in range(4)
        ]

    def vector_of(row):
        return table[row : row + 1, :]

    def mixed2(rows, fields):
        turned = [pltpu.roll(field, 64, field.ndim - 1) for field in fields]
        return [
            vector_of(rows[g][0][0]) * fields[0]
            + vector_of(rows[g][0][1]) * turned[0]
            + (vector_of(rows[g][1][0]) * fields[1] + vector_of(rows[g][1][1]) * turned[1])
            for g in range(2)
        ]

    def mixed1(rows, field, segment):
        total = vector_of(rows[0]) * field
        for k in range(1, 4):
            total += vector_of(rows[k]) * pltpu.roll(field, k * segment, field.ndim - 1)
        return total

    def row_index(shape):
        return lax.broadcasted_iota(jnp.int32, shape, 0)

    def children_matrix(columns, segment):
        shape = (2 * LANES, columns)
        row, column = row_index(shape) % LANES, lane_index(shape)
        if segment is None:
            return jnp.where(row == column // 2, 1.0, 0.0).astype(BF16)
        odd = column % 2
        other = column // 2 + 2 * odd - 1
        place = column % segment
        valid = (place != 0) & (place != segment - 1)
        own = jnp.where(row == column // 2, 3.0, 0.0)
        return (own - jnp.where((row == other) & valid, 1.0, 0.0)).astype(BF16)

    started = []

    def send(src, dst, place):
        number = len(started)
        copy = pltpu.make_async_remote_copy(
            src_ref=src, dst_ref=dst, send_sem=send_sem.at[number], recv_sem=recv_sem.at[number],
            device_id=device(*place), device_id_type=MESH,
        )
        copy.start()
        started.append(copy)
        return copy

    def pack(g, s, planes, h, xs, ys):
        for p, (k, c) in enumerate(planes):
            s[0, p, 0:xs, :] = g[c, h : h + xs, PAD + k, :]
            s[1, p, 0:xs, :] = g[c, h : h + xs, PAD + ys - 1 - k, :]

    def send_corners(s, corner, xs, near):
        copies = []
        first, last = pl.ds(0, 8), pl.ds(max(xs - 8, 0), 8)
        for side, dy in ((1, 1), (0, -1)):
            for end, dx in ((last, 1), (first, -1)):
                copies.append(
                    send(
                        s.at[side, pl.ds(0, near), end],
                        corner.at[(0 if dx > 0 else 1) * 2 + (0 if dy > 0 else 1)],
                        (dx, dy),
                    )
                )
        return copies

    def exchange(g, s, p, corner, h, xs, ys, near):
        own = pl.ds(PAD, ys)
        copies = [
            send(g.at[:, pl.ds(xs, h), own], g.at[:, pl.ds(0, h), own], (1, 0)),
            send(g.at[:, pl.ds(h, h), own], g.at[:, pl.ds(xs + h, h), own], (-1, 0)),
            send(s.at[1], p.at[0], (0, 1)),
            send(s.at[0], p.at[1], (0, -1)),
        ]
        return copies + send_corners(s, corner, xs, near)

    def unpack(copies, g, p, corner, planes, h, xs, ys, near, reach, a_reach):
        for copy in copies:
            copy.wait_recv()
        groups = g.shape[0]
        for n, (k, c) in enumerate(planes):
            g[c, h : h + xs, PAD - 1 - k, :] = p[0, n, 0:xs, :]
            g[c, h : h + xs, PAD + ys + k, :] = p[1, n, 0:xs, :]
        top = min(xs, 8) - 1
        for n, (k, c) in enumerate(planes[:near]):
            for i in range((a_reach if c == groups - 1 else reach) - 1 - k):
                for from_dy in range(2):
                    row = PAD - 1 - k if from_dy == 0 else PAD + ys + k
                    g[c, h - 1 - i, row : row + 1, :] = corner[from_dy, n, top - i : top - i + 1, :]
                    g[c, h + xs + i, row : row + 1, :] = corner[2 + from_dy, n, i : i + 1, :]

        @pl.when(mx == 0)
        def _():
            g[:, 0:h] = jnp.zeros((groups, h) + g.shape[2:], F32)

        @pl.when(mx == nx - 1)
        def _():
            g[:, h + xs :] = jnp.zeros((groups, h) + g.shape[2:], F32)

        @pl.when(my == 0)
        def _():
            g[:, :, 0:PAD] = jnp.zeros(g.shape[:2] + (PAD, LANES), F32)

        @pl.when(my == ny - 1)
        def _():
            g[:, :, PAD + ys :] = jnp.zeros(g.shape[:2] + (PAD, LANES), F32)

    def steps(count, body):
        def step(i, carry):
            body(i)
            return carry

        lax.fori_loop(0, count, step, 0)

    def stencil_of(field, coefficient, c, x, row, rows, segment):
        center = field[c, x, row : row + rows, :]
        beside = field[c, x - 1, row : row + rows, :] + field[c, x + 1, row : row + rows, :]
        beside += field[c, x, row - 1 : row - 1 + rows, :]
        beside += field[c, x, row + 1 : row + 1 + rows, :]
        return stencil(center, beside, coefficient, segment)

    y_rows = y0 + 2 * PAD

    def fine_rows(buffer, c, x, row, rows):
        start = x * y_rows + row
        if row % 8 == 0:
            start = pl.multiple_of(start, 8)
        return buffer[c, pl.ds(start, rows), :]

    def fine_plane(row):
        return pl.ds(2 * y_rows + row, x0, stride=y_rows)

    def fine_stencil(buffer, coefficient, c, x):
        center = fine_rows(buffer, c, x, PAD, y0)
        beside = fine_rows(buffer, c, x - 1, PAD, y0) + fine_rows(buffer, c, x + 1, PAD, y0)
        beside += fine_rows(buffer, c, x, PAD - 1, y0) + fine_rows(buffer, c, x, PAD + 1, y0)
        return stencil(center, beside, coefficient, LANES)

    def smooth_fine(x):
        fields = mixed4(S0, [f0[c, x] for c in range(4)])
        for c in range(4):
            start = pl.multiple_of((x + 2) * y_rows + PAD, 8)
            g0[c, pl.ds(start, y0), :] = fields[c]

    def smooth_part(n):
        load_parts[n].wait()
        x, xs = parts[n]
        steps(xs, lambda i: smooth_fine(i + x))

    smooth_part(0)
    smooth_part(1)
    load_fine.wait()
    pl.semaphore_wait(barrier, len(peers))
    copies = []
    for layer, dst, dx in ((x0 + 1, 1, 1), (2, x0 + 2, -1), (x0, 0, 1), (3, x0 + 3, -1)):
        copies.append(
            send(
                g0.at[:, pl.ds(layer * y_rows + PAD, y0)],
                g0.at[:, pl.ds(dst * y_rows + PAD, y0)],
                (dx, 0),
            )
        )
    copies.append(send(a0.at[pl.ds(x0, 1)], a0.at[pl.ds(0, 1)], (1, 0)))
    copies.append(send(a0.at[pl.ds(1, 1)], a0.at[pl.ds(x0 + 1, 1)], (-1, 0)))
    smooth_part(2)
    for c in range(4):
        for k in range(2):
            n = c if k == 0 else 5 + c
            s0[0, n] = g0[c, fine_plane(PAD + k), :]
            s0[1, n] = g0[c, fine_plane(PAD + y0 - 1 - k), :]
    s0[0, 4] = a0[1 : x0 + 1, 0, :]
    s0[1, 4] = a0[1 : x0 + 1, y0 - 1, :]
    copies.append(send(s0.at[1], p0.at[0], (0, 1)))
    copies.append(send(s0.at[0], p0.at[1], (0, -1)))
    copies += send_corners(s0, c0, x0, 4)

    for c in range(4):
        for row in (PAD - 1, PAD + y0):
            g0[c, fine_plane(row), :] = jnp.zeros((x0, LANES), F32)
    B0 = mix_matrix(0)
    T0 = product(S0, B0)

    def relax_fine(x):
        coefficient = a0[x - 1]
        change = mixed4(T0, [fine_stencil(g0, coefficient, c, x) for c in range(4)])
        for c in range(4):
            value = 2.0 * fine_rows(g0, c, x, PAD, y0) - change[c]
            v0[c, pl.ds(pl.multiple_of(x * y_rows + PAD, 8), y0), :] = value

    steps(x0 - 2, lambda i: relax_fine(i + 3))
    for load in load_coarser:
        load.wait()
    third_cells = jnp.concatenate([a3[...]] * 8, axis=-1)
    k3[4 : 4 + x3, PAD : PAD + y3, :] = third_cells
    for x in range(x3):
        t3[x * y3 : (x + 1) * y3, :] = third_cells[x]
    coarse_copies = [send(t3, u3.at[0], (0, 1)), send(t3, u3.at[1], (0, -1))]
    g1[2, 3 : 3 + x1, PAD : PAD + y1, :] = jnp.concatenate([a1[...]] * 2, axis=-1)
    g2[1, 3 : 3 + x2, PAD : PAD + y2, :] = jnp.concatenate([a2[...]] * 4, axis=-1)
    smooth1, mixer1 = smooth_matrix(1), mix_matrix(1)
    S1, B1, T1 = pair_rows(smooth1), pair_rows(mixer1), pair_rows(product(smooth1, mixer1))
    smooth2, mixer2 = smooth_matrix(2), mix_matrix(2)
    S2, B2 = quad_rows(smooth2, 32), quad_rows(mixer2, 32)
    T2 = quad_rows(product(smooth2, mixer2), 32)
    smooth3, mixer3 = smooth_matrix(3), mix_matrix(3)
    S3, T3 = quad_rows(smooth3, 16), quad_rows(product(smooth3, mixer3), 16)
    T0_below = pair_rows(T0)
    T1_below = quad_rows(product(smooth1, mixer1), 32)
    T2_below = quad_rows(product(smooth2, mixer2), 16)

    wide, narrow = (2 * LANES, LANES), (LANES, LANES)
    down[...] = jnp.where(row_index(wide) // 2 == lane_index(wide), 0.125, 0.0).astype(BF16)
    last_down[...] = jnp.where(
        row_index(narrow) // 2 == lane_index(narrow) % 64, 0.125, 0.0
    ).astype(BF16)
    up[...] = children_matrix(2 * LANES, None)
    rise_fine[...] = children_matrix(2 * LANES, LANES)
    rise_second[...] = children_matrix(2 * LANES, 64)
    last_up[...] = children_matrix(LANES, None)
    last_rise[...] = children_matrix(LANES, 32)

    for copy in copies:
        copy.wait_recv()

    @pl.when(mx == 0)
    def _():
        g0[:, 0 : 2 * y_rows] = jnp.zeros((4, 2 * y_rows, LANES), F32)
        c0[0:2] = jnp.zeros((2,) + c0.shape[1:], F32)
        a0[0] = jnp.zeros((y0, LANES), F32)

    @pl.when(mx == nx - 1)
    def _():
        g0[:, (x0 + 2) * y_rows :] = jnp.zeros((4, 2 * y_rows, LANES), F32)
        c0[2:4] = jnp.zeros((2,) + c0.shape[1:], F32)
        a0[x0 + 1] = jnp.zeros((y0, LANES), F32)

    for side, edge in ((0, 0), (1, ny - 1)):

        @pl.when(my == edge)
        def _(side=side):
            p0[side] = jnp.zeros(p0.shape[1:], F32)
            c0[side] = jnp.zeros(c0.shape[1:], F32)
            c0[2 + side] = jnp.zeros(c0.shape[1:], F32)

    for c in range(4):
        for side, row in ((0, PAD - 1), (1, PAD + y0)):
            left, right = c0[side, c, 7:8, :], c0[2 + side, c, 0:1, :]
            g0[c, y_rows + row : y_rows + row + 1, :] = left
            g0[c, (x0 + 2) * y_rows + row : (x0 + 2) * y_rows + row + 1, :] = right
            h0[side, c, PAD - 1 : PAD, :] = left
            h0[side, c, PAD + x0 : PAD + x0 + 1, :] = right
            h0[side, c, PAD : PAD + x0, :] = p0[side, c]
    steps(4, lambda i: relax_fine(1 + i + (x0 - 2) * (i // 2)))
    for side, own, halo in ((0, PAD, PAD - 1), (1, PAD + y0 - 1, PAD + y0)):
        near = [p0[side, c] for c in range(4)]
        change = mixed4(T0, [s0[side, 4] * near[c] for c in range(4)])
        for c in range(4):
            v0[c, fine_plane(own), :] += change[c]
        applied = []
        for c in range(4):
            beside = h0[side, c, PAD - 1 : PAD - 1 + x0, :] + h0[side, c, PAD + 1 : PAD + 1 + x0, :]
            beside += p0[side, 5 + c] + s0[side, c]
            applied.append(stencil(near[c], beside, p0[side, 4], LANES))
        change = mixed4(T0, applied)
        for c in range(4):
            v0[c, fine_plane(halo), :] = 2.0 * near[c] - change[c]

    def residual_fine(i):
        total = [None] * 4
        for s in range(2):
            x = 2 * i + s
            applied = mixed4(B0, [fine_stencil(v0, a0[x + 1], c, x + 2) for c in range(4)])
            for c in range(4):
                rest = f0[c, x] - applied[c]
                total[c] = rest if s == 0 else total[c] + rest
        for c in range(4):
            r0[c, i] = total[c]

    steps(x1, residual_fine)

    for g in range(2):
        pieces = [
            r0[c, :, pl.ds(0, y1, stride=2), :] + r0[c, :, pl.ds(1, y1, stride=2), :]
            for c in (2 * g, 2 * g + 1)
        ]
        joined = jnp.concatenate([piece.reshape(x1 * y1, LANES) for piece in pieces], axis=-1)
        f1[g] = spread(joined, down[...]).reshape(x1, y1, LANES)
    fields = mixed2(S1, [f1[g] for g in range(2)])
    for g in range(2):
        g1[g, 3 : 3 + x1, PAD : PAD + y1, :] = fields[g]
    planes1 = [(0, 0), (0, 1), (0, 2), (1, 0), (1, 1), (1, 2), (2, 0), (2, 1)]
    pack(g1, s1, planes1, 3, x1, y1)
    copies = exchange(g1, s1, p1, c1, 3, x1, y1, 5)

    def fill_beside(buffer, received):
        for side, row in ((0, PAD - y3), (1, PAD + y3)):
            inside = (my > 0) if side == 0 else (my < ny - 1)
            for x in range(x3):
                buffer[4 + x, row : row + y3, :] = jnp.where(
                    inside, received[side, x * y3 : (x + 1) * y3, :], 0.0
                )

    def send_block(buffer):
        block, used = pl.ds(4, x3), pl.ds(0, 2 * PAD)
        return [
            send(buffer.at[block, used], buffer.at[pl.ds(4 - dx * x3, x3), used], (dx, 0))
            for dx in (1, -1, 2, -2)
        ]

    def receive_block(buffer, copies):
        for copy in copies:
            copy.wait_recv()
        for dx in (1, -1, 2, -2):
            outside = (mx < dx) if dx > 0 else (mx >= nx + dx)

            @pl.when(outside)
            def _(dx=dx):
                buffer[4 - dx * x3 : 4 - dx * x3 + x3] = jnp.zeros((x3,) + buffer.shape[1:], F32)

    for copy in coarse_copies:
        copy.wait_recv()
    fill_beside(k3, u3)
    coarse_copies = send_block(k3)

    def settle_fine(x):
        change = mixed4(T0, [fine_stencil(v0, a0[x + 1], c, x + 2) for c in range(4)])
        for c in range(4):
            value = fine_rows(v0, c, x + 2, PAD, y0) + fine_rows(g0, c, x + 2, PAD, y0)
            f0[c, x] = value - change[c]

    steps(x0, settle_fine)
    unpack(copies, g1, p1, c1, planes1, 3, x1, y1, 5, 3, 2)

    def relax_second(step):
        x = step + 1
        row, rows = PAD - 2, y1 + 4
        coefficient = g1[2, x, row : row + rows, :]
        change = mixed2(T1, [stencil_of(g1, coefficient, c, x, row, rows, 64) for c in range(2)])
        for c in range(2):
            v1[c, x, row : row + rows, :] = 2.0 * g1[c, x, row : row + rows, :] - change[c]

    steps(x1 + 4, relax_second)

    def residual_second(i):
        total = [None] * 2
        for s in range(2):
            x = 2 * i + s
            coefficient = g1[2, x + 3, PAD : PAD + y1, :]
            applied = mixed2(
                B1, [stencil_of(v1, coefficient, c, x + 3, PAD, y1, 64) for c in range(2)]
            )
            for c in range(2):
                rest = f1[c, x] - applied[c]
                total[c] = rest if s == 0 else total[c] + rest
        for c in range(2):
            r1[c, i] = total[c]

    steps(x2, residual_second)

    pieces = [
        r1[c, :, pl.ds(0, y2, stride=2), :] + r1[c, :, pl.ds(1, y2, stride=2), :] for c in range(2)
    ]
    joined = jnp.concatenate([piece.reshape(x2 * y2, LANES) for piece in pieces], axis=-1)
    f2[...] = spread(joined, down[...]).reshape(x2, y2, LANES)
    g2[0, 3 : 3 + x2, PAD : PAD + y2, :] = mixed1(S2, f2[...], 32)
    planes2 = [(0, 0), (0, 1), (1, 0), (1, 1), (2, 0)]
    pack(g2, s2, planes2, 3, x2, y2)
    copies = exchange(g2, s2, p2, c2, 3, x2, y2, 5)
    receive_block(k3, coarse_copies)

    def settle_second(step):
        x = step + 2
        row, rows = PAD - 1, y1 + 2
        coefficient = g1[2, x, row : row + rows, :]
        change = mixed2(T1, [stencil_of(v1, coefficient, c, x, row, rows, 64) for c in range(2)])
        for c in range(2):
            value = v1[c, x, row : row + rows, :] + g1[c, x, row : row + rows, :] - change[c]
            x1_part[c, step, row : row + rows, :] = value

    steps(x1 + 2, settle_second)
    unpack(copies, g2, p2, c2, planes2, 3, x2, y2, 5, 4, 3)

    def block_stencil(load, coefficient, x, xs, row, rows, segment):
        center = load(x, xs, row, rows)
        beside = load(x - 1, xs, row, rows) + load(x + 1, xs, row, rows)
        beside += load(x, xs, row - 1, rows) + load(x, xs, row + 1, rows)
        return center, stencil(center, beside, coefficient, segment)

    def from_g2(x, xs, row, rows):
        return g2[0, x : x + xs, row : row + rows, :]

    def from_v2(x, xs, row, rows):
        return v2[x : x + xs, row : row + rows, :]

    row, rows = PAD - 2, y2 + 4
    center, applied = block_stencil(
        from_g2, g2[1, 1 : x2 + 5, row : row + rows, :], 1, x2 + 4, row, rows, 32
    )
    v2[1 : x2 + 5, row : row + rows, :] = 2.0 * center - mixed1(T2, applied, 32)
    _, applied = block_stencil(
        from_v2, g2[1, 3 : 3 + x2, PAD : PAD + y2, :], 3, x2, PAD, y2, 32
    )
    rest = f2[...] - mixed1(B2, applied, 32)
    pairs = jnp.concatenate([rest[2 * i] + rest[2 * i + 1] for i in range(x3)], axis=0)
    r3[...] = spread(pairs, last_down[...]).reshape(x3, y2, LANES)

    forcing = r3[:, pl.ds(0, y3, stride=2), :] + r3[:, pl.ds(1, y3, stride=2), :]
    smoothed = mixed1(S3, forcing, 16)
    g3[4 : 4 + x3, PAD : PAD + y3, :] = smoothed
    for x in range(x3):
        s3[x * y3 : (x + 1) * y3, :] = smoothed[x]
        line[x : x + 1, :] = jnp.sum(smoothed[x], axis=0, keepdims=True)
    copies = [send(line, lines.at[k - 1], (0, k)) for k in range(1, ny)]
    copies += [send(s3, p3.at[0], (0, 1)), send(s3, p3.at[1], (0, -1))]
    row, rows = PAD - 1, y2 + 2
    center, applied = block_stencil(
        from_v2, g2[1, 2 : x2 + 4, row : row + rows, :], 2, x2 + 2, row, rows, 32
    )
    x2_part[:, row : row + rows, :] = (
        center + g2[0, 2 : x2 + 4, row : row + rows, :] - mixed1(T2, applied, 32)
    )
    for copy in copies:
        copy.wait_recv()
    total = line[...]
    for k in range(1, ny):
        total += lines[k - 1]
    total *= 4.0 / math.sqrt(ny * y3)
    for x in range(x3):
        g3[4 + x, 0:1, :] = total[x : x + 1, :]
    fill_beside(g3, p3)
    receive_block(g3, send_block(g3))

    low, high = PAD - y3, PAD + 2 * y3
    cell = lax.broadcasted_iota(jnp.int32, (1, 3 * y3, LANES), 1) + (my - 1) * y3
    inside = (cell >= 0) & (cell < ny * y3)
    w3[:, low:high, :] = g3[:, low:high, :] + jnp.where(inside, g3[:, 0:1, :], 0.0)

    def from_w3(x, xs, row, rows):
        return w3[x : x + xs, row : row + rows, :]

    for sweep in range(1, 4):
        x, xs = sweep, 8 + x3 - 2 * sweep
        row, rows = low + sweep, high - low - 2 * sweep
        center, applied = block_stencil(
            from_w3, k3[x : x + xs, row : row + rows, :], x, xs, row, rows, 16
        )
        value = center + g3[x : x + xs, row : row + rows, :] - mixed1(T3, applied, 16)
        if sweep < 3:
            w3[x : x + xs, row : row + rows, :] = value
        else:
            b3[:, row : row + rows, :] = value

    below = b3[...]
    mixed = mixed1(T2_below, below, 16)
    flat = ((x3 + 2) * 2 * PAD, LANES)
    e2[...] = spread_stacked((below - mixed).reshape(flat), last_up[...]).reshape(e2.shape)
    m2[...] = spread_stacked(mixed.reshape(flat), last_rise[...]).reshape(m2.shape)
    q2[...] = spread_stacked(mixed.reshape(flat), last_up[...]).reshape(q2.shape)

    def raised(m, q, c, i, s, t, row, rows):
        other_y = q[c, i, row + 2 * t - 1 : row + 2 * t - 1 + rows, :]
        other_x = q[c, i + 2 * s - 1, row : row + rows, :]
        return m[c, i, row : row + rows, :] - other_y - other_x

    for x in range(-1, x2 + 1):
        i, s = x // 2 + 1, x % 2
        for t in range(2):
            row, rows = PAD - t, y3 + 1
            cells = pl.ds(PAD - t, rows, stride=2)
            value = raised(m2, q2, 0, i, s, t, row, rows)
            w2[x + 1, cells, :] = (
                x2_part[x + 1, cells, :]
                + e2[0, i, row : row + rows, :]
                - g2[1, x + 3, cells, :] * value
            )

    below = w2[...]
    mixed = mixed1(T1_below, below, 32)
    flat = ((x2 + 2) * (y2 + 2 * PAD), LANES)
    shape = (x2 + 2, y2 + 2 * PAD, LANES)
    for field, matrix, target in (
        (below - mixed, up, e1),
        (mixed, rise_second, m1),
        (mixed, up, q1),
    ):
        children = spread_stacked(field.reshape(flat), matrix[...])
        for c in range(2):
            target[c] = children[:, c * LANES : (c + 1) * LANES].reshape(shape)
    for x in range(-1, x1 + 1):
        i, s = x // 2 + 1, x % 2
        for t in range(2):
            row, rows = PAD - t, y2 + 1
            cells = pl.ds(PAD - t, rows, stride=2)
            coefficient = g1[2, x + 3, cells, :]
            for c in range(2):
                value = raised(m1, q1, c, i, s, t, row, rows)
                w1[c, x + 1, cells, :] = (
                    x1_part[c, x + 1, cells, :]
                    + e1[c, i, row : row + rows, :]
                    - coefficient * value
                )

    below = [w1[c] for c in range(2)]
    mixed = mixed2(T0_below, below)
    own = slice(1, x1 + 1), slice(PAD, PAD + y1)
    for g in range(2):
        inner = (x1 * y1, LANES)
        for field, matrix, target in (
            ((below[g] - mixed[g])[own].reshape(inner), up, e0),
            (mixed[g][own].reshape(inner), rise_fine, m0),
        ):
            children = spread_stacked(field, matrix[...])
            for c in range(2):
                part = children[:, c * LANES : (c + 1) * LANES]
                target[2 * g + c, 1 : x1 + 1, PAD : PAD + y1, :] = part.reshape(x1, y1, LANES)
        children = spread_stacked(
            mixed[g].reshape((x1 + 2) * (y1 + 2 * PAD), LANES), up[...]
        )
        for c in range(2):
            part = children[:, c * LANES : (c + 1) * LANES]
            q0[2 * g + c] = part.reshape(x1 + 2, y1 + 2 * PAD, LANES)

    def finish_fine(step):
        i = step + 1
        for t in range(2):
            cells = pl.ds(t, y1, stride=2)
            coefficient = [a0[2 * step + s + 1, pl.ds(t, y1, stride=2), :] for s in range(2)]
            for c in range(4):
                for s in range(2):
                    value = raised(m0, q0, c, i, s, t, PAD, y1)
                    x = 2 * step + s
                    f0[c, x, cells, :] = (
                        f0[c, x, cells, :]
                        + e0[c, i, PAD : PAD + y1, :]
                        - coefficient[s] * value
                    )

    quarter = x1 // 4
    stores = []
    for q in range(4):
        steps(quarter, lambda i, q=q: finish_fine(i + q * quarter))
        part = pl.ds(2 * q * quarter, 2 * quarter)
        store = pltpu.make_async_copy(f0.at[:, part], out.at[:, part], out_sem.at[q])
        store.start()
        stores.append(store)
    for copy in started:
        copy.wait_send()
    for store in stores:
        store.wait()


def per_device(nx, ny, source, fine, second, third, coarse, mixers, smoothers):
    x0, y0 = source.shape[1:3]
    x1, y1 = second.shape[:2]
    x2, y2 = third.shape[:2]
    x3, y3 = coarse.shape[:2]

    def padded(groups, xs, ys, h):
        return pltpu.VMEM((groups, xs + 2 * h, ys + 2 * PAD, LANES), F32)

    def vmem(*shape):
        return pltpu.VMEM(shape, F32)

    def faces(planes, near, xs):
        rows = max(xs, 8)
        return [
            vmem(2, planes, rows, LANES),
            vmem(2, planes, rows, LANES),
            vmem(4, near, 8, LANES),
        ]

    def three(groups, xs, ys):
        return [vmem(groups, xs + 2, ys + 2 * PAD, LANES)] * 3

    double = pltpu.VMEM((2 * LANES, 2 * LANES), BF16)
    tall = pltpu.VMEM((2 * LANES, LANES), BF16)
    scratch = (
        [vmem(4, x0, y0, LANES), vmem(x0 + 2, y0, LANES)]
        + [vmem(4, (x0 + 4) * (y0 + 2 * PAD), LANES)] * 2
        + [vmem(2, 4, x0 + 2 * PAD, LANES)]
        + [vmem(4, x1, y0, LANES)]
        + three(4, x1, y1)
        + faces(9, 4, x0)
        + [vmem(*second.shape), vmem(2, x1, y1, LANES), padded(3, x1, y1, 3), padded(2, x1, y1, 3)]
        + [vmem(2, x2, y1, LANES), vmem(2, x1 + 2, y1 + 2 * PAD, LANES)]
        + three(2, x2, y2)
        + [vmem(2, x1 + 2, y1 + 2 * PAD, LANES)]
        + faces(8, 5, x1)
        + [vmem(*third.shape), vmem(x2, y2, LANES), padded(2, x2, y2, 3)]
        + [vmem(x2 + 6, y2 + 2 * PAD, LANES), vmem(x3, y2, LANES)]
        + [vmem(x2 + 2, y2 + 2 * PAD, LANES)]
        + [vmem(1, x3 + 2, 2 * PAD, LANES)] * 3
        + [vmem(x2 + 2, y2 + 2 * PAD, LANES)]
        + faces(5, 5, x2)
        + [vmem(*coarse.shape), vmem(x3, y2, LANES)]
        + [vmem(x3 + 8, 24, LANES)] * 3
        + [vmem(x3 + 2, 2 * PAD, LANES)]
        + [vmem(x3 * y3, LANES), vmem(2, x3 * y3, LANES)] * 2
        + [vmem(x3, LANES), vmem(ny - 1, x3, LANES)]
        + [vmem(64, LANES)]
        + [tall, double, double, double, pltpu.VMEM((LANES, LANES), BF16), tall, tall]
    )
    copies = 8 * 3 + 4 + 2 * 2 + (ny - 1) + 4 * 2
    scratch += [
        pltpu.SemaphoreType.DMA((copies,)),
        pltpu.SemaphoreType.DMA((copies,)),
        pltpu.SemaphoreType.DMA((7,)),
        pltpu.SemaphoreType.DMA((4,)),
    ]
    anywhere = pl.BlockSpec(memory_space=pl.ANY)
    scalars = pl.BlockSpec(memory_space=pltpu.SMEM)
    return pl.pallas_call(
        functools.partial(kernel, nx, ny),
        out_shape=jax.ShapeDtypeStruct(source.shape, F32),
        in_specs=[anywhere] * 5 + [scalars] * 2,
        out_specs=anywhere,
        scratch_shapes=scratch,
        compiler_params=pltpu.CompilerParams(
            collective_id=0, has_side_effects=True, vmem_limit_bytes=60 * 1024 * 1024
        ),
    )(source, fine, second, third, coarse, mixers, smoothers)


def solution(mesh):
    field, cells = P(None, "gx", "gy", None), P("gx", "gy", None)
    return jax.shard_map(
        functools.partial(per_device, mesh.shape["gx"], mesh.shape["gy"]),
        mesh=mesh,
        in_specs=(field, cells, cells, cells, cells, P(), P()),
        out_specs=field,
        check_vma=False,
    )
```

```python
import functools
import math

import jax
import jax.numpy as jnp
from jax import lax
from jax.experimental import pallas as pl
from jax.experimental.pallas import tpu as pltpu
from jax.sharding import PartitionSpec as P

MESH = pl.DeviceIdType.MESH
F32 = jnp.float32
BF16 = jnp.bfloat16
LANES = 128
PAD = 8


def spread(field, matrix):
    high = field.astype(BF16)
    low = (field - high.astype(F32)).astype(BF16)
    return jnp.dot(high, matrix, preferred_element_type=F32) + jnp.dot(
        low, matrix, preferred_element_type=F32
    )


def spread_stacked(field, matrix):
    high = field.astype(BF16)
    low = (field - high.astype(F32)).astype(BF16)
    return jnp.dot(jnp.concatenate([high, low], axis=-1), matrix, preferred_element_type=F32)


def lane_index(shape):
    return lax.broadcasted_iota(jnp.int32, shape, len(shape) - 1)


def beside_z(field, segment):
    lane = lane_index((1, LANES)) % segment
    axis = field.ndim - 1
    before = jnp.where(lane == 0, 0.0, pltpu.roll(field, 1, axis))
    after = jnp.where(lane == segment - 1, 0.0, pltpu.roll(field, LANES - 1, axis))
    return before + after


def stencil(center, beside, coefficient, segment):
    total = beside + beside_z(center, segment)
    return coefficient * (6.0 * center - total) + center


def kernel(
    nx, ny,
    source, fine, second, third, coarse, mixers_in, smoothers_in, out,
    f0, a0, g0, v0, h0, r0, e0, m0, q0, s0, p0, c0,
    a1, f1, g1, v1, r1, x1_part, e1, m1, q1, w1, s1, p1, c1,
    a2, f2, g2, v2, r2, x2_part, e2, m2, q2, w2, s2, p2, c2,
    a3, r3, g3, k3, w3, b3, s3, p3, t3, u3, line, lines,
    table, down, up, rise_fine, rise_second, last_down, last_up, last_rise,
    mixers, smoothers, send_sem, recv_sem, local_sem,
):
    mx, my = lax.axis_index("gx"), lax.axis_index("gy")

    def device(dx, dy):
        return (lax.rem(mx + (dx + nx), nx), lax.rem(my + (dy + ny), ny))

    barrier = pltpu.get_barrier_semaphore()
    peers = [(0, k) for k in range(1, ny)]
    peers += [(dx, dy) for dx in (-1, 1) for dy in (-1, 0, 1)] + [(-2, 0), (2, 0)]
    x0, y0 = f0.shape[1:3]
    x1, y1 = f1.shape[1:3]
    x2, y2 = f2.shape[:2]
    x3, y3 = a3.shape[:2]
    first_rows = min(4, x0 // 4)
    parts = [(0, first_rows), (x0 - first_rows, first_rows), (first_rows, x0 - 2 * first_rows)]
    load_fine = pltpu.make_async_copy(fine, a0.at[pl.ds(1, x0)], local_sem.at[0])
    load_parts = [
        pltpu.make_async_copy(
            source.at[:, pl.ds(x, xs)], f0.at[:, pl.ds(x, xs)], local_sem.at[4 + n]
        )
        for n, (x, xs) in enumerate(parts)
    ]
    load_coarser = [
        pltpu.make_async_copy(second, a1, local_sem.at[1]),
        pltpu.make_async_copy(third, a2, local_sem.at[2]),
        pltpu.make_async_copy(coarse, a3, local_sem.at[3]),
    ]
    load_smoothers = pltpu.make_async_copy(smoothers_in, smoothers, local_sem.at[7])
    load_mixers = pltpu.make_async_copy(mixers_in, mixers, local_sem.at[8])
    for load in [load_smoothers] + load_parts + [load_fine, load_mixers] + load_coarser:
        load.start()
    for dx, dy in peers:
        pl.semaphore_signal(barrier, inc=1, device_id=device(dx, dy), device_id_type=MESH)

    def smooth_matrix(level):
        return [
            [smoothers[level, i, j] + (0.25 if i == j else 0.0) for j in range(4)]
            for i in range(4)
        ]

    def mix_matrix(level):
        return [
            [mixers[level, i, j] + (1.0 if i == j else 0.0) for j in range(4)] for i in range(4)
        ]

    def product(left, right):
        return [
            [sum(left[i][k] * right[k][j] for k in range(4)) for j in range(4)] for i in range(4)
        ]

    lane = lane_index((1, LANES))
    rows_used = [0]

    def keep(vector):
        row = rows_used[0]
        rows_used[0] += 1
        table[row : row + 1, :] = vector
        return row

    def pair_rows(matrix):
        return [
            [
                [
                    keep(
                        jnp.where(
                            lane < 64,
                            matrix[2 * g][2 * h + s],
                            matrix[2 * g + 1][2 * h + 1 - s],
                        )
                    )
                    for s in range(2)
                ]
                for h in range(2)
            ]
            for g in range(2)
        ]

    def quad_rows(matrix, segment):
        channel = (lane // segment) % 4
        rows = []
        for k in range(4):
            vector = jnp.zeros((1, LANES), F32)
            for i in range(4):
                vector = jnp.where(channel == i, matrix[i][(i - k) % 4], vector)
            rows.append(keep(vector))
        return rows

    load_smoothers.wait()
    S0 = smooth_matrix(0)

    def mixed4(matrix, fields):
        return [
            matrix[i][0] * fields[0]
            + matrix[i][1] * fields[1]
            + (matrix[i][2] * fields[2] + matrix[i][3] * fields[3])
            for i in range(4)
        ]

    def vector_of(row):
        return table[row : row + 1, :]

    def mixed2(rows, fields):
        turned = [pltpu.roll(field, 64, field.ndim - 1) for field in fields]
        return [
            vector_of(rows[g][0][0]) * fields[0]
            + vector_of(rows[g][0][1]) * turned[0]
            + (vector_of(rows[g][1][0]) * fields[1] + vector_of(rows[g][1][1]) * turned[1])
            for g in range(2)
        ]

    def mixed1(rows, field, segment):
        total = vector_of(rows[0]) * field
        for k in range(1, 4):
            total += vector_of(rows[k]) * pltpu.roll(field, k * segment, field.ndim - 1)
        return total

    def row_index(shape):
        return lax.broadcasted_iota(jnp.int32, shape, 0)

    def children_matrix(columns, segment):
        shape = (2 * LANES, columns)
        row, column = row_index(shape) % LANES, lane_index(shape)
        if segment is None:
            return jnp.where(row == column // 2, 1.0, 0.0).astype(BF16)
        odd = column % 2
        other = column // 2 + 2 * odd - 1
        place = column % segment
        valid = (place != 0) & (place != segment - 1)
        own = jnp.where(row == column // 2, 3.0, 0.0)
        return (own - jnp.where((row == other) & valid, 1.0, 0.0)).astype(BF16)

    started = []

    def send(src, dst, place):
        number = len(started)
        copy = pltpu.make_async_remote_copy(
            src_ref=src, dst_ref=dst, send_sem=send_sem.at[number], recv_sem=recv_sem.at[number],
            device_id=device(*place), device_id_type=MESH,
        )
        copy.start()
        started.append(copy)
        return copy

    def pack(g, s, planes, h, xs, ys):
        for p, (k, c) in enumerate(planes):
            s[0, p, 0:xs, :] = g[c, h : h + xs, PAD + k, :]
            s[1, p, 0:xs, :] = g[c, h : h + xs, PAD + ys - 1 - k, :]

    def send_corners(s, corner, xs, near):
        copies = []
        first, last = pl.ds(0, 8), pl.ds(max(xs - 8, 0), 8)
        for side, dy in ((1, 1), (0, -1)):
            for end, dx in ((last, 1), (first, -1)):
                copies.append(
                    send(
                        s.at[side, pl.ds(0, near), end],
                        corner.at[(0 if dx > 0 else 1) * 2 + (0 if dy > 0 else 1)],
                        (dx, dy),
                    )
                )
        return copies

    def exchange(g, s, p, corner, h, xs, ys, near):
        own = pl.ds(PAD, ys)
        copies = [
            send(g.at[:, pl.ds(xs, h), own], g.at[:, pl.ds(0, h), own], (1, 0)),
            send(g.at[:, pl.ds(h, h), own], g.at[:, pl.ds(xs + h, h), own], (-1, 0)),
        ]
        copies += send_corners(s, corner, xs, near)
        copies.append(send(s.at[1], p.at[0], (0, 1)))
        copies.append(send(s.at[0], p.at[1], (0, -1)))
        return copies

    def unpack(copies, g, p, corner, planes, h, xs, ys, near, reach, a_reach):
        for copy in copies:
            copy.wait_recv()
        groups = g.shape[0]
        for n, (k, c) in enumerate(planes):
            g[c, h : h + xs, PAD - 1 - k, :] = p[0, n, 0:xs, :]
            g[c, h : h + xs, PAD + ys + k, :] = p[1, n, 0:xs, :]
        top = min(xs, 8) - 1
        for n, (k, c) in enumerate(planes[:near]):
            for i in range((a_reach if c == groups - 1 else reach) - 1 - k):
                for from_dy in range(2):
                    row = PAD - 1 - k if from_dy == 0 else PAD + ys + k
                    g[c, h - 1 - i, row : row + 1, :] = corner[from_dy, n, top - i : top - i + 1, :]
                    g[c, h + xs + i, row : row + 1, :] = corner[2 + from_dy, n, i : i + 1, :]

        @pl.when(mx == 0)
        def _():
            g[:, 0:h] = jnp.zeros((groups, h) + g.shape[2:], F32)

        @pl.when(mx == nx - 1)
        def _():
            g[:, h + xs :] = jnp.zeros((groups, h) + g.shape[2:], F32)

        @pl.when(my == 0)
        def _():
            g[:, :, 0:PAD] = jnp.zeros(g.shape[:2] + (PAD, LANES), F32)

        @pl.when(my == ny - 1)
        def _():
            g[:, :, PAD + ys :] = jnp.zeros(g.shape[:2] + (PAD, LANES), F32)

    def steps(count, body):
        def step(i, carry):
            body(i)
            return carry

        lax.fori_loop(0, count, step, 0)

    def stencil_of(field, coefficient, c, x, row, rows, segment):
        center = field[c, x, row : row + rows, :]
        beside = field[c, x - 1, row : row + rows, :] + field[c, x + 1, row : row + rows, :]
        beside += field[c, x, row - 1 : row - 1 + rows, :]
        beside += field[c, x, row + 1 : row + 1 + rows, :]
        return stencil(center, beside, coefficient, segment)

    y_rows = y0 + 2 * PAD

    def fine_rows(buffer, c, x, row, rows):
        start = x * y_rows + row
        if row % 8 == 0:
            start = pl.multiple_of(start, 8)
        return buffer[c, pl.ds(start, rows), :]

    def fine_plane(row):
        return pl.ds(2 * y_rows + row, x0, stride=y_rows)

    def fine_stencil(buffer, coefficient, c, x):
        center = fine_rows(buffer, c, x, PAD, y0)
        beside = fine_rows(buffer, c, x - 1, PAD, y0) + fine_rows(buffer, c, x + 1, PAD, y0)
        beside += fine_rows(buffer, c, x, PAD - 1, y0) + fine_rows(buffer, c, x, PAD + 1, y0)
        return stencil(center, beside, coefficient, LANES)

    def smooth_fine(x):
        fields = mixed4(S0, [f0[c, x] for c in range(4)])
        for c in range(4):
            start = pl.multiple_of((x + 2) * y_rows + PAD, 8)
            g0[c, pl.ds(start, y0), :] = fields[c]

    def smooth_part(n):
        load_parts[n].wait()
        x, xs = parts[n]
        steps(xs, lambda i: smooth_fine(i + x))

    smooth_part(0)
    smooth_part(1)
    load_fine.wait()
    pl.semaphore_wait(barrier, len(peers))
    copies = []
    for layer, dst, dx in ((x0 + 1, 1, 1), (2, x0 + 2, -1), (x0, 0, 1), (3, x0 + 3, -1)):
        copies.append(
            send(
                g0.at[:, pl.ds(layer * y_rows + PAD, y0)],
                g0.at[:, pl.ds(dst * y_rows + PAD, y0)],
                (dx, 0),
            )
        )
    copies.append(send(a0.at[pl.ds(x0, 1)], a0.at[pl.ds(0, 1)], (1, 0)))
    copies.append(send(a0.at[pl.ds(1, 1)], a0.at[pl.ds(x0 + 1, 1)], (-1, 0)))
    smooth_part(2)
    for c in range(4):
        for k in range(2):
            n = c if k == 0 else 5 + c
            s0[0, n] = g0[c, fine_plane(PAD + k), :]
            s0[1, n] = g0[c, fine_plane(PAD + y0 - 1 - k), :]
    s0[0, 4] = a0[1 : x0 + 1, 0, :]
    s0[1, 4] = a0[1 : x0 + 1, y0 - 1, :]
    copies += send_corners(s0, c0, x0, 4)
    copies.append(send(s0.at[1], p0.at[0], (0, 1)))
    copies.append(send(s0.at[0], p0.at[1], (0, -1)))

    for c in range(4):
        for row in (PAD - 1, PAD + y0):
            g0[c, fine_plane(row), :] = jnp.zeros((x0, LANES), F32)
    load_mixers.wait()
    B0 = mix_matrix(0)
    T0 = product(S0, B0)

    def relax_fine(x):
        coefficient = a0[x - 1]
        change = mixed4(T0, [fine_stencil(g0, coefficient, c, x) for c in range(4)])
        for c in range(4):
            value = 2.0 * fine_rows(g0, c, x, PAD, y0) - change[c]
            v0[c, pl.ds(pl.multiple_of(x * y_rows + PAD, 8), y0), :] = value

    steps(x0 - 2, lambda i: relax_fine(i + 3))
    for load in load_coarser:
        load.wait()
    third_cells = jnp.concatenate([a3[...]] * 8, axis=-1)
    k3[4 : 4 + x3, PAD : PAD + y3, :] = third_cells
    for x in range(x3):
        t3[x * y3 : (x + 1) * y3, :] = third_cells[x]
    coarse_copies = [send(t3, u3.at[0], (0, 1)), send(t3, u3.at[1], (0, -1))]
    g1[2, 3 : 3 + x1, PAD : PAD + y1, :] = jnp.concatenate([a1[...]] * 2, axis=-1)
    g2[1, 3 : 3 + x2, PAD : PAD + y2, :] = jnp.concatenate([a2[...]] * 4, axis=-1)
    smooth1, mixer1 = smooth_matrix(1), mix_matrix(1)
    S1, B1, T1 = pair_rows(smooth1), pair_rows(mixer1), pair_rows(product(smooth1, mixer1))
    smooth2, mixer2 = smooth_matrix(2), mix_matrix(2)
    S2, B2 = quad_rows(smooth2, 32), quad_rows(mixer2, 32)
    T2 = quad_rows(product(smooth2, mixer2), 32)
    smooth3, mixer3 = smooth_matrix(3), mix_matrix(3)
    S3, T3 = quad_rows(smooth3, 16), quad_rows(product(smooth3, mixer3), 16)
    T0_below = pair_rows(T0)
    T1_below = quad_rows(product(smooth1, mixer1), 32)
    T2_below = quad_rows(product(smooth2, mixer2), 16)

    wide, narrow = (2 * LANES, LANES), (LANES, LANES)
    down[...] = jnp.where(row_index(wide) // 2 == lane_index(wide), 0.125, 0.0).astype(BF16)
    last_down[...] = jnp.where(
        row_index(narrow) // 2 == lane_index(narrow) % 64, 0.125, 0.0
    ).astype(BF16)
    up[...] = children_matrix(2 * LANES, None)
    rise_fine[...] = children_matrix(2 * LANES, LANES)
    rise_second[...] = children_matrix(2 * LANES, 64)
    last_up[...] = children_matrix(LANES, None)
    last_rise[...] = children_matrix(LANES, 32)

    for copy in copies:
        copy.wait_recv()

    @pl.when(mx == 0)
    def _():
        g0[:, 0 : 2 * y_rows] = jnp.zeros((4, 2 * y_rows, LANES), F32)
        c0[0:2] = jnp.zeros((2,) + c0.shape[1:], F32)
        a0[0] = jnp.zeros((y0, LANES), F32)

    @pl.when(mx == nx - 1)
    def _():
        g0[:, (x0 + 2) * y_rows :] = jnp.zeros((4, 2 * y_rows, LANES), F32)
        c0[2:4] = jnp.zeros((2,) + c0.shape[1:], F32)
        a0[x0 + 1] = jnp.zeros((y0, LANES), F32)

    for side, edge in ((0, 0), (1, ny - 1)):

        @pl.when(my == edge)
        def _(side=side):
            p0[side] = jnp.zeros(p0.shape[1:], F32)
            c0[side] = jnp.zeros(c0.shape[1:], F32)
            c0[2 + side] = jnp.zeros(c0.shape[1:], F32)

    for c in range(4):
        for side, row in ((0, PAD - 1), (1, PAD + y0)):
            left, right = c0[side, c, 7:8, :], c0[2 + side, c, 0:1, :]
            g0[c, y_rows + row : y_rows + row + 1, :] = left
            g0[c, (x0 + 2) * y_rows + row : (x0 + 2) * y_rows + row + 1, :] = right
            h0[side, c, PAD - 1 : PAD, :] = left
            h0[side, c, PAD + x0 : PAD + x0 + 1, :] = right
            h0[side, c, PAD : PAD + x0, :] = p0[side, c]
    steps(4, lambda i: relax_fine(1 + i + (x0 - 2) * (i // 2)))
    for side, own, halo in ((0, PAD, PAD - 1), (1, PAD + y0 - 1, PAD + y0)):
        near = [p0[side, c] for c in range(4)]
        change = mixed4(T0, [s0[side, 4] * near[c] for c in range(4)])
        for c in range(4):
            v0[c, fine_plane(own), :] += change[c]
        applied = []
        for c in range(4):
            beside = h0[side, c, PAD - 1 : PAD - 1 + x0, :] + h0[side, c, PAD + 1 : PAD + 1 + x0, :]
            beside += p0[side, 5 + c] + s0[side, c]
            applied.append(stencil(near[c], beside, p0[side, 4], LANES))
        change = mixed4(T0, applied)
        for c in range(4):
            v0[c, fine_plane(halo), :] = 2.0 * near[c] - change[c]

    def residual_fine(i):
        total = [None] * 4
        for s in range(2):
            x = 2 * i + s
            applied = mixed4(B0, [fine_stencil(v0, a0[x + 1], c, x + 2) for c in range(4)])
            for c in range(4):
                rest = f0[c, x] - applied[c]
                total[c] = rest if s == 0 else total[c] + rest
        for c in range(4):
            r0[c, i] = total[c]

    steps(x1, residual_fine)

    for g in range(2):
        pieces = [
            r0[c, :, pl.ds(0, y1, stride=2), :] + r0[c, :, pl.ds(1, y1, stride=2), :]
            for c in (2 * g, 2 * g + 1)
        ]
        joined = jnp.concatenate([piece.reshape(x1 * y1, LANES) for piece in pieces], axis=-1)
        f1[g] = spread(joined, down[...]).reshape(x1, y1, LANES)
    fields = mixed2(S1, [f1[g] for g in range(2)])
    for g in range(2):
        g1[g, 3 : 3 + x1, PAD : PAD + y1, :] = fields[g]
    planes1 = [(0, 0), (0, 1), (0, 2), (1, 0), (1, 1), (1, 2), (2, 0), (2, 1)]
    pack(g1, s1, planes1, 3, x1, y1)
    copies = exchange(g1, s1, p1, c1, 3, x1, y1, 5)

    def fill_beside(buffer, received):
        for side, row in ((0, PAD - y3), (1, PAD + y3)):
            inside = (my > 0) if side == 0 else (my < ny - 1)
            for x in range(x3):
                buffer[4 + x, row : row + y3, :] = jnp.where(
                    inside, received[side, x * y3 : (x + 1) * y3, :], 0.0
                )

    def send_block(buffer):
        block, used = pl.ds(4, x3), pl.ds(0, 2 * PAD)
        return [
            send(buffer.at[block, used], buffer.at[pl.ds(4 - dx * x3, x3), used], (dx, 0))
            for dx in (1, -1, 2, -2)
        ]

    def receive_block(buffer, copies):
        for copy in copies:
            copy.wait_recv()
        for dx in (1, -1, 2, -2):
            outside = (mx < dx) if dx > 0 else (mx >= nx + dx)

            @pl.when(outside)
            def _(dx=dx):
                buffer[4 - dx * x3 : 4 - dx * x3 + x3] = jnp.zeros((x3,) + buffer.shape[1:], F32)

    for copy in coarse_copies:
        copy.wait_recv()
    fill_beside(k3, u3)
    coarse_copies = send_block(k3)

    def settle_fine(x):
        change = mixed4(T0, [fine_stencil(v0, a0[x + 1], c, x + 2) for c in range(4)])
        for c in range(4):
            value = fine_rows(v0, c, x + 2, PAD, y0) + fine_rows(g0, c, x + 2, PAD, y0)
            f0[c, x] = value - change[c]

    steps(x0, settle_fine)
    unpack(copies, g1, p1, c1, planes1, 3, x1, y1, 5, 3, 2)

    def relax_second(step):
        x = step + 1
        row, rows = PAD - 2, y1 + 4
        coefficient = g1[2, x, row : row + rows, :]
        change = mixed2(T1, [stencil_of(g1, coefficient, c, x, row, rows, 64) for c in range(2)])
        for c in range(2):
            v1[c, x, row : row + rows, :] = 2.0 * g1[c, x, row : row + rows, :] - change[c]

    steps(x1 + 4, relax_second)

    def residual_second(i):
        total = [None] * 2
        for s in range(2):
            x = 2 * i + s
            coefficient = g1[2, x + 3, PAD : PAD + y1, :]
            applied = mixed2(
                B1, [stencil_of(v1, coefficient, c, x + 3, PAD, y1, 64) for c in range(2)]
            )
            for c in range(2):
                rest = f1[c, x] - applied[c]
                total[c] = rest if s == 0 else total[c] + rest
        for c in range(2):
            r1[c, i] = total[c]

    steps(x2, residual_second)

    pieces = [
        r1[c, :, pl.ds(0, y2, stride=2), :] + r1[c, :, pl.ds(1, y2, stride=2), :] for c in range(2)
    ]
    joined = jnp.concatenate([piece.reshape(x2 * y2, LANES) for piece in pieces], axis=-1)
    f2[...] = spread(joined, down[...]).reshape(x2, y2, LANES)
    g2[0, 3 : 3 + x2, PAD : PAD + y2, :] = mixed1(S2, f2[...], 32)
    planes2 = [(0, 0), (0, 1), (1, 0), (1, 1), (2, 0)]
    pack(g2, s2, planes2, 3, x2, y2)
    copies = exchange(g2, s2, p2, c2, 3, x2, y2, 5)
    receive_block(k3, coarse_copies)

    def settle_second(step):
        x = step + 2
        row, rows = PAD - 1, y1 + 2
        coefficient = g1[2, x, row : row + rows, :]
        change = mixed2(T1, [stencil_of(v1, coefficient, c, x, row, rows, 64) for c in range(2)])
        for c in range(2):
            value = v1[c, x, row : row + rows, :] + g1[c, x, row : row + rows, :] - change[c]
            x1_part[c, step, row : row + rows, :] = value

    steps(x1 + 2, settle_second)
    unpack(copies, g2, p2, c2, planes2, 3, x2, y2, 5, 4, 3)

    def block_stencil(load, coefficient, x, xs, row, rows, segment):
        center = load(x, xs, row, rows)
        beside = load(x - 1, xs, row, rows) + load(x + 1, xs, row, rows)
        beside += load(x, xs, row - 1, rows) + load(x, xs, row + 1, rows)
        return center, stencil(center, beside, coefficient, segment)

    def from_g2(x, xs, row, rows):
        return g2[0, x : x + xs, row : row + rows, :]

    def from_v2(x, xs, row, rows):
        return v2[x : x + xs, row : row + rows, :]

    row, rows = PAD - 2, y2 + 4
    center, applied = block_stencil(
        from_g2, g2[1, 1 : x2 + 5, row : row + rows, :], 1, x2 + 4, row, rows, 32
    )
    v2[1 : x2 + 5, row : row + rows, :] = 2.0 * center - mixed1(T2, applied, 32)
    _, applied = block_stencil(
        from_v2, g2[1, 3 : 3 + x2, PAD : PAD + y2, :], 3, x2, PAD, y2, 32
    )
    rest = f2[...] - mixed1(B2, applied, 32)
    pairs = jnp.concatenate([rest[2 * i] + rest[2 * i + 1] for i in range(x3)], axis=0)
    r3[...] = spread(pairs, last_down[...]).reshape(x3, y2, LANES)

    forcing = r3[:, pl.ds(0, y3, stride=2), :] + r3[:, pl.ds(1, y3, stride=2), :]
    smoothed = mixed1(S3, forcing, 16)
    g3[4 : 4 + x3, PAD : PAD + y3, :] = smoothed
    for x in range(x3):
        s3[x * y3 : (x + 1) * y3, :] = smoothed[x]
        line[x : x + 1, :] = jnp.sum(smoothed[x], axis=0, keepdims=True)
    copies = [send(line, lines.at[k - 1], (0, k)) for k in range(1, ny)]
    copies += [send(s3, p3.at[0], (0, 1)), send(s3, p3.at[1], (0, -1))]
    row, rows = PAD - 1, y2 + 2
    center, applied = block_stencil(
        from_v2, g2[1, 2 : x2 + 4, row : row + rows, :], 2, x2 + 2, row, rows, 32
    )
    x2_part[:, row : row + rows, :] = (
        center + g2[0, 2 : x2 + 4, row : row + rows, :] - mixed1(T2, applied, 32)
    )
    for copy in copies:
        copy.wait_recv()
    total = line[...]
    for k in range(1, ny):
        total += lines[k - 1]
    total *= 4.0 / math.sqrt(ny * y3)
    for x in range(x3):
        g3[4 + x, 0:1, :] = total[x : x + 1, :]
    fill_beside(g3, p3)
    receive_block(g3, send_block(g3))

    low, high = PAD - y3, PAD + 2 * y3
    cell = lax.broadcasted_iota(jnp.int32, (1, 3 * y3, LANES), 1) + (my - 1) * y3
    inside = (cell >= 0) & (cell < ny * y3)
    w3[:, low:high, :] = g3[:, low:high, :] + jnp.where(inside, g3[:, 0:1, :], 0.0)

    def from_w3(x, xs, row, rows):
        return w3[x : x + xs, row : row + rows, :]

    for sweep in range(1, 4):
        x, xs = sweep, 8 + x3 - 2 * sweep
        row, rows = low + sweep, high - low - 2 * sweep
        center, applied = block_stencil(
            from_w3, k3[x : x + xs, row : row + rows, :], x, xs, row, rows, 16
        )
        value = center + g3[x : x + xs, row : row + rows, :] - mixed1(T3, applied, 16)
        if sweep < 3:
            w3[x : x + xs, row : row + rows, :] = value
        else:
            b3[:, row : row + rows, :] = value

    below = b3[...]
    mixed = mixed1(T2_below, below, 16)
    flat = ((x3 + 2) * 2 * PAD, LANES)
    e2[...] = spread_stacked((below - mixed).reshape(flat), last_up[...]).reshape(e2.shape)
    m2[...] = spread_stacked(mixed.reshape(flat), last_rise[...]).reshape(m2.shape)
    q2[...] = spread_stacked(mixed.reshape(flat), last_up[...]).reshape(q2.shape)

    def raised(m, q, c, i, s, t, row, rows):
        other_y = q[c, i, row + 2 * t - 1 : row + 2 * t - 1 + rows, :]
        other_x = q[c, i + 2 * s - 1, row : row + rows, :]
        return m[c, i, row : row + rows, :] - other_y - other_x

    for x in range(-1, x2 + 1):
        i, s = x // 2 + 1, x % 2
        for t in range(2):
            row, rows = PAD - t, y3 + 1
            cells = pl.ds(PAD - t, rows, stride=2)
            value = raised(m2, q2, 0, i, s, t, row, rows)
            w2[x + 1, cells, :] = (
                x2_part[x + 1, cells, :]
                + e2[0, i, row : row + rows, :]
                - g2[1, x + 3, cells, :] * value
            )

    below = w2[...]
    mixed = mixed1(T1_below, below, 32)
    flat = ((x2 + 2) * (y2 + 2 * PAD), LANES)
    shape = (x2 + 2, y2 + 2 * PAD, LANES)
    for field, matrix, target in (
        (below - mixed, up, e1),
        (mixed, rise_second, m1),
        (mixed, up, q1),
    ):
        children = spread_stacked(field.reshape(flat), matrix[...])
        for c in range(2):
            target[c] = children[:, c * LANES : (c + 1) * LANES].reshape(shape)
    for x in range(-1, x1 + 1):
        i, s = x // 2 + 1, x % 2
        for t in range(2):
            row, rows = PAD - t, y2 + 1
            cells = pl.ds(PAD - t, rows, stride=2)
            coefficient = g1[2, x + 3, cells, :]
            for c in range(2):
                value = raised(m1, q1, c, i, s, t, row, rows)
                w1[c, x + 1, cells, :] = (
                    x1_part[c, x + 1, cells, :]
                    + e1[c, i, row : row + rows, :]
                    - coefficient * value
                )

    below = [w1[c] for c in range(2)]
    mixed = mixed2(T0_below, below)
    own = slice(1, x1 + 1), slice(PAD, PAD + y1)
    for g in range(2):
        inner = (x1 * y1, LANES)
        for field, matrix, target in (
            ((below[g] - mixed[g])[own].reshape(inner), up, e0),
            (mixed[g][own].reshape(inner), rise_fine, m0),
        ):
            children = spread_stacked(field, matrix[...])
            for c in range(2):
                part = children[:, c * LANES : (c + 1) * LANES]
                target[2 * g + c, 1 : x1 + 1, PAD : PAD + y1, :] = part.reshape(x1, y1, LANES)
        children = spread_stacked(
            mixed[g].reshape((x1 + 2) * (y1 + 2 * PAD), LANES), up[...]
        )
        for c in range(2):
            part = children[:, c * LANES : (c + 1) * LANES]
            q0[2 * g + c] = part.reshape(x1 + 2, y1 + 2 * PAD, LANES)

    def finish_fine(step):
        i = step + 1
        for t in range(2):
            cells = pl.ds(t, y1, stride=2)
            coefficient = [a0[2 * step + s + 1, pl.ds(t, y1, stride=2), :] for s in range(2)]
            for c in range(4):
                for s in range(2):
                    value = raised(m0, q0, c, i, s, t, PAD, y1)
                    x = 2 * step + s
                    out[c, x, cells, :] = (
                        f0[c, x, cells, :]
                        + e0[c, i, PAD : PAD + y1, :]
                        - coefficient[s] * value
                    )

    steps(x1, finish_fine)
    for copy in started:
        copy.wait_send()


def per_device(nx, ny, source, fine, second, third, coarse, mixers, smoothers):
    x0, y0 = source.shape[1:3]
    x1, y1 = second.shape[:2]
    x2, y2 = third.shape[:2]
    x3, y3 = coarse.shape[:2]

    def padded(groups, xs, ys, h):
        return pltpu.VMEM((groups, xs + 2 * h, ys + 2 * PAD, LANES), F32)

    def vmem(*shape):
        return pltpu.VMEM(shape, F32)

    def faces(planes, near, xs):
        rows = max(xs, 8)
        return [
            vmem(2, planes, rows, LANES),
            vmem(2, planes, rows, LANES),
            vmem(4, near, 8, LANES),
        ]

    def three(groups, xs, ys):
        return [vmem(groups, xs + 2, ys + 2 * PAD, LANES)] * 3

    double = pltpu.VMEM((2 * LANES, 2 * LANES), BF16)
    tall = pltpu.VMEM((2 * LANES, LANES), BF16)
    scratch = (
        [vmem(4, x0, y0, LANES), vmem(x0 + 2, y0, LANES)]
        + [vmem(4, (x0 + 4) * (y0 + 2 * PAD), LANES)] * 2
        + [vmem(2, 4, x0 + 2 * PAD, LANES)]
        + [vmem(4, x1, y0, LANES)]
        + three(4, x1, y1)
        + faces(9, 4, x0)
        + [vmem(*second.shape), vmem(2, x1, y1, LANES), padded(3, x1, y1, 3), padded(2, x1, y1, 3)]
        + [vmem(2, x2, y1, LANES), vmem(2, x1 + 2, y1 + 2 * PAD, LANES)]
        + three(2, x2, y2)
        + [vmem(2, x1 + 2, y1 + 2 * PAD, LANES)]
        + faces(8, 5, x1)
        + [vmem(*third.shape), vmem(x2, y2, LANES), padded(2, x2, y2, 3)]
        + [vmem(x2 + 6, y2 + 2 * PAD, LANES), vmem(x3, y2, LANES)]
        + [vmem(x2 + 2, y2 + 2 * PAD, LANES)]
        + [vmem(1, x3 + 2, 2 * PAD, LANES)] * 3
        + [vmem(x2 + 2, y2 + 2 * PAD, LANES)]
        + faces(5, 5, x2)
        + [vmem(*coarse.shape), vmem(x3, y2, LANES)]
        + [vmem(x3 + 8, 24, LANES)] * 3
        + [vmem(x3 + 2, 2 * PAD, LANES)]
        + [vmem(x3 * y3, LANES), vmem(2, x3 * y3, LANES)] * 2
        + [vmem(x3, LANES), vmem(ny - 1, x3, LANES)]
        + [vmem(64, LANES)]
        + [tall, double, double, double, pltpu.VMEM((LANES, LANES), BF16), tall, tall]
    )
    copies = 8 * 3 + 4 + 2 * 2 + (ny - 1) + 4 * 2
    scratch += [
        pltpu.SMEM(mixers.shape, F32),
        pltpu.SMEM(smoothers.shape, F32),
        pltpu.SemaphoreType.DMA((copies,)),
        pltpu.SemaphoreType.DMA((copies,)),
        pltpu.SemaphoreType.DMA((9,)),
    ]
    anywhere = pl.BlockSpec(memory_space=pl.ANY)
    return pl.pallas_call(
        functools.partial(kernel, nx, ny),
        out_shape=pltpu.VMEM(source.shape, F32),
        in_specs=[anywhere] * 7,
        out_specs=pl.BlockSpec(memory_space=pltpu.VMEM),
        scratch_shapes=scratch,
        compiler_params=pltpu.CompilerParams(
            collective_id=0, has_side_effects=True, vmem_limit_bytes=56 * 1024 * 1024
        ),
    )(source, fine, second, third, coarse, mixers, smoothers)


def solution(mesh):
    field, cells = P(None, "gx", "gy", None), P("gx", "gy", None)
    return jax.shard_map(
        functools.partial(per_device, mesh.shape["gx"], mesh.shape["gy"]),
        mesh=mesh,
        in_specs=(field, cells, cells, cells, cells, P(), P()),
        out_specs=field,
        check_vma=False,
    )
```

```python
import functools
import math

import jax
import jax.numpy as jnp
from jax import lax
from jax.experimental import pallas as pl
from jax.experimental.pallas import tpu as pltpu
from jax.sharding import PartitionSpec as P

MESH = pl.DeviceIdType.MESH
F32 = jnp.float32
BF16 = jnp.bfloat16
LANES = 128
PAD = 8


def spread(field, matrix):
    high = field.astype(BF16)
    low = (field - high.astype(F32)).astype(BF16)
    return jnp.dot(high, matrix, preferred_element_type=F32) + jnp.dot(
        low, matrix, preferred_element_type=F32
    )


def spread_stacked(field, matrix):
    high = field.astype(BF16)
    low = (field - high.astype(F32)).astype(BF16)
    return jnp.dot(jnp.concatenate([high, low], axis=-1), matrix, preferred_element_type=F32)


def lane_index(shape):
    return lax.broadcasted_iota(jnp.int32, shape, len(shape) - 1)


def beside_z(field, segment):
    lane = lane_index((1, LANES)) % segment
    axis = field.ndim - 1
    before = jnp.where(lane == 0, 0.0, pltpu.roll(field, 1, axis))
    after = jnp.where(lane == segment - 1, 0.0, pltpu.roll(field, LANES - 1, axis))
    return before + after


def stencil(center, beside, coefficient, segment):
    total = beside + beside_z(center, segment)
    return coefficient * (6.0 * center - total) + center


def kernel(
    nx, ny,
    source, fine, second, third, coarse, mixers_in, smoothers_in, out,
    fx, f0, a0, g0, v0, h0, r0, e0, m0, q0, s0, p0, d0, c0,
    a1, f1, g1, v1, r1, x1_part, e1, m1, q1, w1, s1, p1, d1, c1,
    a2, f2, g2, v2, r2, x2_part, e2, m2, q2, w2, s2, p2, d2, c2,
    a3, r3, g3, k3, w3, b3, s3, p3, t3, u3, b_k3, l_k3, b_g3, l_g3, line, lines,
    table, down, up, rise_fine, rise_second, last_down, last_up, last_rise,
    mixers, smoothers, send_sem, recv_sem, local_sem,
):
    mx, my = lax.axis_index("gx"), lax.axis_index("gy")

    def device(dx, dy):
        return (lax.rem(mx + (dx + nx), nx), lax.rem(my + (dy + ny), ny))

    barrier = pltpu.get_barrier_semaphore()
    peers = [(0, k) for k in range(1, ny)]
    peers += [(dx, dy) for dx in (-1, 1) for dy in (-1, 0, 1)] + [(-2, 0), (2, 0)]
    x0, y0 = f0.shape[1:3]
    x1, y1 = f1.shape[1:3]
    x2, y2 = f2.shape[:2]
    x3, y3 = a3.shape[:2]
    part_rows = x0 // 4
    parts = [(n * part_rows, part_rows) for n in range(4)]
    load_fine = pltpu.make_async_copy(fine, a0.at[pl.ds(1, x0)], local_sem.at[0])
    load_parts = [
        pltpu.make_async_copy(
            source.at[:, pl.ds(x, xs)], f0.at[:, pl.ds(x, xs)], local_sem.at[4 + n]
        )
        for n, (x, xs) in enumerate(parts)
    ]
    load_coarser = [
        pltpu.make_async_copy(second, a1, local_sem.at[1]),
        pltpu.make_async_copy(third, a2, local_sem.at[2]),
        pltpu.make_async_copy(coarse, a3, local_sem.at[3]),
    ]
    load_smoothers = pltpu.make_async_copy(smoothers_in, smoothers, local_sem.at[8])
    load_mixers = pltpu.make_async_copy(mixers_in, mixers, local_sem.at[9])
    for load in [load_smoothers] + load_parts + [load_fine, load_mixers] + load_coarser:
        load.start()
    for dx, dy in peers:
        pl.semaphore_signal(barrier, inc=1, device_id=device(dx, dy), device_id_type=MESH)

    def smooth_matrix(level):
        return [
            [smoothers[level, i, j] + (0.25 if i == j else 0.0) for j in range(4)]
            for i in range(4)
        ]

    def mix_matrix(level):
        return [
            [mixers[level, i, j] + (1.0 if i == j else 0.0) for j in range(4)] for i in range(4)
        ]

    def product(left, right):
        return [
            [sum(left[i][k] * right[k][j] for k in range(4)) for j in range(4)] for i in range(4)
        ]

    lane = lane_index((1, LANES))
    rows_used = [0]

    def keep(vector):
        row = rows_used[0]
        rows_used[0] += 1
        table[row : row + 1, :] = vector
        return row

    def pair_rows(matrix):
        return [
            [
                [
                    keep(
                        jnp.where(
                            lane < 64,
                            matrix[2 * g][2 * h + s],
                            matrix[2 * g + 1][2 * h + 1 - s],
                        )
                    )
                    for s in range(2)
                ]
                for h in range(2)
            ]
            for g in range(2)
        ]

    def quad_rows(matrix, segment):
        channel = (lane // segment) % 4
        rows = []
        for k in range(4):
            vector = jnp.zeros((1, LANES), F32)
            for i in range(4):
                vector = jnp.where(channel == i, matrix[i][(i - k) % 4], vector)
            rows.append(keep(vector))
        return rows

    load_smoothers.wait()
    S0 = smooth_matrix(0)

    def mixed4(matrix, fields):
        return [
            matrix[i][0] * fields[0]
            + matrix[i][1] * fields[1]
            + (matrix[i][2] * fields[2] + matrix[i][3] * fields[3])
            for i in range(4)
        ]

    def vector_of(row):
        return table[row : row + 1, :]

    def mixed2(rows, fields):
        turned = [pltpu.roll(field, 64, field.ndim - 1) for field in fields]
        return [
            vector_of(rows[g][0][0]) * fields[0]
            + vector_of(rows[g][0][1]) * turned[0]
            + (vector_of(rows[g][1][0]) * fields[1] + vector_of(rows[g][1][1]) * turned[1])
            for g in range(2)
        ]

    def mixed1(rows, field, segment):
        total = vector_of(rows[0]) * field
        for k in range(1, 4):
            total += vector_of(rows[k]) * pltpu.roll(field, k * segment, field.ndim - 1)
        return total

    def row_index(shape):
        return lax.broadcasted_iota(jnp.int32, shape, 0)

    def children_matrix(columns, segment):
        shape = (2 * LANES, columns)
        row, column = row_index(shape) % LANES, lane_index(shape)
        if segment is None:
            return jnp.where(row == column // 2, 1.0, 0.0).astype(BF16)
        odd = column % 2
        other = column // 2 + 2 * odd - 1
        place = column % segment
        valid = (place != 0) & (place != segment - 1)
        own = jnp.where(row == column // 2, 3.0, 0.0)
        return (own - jnp.where((row == other) & valid, 1.0, 0.0)).astype(BF16)

    started = []

    def send(src, dst, place):
        number = len(started)
        copy = pltpu.make_async_remote_copy(
            src_ref=src, dst_ref=dst, send_sem=send_sem.at[number], recv_sem=recv_sem.at[number],
            device_id=device(*place), device_id_type=MESH,
        )
        copy.start()
        started.append(copy)
        return copy

    def pack(g, s, planes, h, xs, ys):
        for p, (k, c) in enumerate(planes):
            s[0, p, 0:xs, :] = g[c, h : h + xs, PAD + k, :]
            s[1, p, 0:xs, :] = g[c, h : h + xs, PAD + ys - 1 - k, :]

    def corner_cells(planes, reach_of):
        return [
            (n, i) for n, (k, c) in enumerate(planes) for i in range(reach_of(c) - 1 - k)
        ]

    def send_corners(s, packed, corner, cells, xs):
        copies = []
        for side, dy in ((1, 1), (0, -1)):
            for dx in (1, -1):
                slot = (0 if dx > 0 else 1) * 2 + (0 if dy > 0 else 1)
                for r, (n, i) in enumerate(cells):
                    x = xs - 1 - i if dx > 0 else i
                    packed[slot, r : r + 1, :] = s[side, n, x : x + 1, :]
                copies.append(send(packed.at[slot], corner.at[slot], (dx, dy)))
        return copies

    def exchange(g, s, p, packed, corner, cells, h, xs, ys):
        own = pl.ds(PAD, ys)
        copies = [
            send(g.at[:, pl.ds(xs, h), own], g.at[:, pl.ds(0, h), own], (1, 0)),
            send(g.at[:, pl.ds(h, h), own], g.at[:, pl.ds(xs + h, h), own], (-1, 0)),
        ]
        copies += send_corners(s, packed, corner, cells, xs)
        copies.append(send(s.at[1], p.at[0], (0, 1)))
        copies.append(send(s.at[0], p.at[1], (0, -1)))
        return copies

    def unpack(copies, g, p, corner, cells, planes, h, xs, ys):
        for copy in copies:
            copy.wait_recv()
        groups = g.shape[0]
        for n, (k, c) in enumerate(planes):
            g[c, h : h + xs, PAD - 1 - k, :] = p[0, n, 0:xs, :]
            g[c, h : h + xs, PAD + ys + k, :] = p[1, n, 0:xs, :]
        for r, (n, i) in enumerate(cells):
            k, c = planes[n]
            for from_dy in range(2):
                row = PAD - 1 - k if from_dy == 0 else PAD + ys + k
                g[c, h - 1 - i, row : row + 1, :] = corner[from_dy, r : r + 1, :]
                g[c, h + xs + i, row : row + 1, :] = corner[2 + from_dy, r : r + 1, :]

        @pl.when(mx == 0)
        def _():
            g[:, 0:h] = jnp.zeros((groups, h) + g.shape[2:], F32)

        @pl.when(mx == nx - 1)
        def _():
            g[:, h + xs :] = jnp.zeros((groups, h) + g.shape[2:], F32)

        @pl.when(my == 0)
        def _():
            g[:, :, 0:PAD] = jnp.zeros(g.shape[:2] + (PAD, LANES), F32)

        @pl.when(my == ny - 1)
        def _():
            g[:, :, PAD + ys :] = jnp.zeros(g.shape[:2] + (PAD, LANES), F32)

    def steps(count, body):
        def step(i, carry):
            body(i)
            return carry

        lax.fori_loop(0, count, step, 0)

    def stencil_of(field, coefficient, c, x, row, rows, segment):
        center = field[c, x, row : row + rows, :]
        beside = field[c, x - 1, row : row + rows, :] + field[c, x + 1, row : row + rows, :]
        beside += field[c, x, row - 1 : row - 1 + rows, :]
        beside += field[c, x, row + 1 : row + 1 + rows, :]
        return stencil(center, beside, coefficient, segment)

    y_rows = y0 + 2 * PAD

    def fine_rows(buffer, c, x, row, rows):
        start = x * y_rows + row
        if row % 8 == 0:
            start = pl.multiple_of(start, 8)
        return buffer[c, pl.ds(start, rows), :]

    def fine_plane(row):
        return pl.ds(2 * y_rows + row, x0, stride=y_rows)

    def fine_stencil(buffer, coefficient, c, x):
        center = fine_rows(buffer, c, x, PAD, y0)
        beside = fine_rows(buffer, c, x - 1, PAD, y0) + fine_rows(buffer, c, x + 1, PAD, y0)
        beside += fine_rows(buffer, c, x, PAD - 1, y0) + fine_rows(buffer, c, x, PAD + 1, y0)
        return stencil(center, beside, coefficient, LANES)

    def smooth_fine(x):
        fields = mixed4(S0, [f0[c, x] for c in range(4)])
        for c in range(4):
            start = pl.multiple_of((x + 2) * y_rows + PAD, 8)
            g0[c, pl.ds(start, y0), :] = fields[c]

    def smooth_part(n):
        load_parts[n].wait()
        x, xs = parts[n]
        steps(xs, lambda i: smooth_fine(i + x))

    pl.semaphore_wait(barrier, len(peers))
    copies = [
        send(source.at[:, pl.ds(x0 - 2, 2)], fx.at[0], (1, 0)),
        send(source.at[:, pl.ds(0, 2)], fx.at[1], (-1, 0)),
        send(fine.at[pl.ds(x0 - 1, 1)], a0.at[pl.ds(0, 1)], (1, 0)),
        send(fine.at[pl.ds(0, 1)], a0.at[pl.ds(x0 + 1, 1)], (-1, 0)),
    ]
    for n in range(len(parts)):
        smooth_part(n)
    load_fine.wait()
    for c in range(4):
        for k in range(2):
            n = c if k == 0 else 5 + c
            s0[0, n] = g0[c, fine_plane(PAD + k), :]
            s0[1, n] = g0[c, fine_plane(PAD + y0 - 1 - k), :]
    s0[0, 4] = a0[1 : x0 + 1, 0, :]
    s0[1, 4] = a0[1 : x0 + 1, y0 - 1, :]
    copies += send_corners(s0, d0, c0, [(c, 0) for c in range(4)], x0)
    copies.append(send(s0.at[1], p0.at[0], (0, 1)))
    copies.append(send(s0.at[0], p0.at[1], (0, -1)))

    for c in range(4):
        for row in (PAD - 1, PAD + y0):
            g0[c, fine_plane(row), :] = jnp.zeros((x0, LANES), F32)
    load_mixers.wait()
    B0 = mix_matrix(0)
    T0 = product(S0, B0)

    def relax_fine(x):
        coefficient = a0[x - 1]
        change = mixed4(T0, [fine_stencil(g0, coefficient, c, x) for c in range(4)])
        for c in range(4):
            value = 2.0 * fine_rows(g0, c, x, PAD, y0) - change[c]
            v0[c, pl.ds(pl.multiple_of(x * y_rows + PAD, 8), y0), :] = value

    steps(x0 - 2, lambda i: relax_fine(i + 3))
    for load in load_coarser:
        load.wait()
    third_cells = jnp.concatenate([a3[...]] * 8, axis=-1)
    k3[4 : 4 + x3, PAD : PAD + y3, :] = third_cells
    for x in range(x3):
        t3[x * y3 : (x + 1) * y3, :] = third_cells[x]
    coarse_copies = [send(t3, u3.at[0], (0, 1)), send(t3, u3.at[1], (0, -1))]
    g1[2, 3 : 3 + x1, PAD : PAD + y1, :] = jnp.concatenate([a1[...]] * 2, axis=-1)
    g2[1, 3 : 3 + x2, PAD : PAD + y2, :] = jnp.concatenate([a2[...]] * 4, axis=-1)
    smooth1, mixer1 = smooth_matrix(1), mix_matrix(1)
    S1, B1, T1 = pair_rows(smooth1), pair_rows(mixer1), pair_rows(product(smooth1, mixer1))
    smooth2, mixer2 = smooth_matrix(2), mix_matrix(2)
    S2, B2 = quad_rows(smooth2, 32), quad_rows(mixer2, 32)
    T2 = quad_rows(product(smooth2, mixer2), 32)
    smooth3, mixer3 = smooth_matrix(3), mix_matrix(3)
    S3, T3 = quad_rows(smooth3, 16), quad_rows(product(smooth3, mixer3), 16)
    T0_below = pair_rows(T0)
    T1_below = quad_rows(product(smooth1, mixer1), 32)
    T2_below = quad_rows(product(smooth2, mixer2), 16)

    wide, narrow = (2 * LANES, LANES), (LANES, LANES)
    down[...] = jnp.where(row_index(wide) // 2 == lane_index(wide), 0.125, 0.0).astype(BF16)
    last_down[...] = jnp.where(
        row_index(narrow) // 2 == lane_index(narrow) % 64, 0.125, 0.0
    ).astype(BF16)
    up[...] = children_matrix(2 * LANES, None)
    rise_fine[...] = children_matrix(2 * LANES, LANES)
    rise_second[...] = children_matrix(2 * LANES, 64)
    last_up[...] = children_matrix(LANES, None)
    last_rise[...] = children_matrix(LANES, 32)

    for copy in copies:
        copy.wait_recv()

    def smooth_beside(i):
        fields = mixed4(S0, [fx[i // 2, c, i % 2] for c in range(4)])
        for c in range(4):
            start = pl.multiple_of((i + x0 * (i // 2)) * y_rows + PAD, 8)
            g0[c, pl.ds(start, y0), :] = fields[c]

    steps(4, smooth_beside)

    @pl.when(mx == 0)
    def _():
        g0[:, 0 : 2 * y_rows] = jnp.zeros((4, 2 * y_rows, LANES), F32)
        c0[0:2] = jnp.zeros((2,) + c0.shape[1:], F32)
        a0[0] = jnp.zeros((y0, LANES), F32)

    @pl.when(mx == nx - 1)
    def _():
        g0[:, (x0 + 2) * y_rows :] = jnp.zeros((4, 2 * y_rows, LANES), F32)
        c0[2:4] = jnp.zeros((2,) + c0.shape[1:], F32)
        a0[x0 + 1] = jnp.zeros((y0, LANES), F32)

    for side, edge in ((0, 0), (1, ny - 1)):

        @pl.when(my == edge)
        def _(side=side):
            p0[side] = jnp.zeros(p0.shape[1:], F32)
            c0[side] = jnp.zeros(c0.shape[1:], F32)
            c0[2 + side] = jnp.zeros(c0.shape[1:], F32)

    for c in range(4):
        for side, row in ((0, PAD - 1), (1, PAD + y0)):
            left, right = c0[side, c : c + 1, :], c0[2 + side, c : c + 1, :]
            g0[c, y_rows + row : y_rows + row + 1, :] = left
            g0[c, (x0 + 2) * y_rows + row : (x0 + 2) * y_rows + row + 1, :] = right
            h0[side, c, PAD - 1 : PAD, :] = left
            h0[side, c, PAD + x0 : PAD + x0 + 1, :] = right
            h0[side, c, PAD : PAD + x0, :] = p0[side, c]
    steps(4, lambda i: relax_fine(1 + i + (x0 - 2) * (i // 2)))
    for side, own, halo in ((0, PAD, PAD - 1), (1, PAD + y0 - 1, PAD + y0)):
        near = [p0[side, c] for c in range(4)]
        change = mixed4(T0, [s0[side, 4] * near[c] for c in range(4)])
        for c in range(4):
            v0[c, fine_plane(own), :] += change[c]
        applied = []
        for c in range(4):
            beside = h0[side, c, PAD - 1 : PAD - 1 + x0, :] + h0[side, c, PAD + 1 : PAD + 1 + x0, :]
            beside += p0[side, 5 + c] + s0[side, c]
            applied.append(stencil(near[c], beside, p0[side, 4], LANES))
        change = mixed4(T0, applied)
        for c in range(4):
            v0[c, fine_plane(halo), :] = 2.0 * near[c] - change[c]

    def residual_fine(i):
        total = [None] * 4
        for s in range(2):
            x = 2 * i + s
            applied = mixed4(B0, [fine_stencil(v0, a0[x + 1], c, x + 2) for c in range(4)])
            for c in range(4):
                rest = f0[c, x] - applied[c]
                total[c] = rest if s == 0 else total[c] + rest
        for c in range(4):
            r0[c, i] = total[c]

    steps(x1, residual_fine)

    for g in range(2):
        pieces = [
            r0[c, :, pl.ds(0, y1, stride=2), :] + r0[c, :, pl.ds(1, y1, stride=2), :]
            for c in (2 * g, 2 * g + 1)
        ]
        joined = jnp.concatenate([piece.reshape(x1 * y1, LANES) for piece in pieces], axis=-1)
        f1[g] = spread(joined, down[...]).reshape(x1, y1, LANES)
    fields = mixed2(S1, [f1[g] for g in range(2)])
    for g in range(2):
        g1[g, 3 : 3 + x1, PAD : PAD + y1, :] = fields[g]
    planes1 = [(0, 0), (0, 1), (0, 2), (1, 0), (1, 1), (1, 2), (2, 0), (2, 1)]
    cells1 = corner_cells(planes1, lambda c: 2 if c == 2 else 3)
    pack(g1, s1, planes1, 3, x1, y1)
    copies = exchange(g1, s1, p1, d1, c1, cells1, 3, x1, y1)

    def fill_beside(buffer, received):
        for side, row in ((0, PAD - y3), (1, PAD + y3)):
            inside = (my > 0) if side == 0 else (my < ny - 1)
            for x in range(x3):
                buffer[4 + x, row : row + y3, :] = jnp.where(
                    inside, received[side, x * y3 : (x + 1) * y3, :], 0.0
                )

    first_half = lane < 64
    block_steps = (2, -2, 1, -1)

    def send_block(buffer, packed, received):
        rows = slice(0, 2 * PAD)
        packed[...] = jnp.where(first_half, buffer[4, rows, :], buffer[5, rows, :])
        return [
            send(packed, received.at[n], (dx, 0)) for n, dx in enumerate(block_steps)
        ]

    def receive_block(buffer, received, copies):
        for copy in copies:
            copy.wait_recv()
        for n, dx in enumerate(block_steps):
            outside = (mx < dx) if dx > 0 else (mx >= nx + dx)
            block = jnp.where(outside, 0.0, received[n])
            turned = pltpu.roll(block, 64, 1)
            x = 4 - 2 * dx
            buffer[x, 0 : 2 * PAD, :] = jnp.where(first_half, block, turned)
            buffer[x + 1, 0 : 2 * PAD, :] = jnp.where(first_half, turned, block)

    for copy in coarse_copies:
        copy.wait_recv()
    fill_beside(k3, u3)
    coarse_copies = send_block(k3, b_k3, l_k3)

    def settle_fine(x):
        change = mixed4(T0, [fine_stencil(v0, a0[x + 1], c, x + 2) for c in range(4)])
        for c in range(4):
            value = fine_rows(v0, c, x + 2, PAD, y0) + fine_rows(g0, c, x + 2, PAD, y0)
            f0[c, x] = value - change[c]

    steps(x0, settle_fine)
    unpack(copies, g1, p1, c1, cells1, planes1, 3, x1, y1)

    def relax_second(step):
        x = step + 1
        row, rows = PAD - 2, y1 + 4
        coefficient = g1[2, x, row : row + rows, :]
        change = mixed2(T1, [stencil_of(g1, coefficient, c, x, row, rows, 64) for c in range(2)])
        for c in range(2):
            v1[c, x, row : row + rows, :] = 2.0 * g1[c, x, row : row + rows, :] - change[c]

    steps(x1 + 4, relax_second)

    def residual_second(i):
        total = [None] * 2
        for s in range(2):
            x = 2 * i + s
            coefficient = g1[2, x + 3, PAD : PAD + y1, :]
            applied = mixed2(
                B1, [stencil_of(v1, coefficient, c, x + 3, PAD, y1, 64) for c in range(2)]
            )
            for c in range(2):
                rest = f1[c, x] - applied[c]
                total[c] = rest if s == 0 else total[c] + rest
        for c in range(2):
            r1[c, i] = total[c]

    steps(x2, residual_second)

    pieces = [
        r1[c, :, pl.ds(0, y2, stride=2), :] + r1[c, :, pl.ds(1, y2, stride=2), :] for c in range(2)
    ]
    joined = jnp.concatenate([piece.reshape(x2 * y2, LANES) for piece in pieces], axis=-1)
    f2[...] = spread(joined, down[...]).reshape(x2, y2, LANES)
    g2[0, 3 : 3 + x2, PAD : PAD + y2, :] = mixed1(S2, f2[...], 32)
    planes2 = [(0, 0), (0, 1), (1, 0), (1, 1), (2, 0)]
    cells2 = corner_cells(planes2, lambda c: 3 if c == 1 else 4)
    pack(g2, s2, planes2, 3, x2, y2)
    copies = exchange(g2, s2, p2, d2, c2, cells2, 3, x2, y2)
    receive_block(k3, l_k3, coarse_copies)

    def settle_second(step):
        x = step + 2
        row, rows = PAD - 1, y1 + 2
        coefficient = g1[2, x, row : row + rows, :]
        change = mixed2(T1, [stencil_of(v1, coefficient, c, x, row, rows, 64) for c in range(2)])
        for c in range(2):
            value = v1[c, x, row : row + rows, :] + g1[c, x, row : row + rows, :] - change[c]
            x1_part[c, step, row : row + rows, :] = value

    steps(x1 + 2, settle_second)
    unpack(copies, g2, p2, c2, cells2, planes2, 3, x2, y2)

    def block_stencil(load, coefficient, x, xs, row, rows, segment):
        center = load(x, xs, row, rows)
        beside = load(x - 1, xs, row, rows) + load(x + 1, xs, row, rows)
        beside += load(x, xs, row - 1, rows) + load(x, xs, row + 1, rows)
        return center, stencil(center, beside, coefficient, segment)

    def from_g2(x, xs, row, rows):
        return g2[0, x : x + xs, row : row + rows, :]

    def from_v2(x, xs, row, rows):
        return v2[x : x + xs, row : row + rows, :]

    row, rows = PAD - 2, y2 + 4
    center, applied = block_stencil(
        from_g2, g2[1, 1 : x2 + 5, row : row + rows, :], 1, x2 + 4, row, rows, 32
    )
    v2[1 : x2 + 5, row : row + rows, :] = 2.0 * center - mixed1(T2, applied, 32)
    _, applied = block_stencil(
        from_v2, g2[1, 3 : 3 + x2, PAD : PAD + y2, :], 3, x2, PAD, y2, 32
    )
    rest = f2[...] - mixed1(B2, applied, 32)
    pairs = jnp.concatenate([rest[2 * i] + rest[2 * i + 1] for i in range(x3)], axis=0)
    r3[...] = spread(pairs, last_down[...]).reshape(x3, y2, LANES)

    forcing = r3[:, pl.ds(0, y3, stride=2), :] + r3[:, pl.ds(1, y3, stride=2), :]
    smoothed = mixed1(S3, forcing, 16)
    g3[4 : 4 + x3, PAD : PAD + y3, :] = smoothed
    for x in range(x3):
        s3[x * y3 : (x + 1) * y3, :] = smoothed[x]
        line[x : x + 1, :] = jnp.sum(smoothed[x], axis=0, keepdims=True)
    copies = [send(line, lines.at[k - 1], (0, k)) for k in range(1, ny)]
    copies += [send(s3, p3.at[0], (0, 1)), send(s3, p3.at[1], (0, -1))]
    row, rows = PAD - 1, y2 + 2
    center, applied = block_stencil(
        from_v2, g2[1, 2 : x2 + 4, row : row + rows, :], 2, x2 + 2, row, rows, 32
    )
    x2_part[:, row : row + rows, :] = (
        center + g2[0, 2 : x2 + 4, row : row + rows, :] - mixed1(T2, applied, 32)
    )
    for copy in copies:
        copy.wait_recv()
    total = line[...]
    for k in range(1, ny):
        total += lines[k - 1]
    total *= 4.0 / math.sqrt(ny * y3)
    for x in range(x3):
        g3[4 + x, 0:1, :] = total[x : x + 1, :]
    fill_beside(g3, p3)
    receive_block(g3, l_g3, send_block(g3, b_g3, l_g3))

    low, high = PAD - y3, PAD + 2 * y3
    cell = lax.broadcasted_iota(jnp.int32, (1, 3 * y3, LANES), 1) + (my - 1) * y3
    inside = (cell >= 0) & (cell < ny * y3)
    w3[:, low:high, :] = g3[:, low:high, :] + jnp.where(inside, g3[:, 0:1, :], 0.0)

    def from_w3(x, xs, row, rows):
        return w3[x : x + xs, row : row + rows, :]

    for sweep in range(1, 4):
        x, xs = sweep, 8 + x3 - 2 * sweep
        row, rows = low + sweep, high - low - 2 * sweep
        center, applied = block_stencil(
            from_w3, k3[x : x + xs, row : row + rows, :], x, xs, row, rows, 16
        )
        value = center + g3[x : x + xs, row : row + rows, :] - mixed1(T3, applied, 16)
        if sweep < 3:
            w3[x : x + xs, row : row + rows, :] = value
        else:
            b3[:, row : row + rows, :] = value

    below = b3[...]
    mixed = mixed1(T2_below, below, 16)
    flat = ((x3 + 2) * 2 * PAD, LANES)
    e2[...] = spread_stacked((below - mixed).reshape(flat), last_up[...]).reshape(e2.shape)
    m2[...] = spread_stacked(mixed.reshape(flat), last_rise[...]).reshape(m2.shape)
    q2[...] = spread_stacked(mixed.reshape(flat), last_up[...]).reshape(q2.shape)

    def raised(m, q, c, i, s, t, row, rows):
        other_y = q[c, i, row + 2 * t - 1 : row + 2 * t - 1 + rows, :]
        other_x = q[c, i + 2 * s - 1, row : row + rows, :]
        return m[c, i, row : row + rows, :] - other_y - other_x

    for x in range(-1, x2 + 1):
        i, s = x // 2 + 1, x % 2
        for t in range(2):
            row, rows = PAD - t, y3 + 1
            cells = pl.ds(PAD - t, rows, stride=2)
            value = raised(m2, q2, 0, i, s, t, row, rows)
            w2[x + 1, cells, :] = (
                x2_part[x + 1, cells, :]
                + e2[0, i, row : row + rows, :]
                - g2[1, x + 3, cells, :] * value
            )

    below = w2[...]
    mixed = mixed1(T1_below, below, 32)
    flat = ((x2 + 2) * (y2 + 2 * PAD), LANES)
    shape = (x2 + 2, y2 + 2 * PAD, LANES)
    for field, matrix, target in (
        (below - mixed, up, e1),
        (mixed, rise_second, m1),
        (mixed, up, q1),
    ):
        children = spread_stacked(field.reshape(flat), matrix[...])
        for c in range(2):
            target[c] = children[:, c * LANES : (c + 1) * LANES].reshape(shape)
    for x in range(-1, x1 + 1):
        i, s = x // 2 + 1, x % 2
        for t in range(2):
            row, rows = PAD - t, y2 + 1
            cells = pl.ds(PAD - t, rows, stride=2)
            coefficient = g1[2, x + 3, cells, :]
            for c in range(2):
                value = raised(m1, q1, c, i, s, t, row, rows)
                w1[c, x + 1, cells, :] = (
                    x1_part[c, x + 1, cells, :]
                    + e1[c, i, row : row + rows, :]
                    - coefficient * value
                )

    below = [w1[c] for c in range(2)]
    mixed = mixed2(T0_below, below)
    own = slice(1, x1 + 1), slice(PAD, PAD + y1)
    for g in range(2):
        inner = (x1 * y1, LANES)
        for field, matrix, target in (
            ((below[g] - mixed[g])[own].reshape(inner), up, e0),
            (mixed[g][own].reshape(inner), rise_fine, m0),
        ):
            children = spread_stacked(field, matrix[...])
            for c in range(2):
                part = children[:, c * LANES : (c + 1) * LANES]
                target[2 * g + c, 1 : x1 + 1, PAD : PAD + y1, :] = part.reshape(x1, y1, LANES)
        children = spread_stacked(
            mixed[g].reshape((x1 + 2) * (y1 + 2 * PAD), LANES), up[...]
        )
        for c in range(2):
            part = children[:, c * LANES : (c + 1) * LANES]
            q0[2 * g + c] = part.reshape(x1 + 2, y1 + 2 * PAD, LANES)

    def finish_fine(step):
        i = step + 1
        for t in range(2):
            cells = pl.ds(t, y1, stride=2)
            coefficient = [a0[2 * step + s + 1, pl.ds(t, y1, stride=2), :] for s in range(2)]
            for c in range(4):
                for s in range(2):
                    value = raised(m0, q0, c, i, s, t, PAD, y1)
                    x = 2 * step + s
                    out[c, x, cells, :] = (
                        f0[c, x, cells, :]
                        + e0[c, i, PAD : PAD + y1, :]
                        - coefficient[s] * value
                    )

    steps(x1, finish_fine)
    for copy in started:
        copy.wait_send()


def per_device(nx, ny, source, fine, second, third, coarse, mixers, smoothers):
    x0, y0 = source.shape[1:3]
    x1, y1 = second.shape[:2]
    x2, y2 = third.shape[:2]
    x3, y3 = coarse.shape[:2]

    def padded(groups, xs, ys, h):
        return pltpu.VMEM((groups, xs + 2 * h, ys + 2 * PAD, LANES), F32)

    def vmem(*shape):
        return pltpu.VMEM(shape, F32)

    def faces(planes, near, xs):
        rows = max(xs, 8)
        return [
            vmem(2, planes, rows, LANES),
            vmem(2, planes, rows, LANES),
            vmem(4, near, LANES),
            vmem(4, near, LANES),
        ]

    def three(groups, xs, ys):
        return [vmem(groups, xs + 2, ys + 2 * PAD, LANES)] * 3

    double = pltpu.VMEM((2 * LANES, 2 * LANES), BF16)
    tall = pltpu.VMEM((2 * LANES, LANES), BF16)
    scratch = (
        [vmem(2, 4, 2, y0, LANES), vmem(4, x0, y0, LANES), vmem(x0 + 2, y0, LANES)]
        + [vmem(4, (x0 + 4) * (y0 + 2 * PAD), LANES)] * 2
        + [vmem(2, 4, x0 + 2 * PAD, LANES)]
        + [vmem(4, x1, y0, LANES)]
        + three(4, x1, y1)
        + faces(9, 8, x0)
        + [vmem(*second.shape), vmem(2, x1, y1, LANES), padded(3, x1, y1, 3), padded(2, x1, y1, 3)]
        + [vmem(2, x2, y1, LANES), vmem(2, x1 + 2, y1 + 2 * PAD, LANES)]
        + three(2, x2, y2)
        + [vmem(2, x1 + 2, y1 + 2 * PAD, LANES)]
        + faces(8, 8, x1)
        + [vmem(*third.shape), vmem(x2, y2, LANES), padded(2, x2, y2, 3)]
        + [vmem(x2 + 6, y2 + 2 * PAD, LANES), vmem(x3, y2, LANES)]
        + [vmem(x2 + 2, y2 + 2 * PAD, LANES)]
        + [vmem(1, x3 + 2, 2 * PAD, LANES)] * 3
        + [vmem(x2 + 2, y2 + 2 * PAD, LANES)]
        + faces(5, 16, x2)
        + [vmem(*coarse.shape), vmem(x3, y2, LANES)]
        + [vmem(x3 + 8, 24, LANES)] * 3
        + [vmem(x3 + 2, 2 * PAD, LANES)]
        + [vmem(x3 * y3, LANES), vmem(2, x3 * y3, LANES)] * 2
        + [vmem(2 * PAD, LANES), vmem(4, 2 * PAD, LANES)] * 2
        + [vmem(x3, LANES), vmem(ny - 1, x3, LANES)]
        + [vmem(64, LANES)]
        + [tall, double, double, double, pltpu.VMEM((LANES, LANES), BF16), tall, tall]
    )
    copies = 8 * 3 + 4 + 2 * 2 + (ny - 1) + 4 * 2
    scratch += [
        pltpu.SMEM(mixers.shape, F32),
        pltpu.SMEM(smoothers.shape, F32),
        pltpu.SemaphoreType.DMA((copies,)),
        pltpu.SemaphoreType.DMA((copies,)),
        pltpu.SemaphoreType.DMA((10,)),
    ]
    anywhere = pl.BlockSpec(memory_space=pl.ANY)
    return pl.pallas_call(
        functools.partial(kernel, nx, ny),
        out_shape=pltpu.VMEM(source.shape, F32),
        in_specs=[anywhere] * 7,
        out_specs=pl.BlockSpec(memory_space=pltpu.VMEM),
        scratch_shapes=scratch,
        compiler_params=pltpu.CompilerParams(
            collective_id=0, has_side_effects=True, vmem_limit_bytes=56 * 1024 * 1024
        ),
    )(source, fine, second, third, coarse, mixers, smoothers)


def solution(mesh):
    field, cells = P(None, "gx", "gy", None), P("gx", "gy", None)
    return jax.shard_map(
        functools.partial(per_device, mesh.shape["gx"], mesh.shape["gy"]),
        mesh=mesh,
        in_specs=(field, cells, cells, cells, cells, P(), P()),
        out_specs=field,
        check_vma=False,
    )
```

```python
import functools
import math

import jax
import jax.numpy as jnp
from jax import lax
from jax.experimental import pallas as pl
from jax.experimental.pallas import tpu as pltpu
from jax.sharding import PartitionSpec as P

MESH = pl.DeviceIdType.MESH
F32 = jnp.float32
BF16 = jnp.bfloat16
LANES = 128
PAD = 8


def spread(field, matrix):
    high = field.astype(BF16)
    low = (field - high.astype(F32)).astype(BF16)
    return jnp.dot(high, matrix, preferred_element_type=F32) + jnp.dot(
        low, matrix, preferred_element_type=F32
    )


def spread_stacked(field, matrix):
    high = field.astype(BF16)
    low = (field - high.astype(F32)).astype(BF16)
    return jnp.dot(jnp.concatenate([high, low], axis=-1), matrix, preferred_element_type=F32)


def lane_index(shape):
    return lax.broadcasted_iota(jnp.int32, shape, len(shape) - 1)


def beside_z(field, segment):
    lane = lane_index((1, LANES)) % segment
    axis = field.ndim - 1
    before = jnp.where(lane == 0, 0.0, pltpu.roll(field, 1, axis))
    after = jnp.where(lane == segment - 1, 0.0, pltpu.roll(field, LANES - 1, axis))
    return before + after


def stencil(center, beside, coefficient, segment):
    total = beside + beside_z(center, segment)
    return coefficient * (6.0 * center - total) + center


def kernel(
    nx, ny,
    source, fine, second, third, coarse, mixers_in, smoothers_in, out,
    fx, o0, f0, a0, g0, v0, h0, r0, e0, m0, q0, s0, p0, d0, c0,
    a1, f1, g1, v1, r1, x1_part, e1, m1, q1, w1, s1, p1, d1, c1,
    a2, f2, g2, v2, r2, x2_part, e2, m2, q2, w2, s2, p2, d2, c2,
    a3, r3, g3, k3, w3, b3, s3, p3, t3, u3, b_k3, l_k3, b_g3, l_g3, line, lines,
    table, down, up, rise_fine, rise_second, last_down, last_up, last_rise,
    mixers, smoothers, send_sem, recv_sem, local_sem,
):
    mx, my = lax.axis_index("gx"), lax.axis_index("gy")

    def device(dx, dy):
        return (lax.rem(mx + (dx + nx), nx), lax.rem(my + (dy + ny), ny))

    barrier = pltpu.get_barrier_semaphore()
    peers = [(0, k) for k in range(1, ny)]
    peers += [(dx, dy) for dx in (-1, 1) for dy in (-1, 0, 1)] + [(-2, 0), (2, 0)]
    x0, y0 = f0.shape[1:3]
    x1, y1 = f1.shape[1:3]
    x2, y2 = f2.shape[:2]
    x3, y3 = a3.shape[:2]
    part_rows = x0 // 4
    parts = [(n * part_rows, part_rows) for n in range(4)]
    load_fine = pltpu.make_async_copy(fine, a0.at[pl.ds(1, x0)], local_sem.at[0])
    load_parts = [
        pltpu.make_async_copy(
            source.at[:, pl.ds(x, xs)], f0.at[:, pl.ds(x, xs)], local_sem.at[4 + n]
        )
        for n, (x, xs) in enumerate(parts)
    ]
    load_coarser = [
        pltpu.make_async_copy(second, a1, local_sem.at[1]),
        pltpu.make_async_copy(third, a2, local_sem.at[2]),
        pltpu.make_async_copy(coarse, a3, local_sem.at[3]),
    ]
    load_smoothers = pltpu.make_async_copy(smoothers_in, smoothers, local_sem.at[8])
    load_mixers = pltpu.make_async_copy(mixers_in, mixers, local_sem.at[9])
    for load in [load_smoothers] + load_parts + [load_fine, load_mixers] + load_coarser:
        load.start()
    for dx, dy in peers:
        pl.semaphore_signal(barrier, inc=1, device_id=device(dx, dy), device_id_type=MESH)

    def smooth_matrix(level):
        return [
            [smoothers[level, i, j] + (0.25 if i == j else 0.0) for j in range(4)]
            for i in range(4)
        ]

    def mix_matrix(level):
        return [
            [mixers[level, i, j] + (1.0 if i == j else 0.0) for j in range(4)] for i in range(4)
        ]

    def product(left, right):
        return [
            [sum(left[i][k] * right[k][j] for k in range(4)) for j in range(4)] for i in range(4)
        ]

    lane = lane_index((1, LANES))
    rows_used = [0]

    def keep(vector):
        row = rows_used[0]
        rows_used[0] += 1
        table[row : row + 1, :] = vector
        return row

    def pair_rows(matrix):
        return [
            [
                [
                    keep(
                        jnp.where(
                            lane < 64,
                            matrix[2 * g][2 * h + s],
                            matrix[2 * g + 1][2 * h + 1 - s],
                        )
                    )
                    for s in range(2)
                ]
                for h in range(2)
            ]
            for g in range(2)
        ]

    def quad_rows(matrix, segment):
        channel = (lane // segment) % 4
        rows = []
        for k in range(4):
            vector = jnp.zeros((1, LANES), F32)
            for i in range(4):
                vector = jnp.where(channel == i, matrix[i][(i - k) % 4], vector)
            rows.append(keep(vector))
        return rows


    def mixed4(matrix, fields):
        return [
            matrix[i][0] * fields[0]
            + matrix[i][1] * fields[1]
            + (matrix[i][2] * fields[2] + matrix[i][3] * fields[3])
            for i in range(4)
        ]

    def vector_of(row):
        return table[row : row + 1, :]

    def mixed2(rows, fields):
        turned = [pltpu.roll(field, 64, field.ndim - 1) for field in fields]
        return [
            vector_of(rows[g][0][0]) * fields[0]
            + vector_of(rows[g][0][1]) * turned[0]
            + (vector_of(rows[g][1][0]) * fields[1] + vector_of(rows[g][1][1]) * turned[1])
            for g in range(2)
        ]

    def mixed1(rows, field, segment):
        total = vector_of(rows[0]) * field
        for k in range(1, 4):
            total += vector_of(rows[k]) * pltpu.roll(field, k * segment, field.ndim - 1)
        return total

    def row_index(shape):
        return lax.broadcasted_iota(jnp.int32, shape, 0)

    def children_matrix(columns, segment):
        shape = (2 * LANES, columns)
        row, column = row_index(shape) % LANES, lane_index(shape)
        if segment is None:
            return jnp.where(row == column // 2, 1.0, 0.0).astype(BF16)
        odd = column % 2
        other = column // 2 + 2 * odd - 1
        place = column % segment
        valid = (place != 0) & (place != segment - 1)
        own = jnp.where(row == column // 2, 3.0, 0.0)
        return (own - jnp.where((row == other) & valid, 1.0, 0.0)).astype(BF16)

    started = []

    def send(src, dst, place):
        number = len(started)
        copy = pltpu.make_async_remote_copy(
            src_ref=src, dst_ref=dst, send_sem=send_sem.at[number], recv_sem=recv_sem.at[number],
            device_id=device(*place), device_id_type=MESH,
        )
        copy.start()
        started.append(copy)
        return copy

    def pack(g, s, planes, h, xs, ys):
        for p, (k, c) in enumerate(planes):
            s[0, p, 0:xs, :] = g[c, h : h + xs, PAD + k, :]
            s[1, p, 0:xs, :] = g[c, h : h + xs, PAD + ys - 1 - k, :]

    def corner_cells(planes, reach_of):
        return [
            (n, i) for n, (k, c) in enumerate(planes) for i in range(reach_of(c) - 1 - k)
        ]

    def send_corners(s, packed, corner, cells, xs):
        copies = []
        for side, dy in ((1, 1), (0, -1)):
            for dx in (1, -1):
                slot = (0 if dx > 0 else 1) * 2 + (0 if dy > 0 else 1)
                for r, (n, i) in enumerate(cells):
                    x = xs - 1 - i if dx > 0 else i
                    packed[slot, r : r + 1, :] = s[side, n, x : x + 1, :]
                copies.append(send(packed.at[slot], corner.at[slot], (dx, dy)))
        return copies

    def exchange(g, s, p, packed, corner, cells, h, xs, ys):
        own = pl.ds(PAD, ys)
        copies = [
            send(g.at[:, pl.ds(xs, h), own], g.at[:, pl.ds(0, h), own], (1, 0)),
            send(g.at[:, pl.ds(h, h), own], g.at[:, pl.ds(xs + h, h), own], (-1, 0)),
        ]
        copies += send_corners(s, packed, corner, cells, xs)
        copies.append(send(s.at[1], p.at[0], (0, 1)))
        copies.append(send(s.at[0], p.at[1], (0, -1)))
        return copies

    def unpack(copies, g, p, corner, cells, planes, h, xs, ys):
        for copy in copies:
            copy.wait_recv()
        groups = g.shape[0]
        for n, (k, c) in enumerate(planes):
            g[c, h : h + xs, PAD - 1 - k, :] = p[0, n, 0:xs, :]
            g[c, h : h + xs, PAD + ys + k, :] = p[1, n, 0:xs, :]
        for r, (n, i) in enumerate(cells):
            k, c = planes[n]
            for from_dy in range(2):
                row = PAD - 1 - k if from_dy == 0 else PAD + ys + k
                g[c, h - 1 - i, row : row + 1, :] = corner[from_dy, r : r + 1, :]
                g[c, h + xs + i, row : row + 1, :] = corner[2 + from_dy, r : r + 1, :]

        @pl.when(mx == 0)
        def _():
            g[:, 0:h] = jnp.zeros((groups, h) + g.shape[2:], F32)

        @pl.when(mx == nx - 1)
        def _():
            g[:, h + xs :] = jnp.zeros((groups, h) + g.shape[2:], F32)

        @pl.when(my == 0)
        def _():
            g[:, :, 0:PAD] = jnp.zeros(g.shape[:2] + (PAD, LANES), F32)

        @pl.when(my == ny - 1)
        def _():
            g[:, :, PAD + ys :] = jnp.zeros(g.shape[:2] + (PAD, LANES), F32)

    def steps(count, body):
        def step(i, carry):
            body(i)
            return carry

        lax.fori_loop(0, count, step, 0)

    def stencil_of(field, coefficient, c, x, row, rows, segment):
        center = field[c, x, row : row + rows, :]
        beside = field[c, x - 1, row : row + rows, :] + field[c, x + 1, row : row + rows, :]
        beside += field[c, x, row - 1 : row - 1 + rows, :]
        beside += field[c, x, row + 1 : row + 1 + rows, :]
        return stencil(center, beside, coefficient, segment)

    y_rows = y0 + 2 * PAD

    def fine_rows(buffer, c, x, row, rows):
        start = x * y_rows + row
        if row % 8 == 0:
            start = pl.multiple_of(start, 8)
        return buffer[c, pl.ds(start, rows), :]

    def fine_plane(row):
        return pl.ds(2 * y_rows + row, x0, stride=y_rows)

    def fine_stencil(buffer, coefficient, c, x, first=0, count=y0):
        row = PAD + first
        center = fine_rows(buffer, c, x, row, count)
        beside = fine_rows(buffer, c, x - 1, row, count) + fine_rows(buffer, c, x + 1, row, count)
        beside += fine_rows(buffer, c, x, row - 1, count) + fine_rows(buffer, c, x, row + 1, count)
        return stencil(center, beside, coefficient, LANES)

    def smooth_fine(x):
        fields = mixed4(S0, [f0[c, x] for c in range(4)])
        for c in range(4):
            start = pl.multiple_of((x + 2) * y_rows + PAD, 8)
            g0[c, pl.ds(start, y0), :] = fields[c]

    pl.semaphore_wait(barrier, len(peers))
    copies = [
        send(source.at[:, pl.ds(x0 - 2, 2)], fx.at[0], (1, 0)),
        send(source.at[:, pl.ds(0, 2)], fx.at[1], (-1, 0)),
        send(fine.at[pl.ds(x0 - 1, 1)], a0.at[pl.ds(0, 1)], (1, 0)),
        send(fine.at[pl.ds(0, 1)], a0.at[pl.ds(x0 + 1, 1)], (-1, 0)),
    ]
    for load in load_parts:
        load.wait()
    load_fine.wait()
    for c in range(4):
        for k in range(2):
            n = c if k == 0 else 5 + c
            s0[0, n] = f0[c, :, k, :]
            s0[1, n] = f0[c, :, y0 - 1 - k, :]
    s0[0, 4] = a0[1 : x0 + 1, 0, :]
    s0[1, 4] = a0[1 : x0 + 1, y0 - 1, :]
    copies += send_corners(s0, d0, c0, [(c, 0) for c in range(4)], x0)
    copies.append(send(s0.at[1], p0.at[0], (0, 1)))
    copies.append(send(s0.at[0], p0.at[1], (0, -1)))

    load_smoothers.wait()
    S0 = smooth_matrix(0)
    steps(x0, smooth_fine)
    for side in range(2):
        fields = mixed4(S0, [s0[side, c] for c in range(4)])
        for c in range(4):
            o0[side, c] = fields[c]

    for c in range(4):
        for row in (PAD - 1, PAD + y0):
            g0[c, fine_plane(row), :] = jnp.zeros((x0, LANES), F32)
    load_mixers.wait()
    B0 = mix_matrix(0)
    T0 = product(S0, B0)

    def relax_fine(x):
        coefficient = a0[x - 1]
        change = mixed4(T0, [fine_stencil(g0, coefficient, c, x) for c in range(4)])
        for c in range(4):
            value = 2.0 * fine_rows(g0, c, x, PAD, y0) - change[c]
            v0[c, pl.ds(pl.multiple_of(x * y_rows + PAD, 8), y0), :] = value

    steps(x0 - 2, lambda i: relax_fine(i + 3))

    def residual_fine(i, first, count):
        total = [None] * 4
        window = slice(first, first + count)
        for s in range(2):
            x = 2 * i + s
            coefficient = a0[x + 1, window, :]
            applied = mixed4(
                B0, [fine_stencil(v0, coefficient, c, x + 2, first, count) for c in range(4)]
            )
            for c in range(4):
                rest = f0[c, x, window, :] - applied[c]
                total[c] = rest if s == 0 else total[c] + rest
        for c in range(4):
            r0[c, i, window, :] = total[c]

    steps(x1 - 2, lambda i: residual_fine(i + 1, 8, y0 - 16))
    for load in load_coarser:
        load.wait()
    third_cells = jnp.concatenate([a3[...]] * 8, axis=-1)
    k3[4 : 4 + x3, PAD : PAD + y3, :] = third_cells
    for x in range(x3):
        t3[x * y3 : (x + 1) * y3, :] = third_cells[x]
    coarse_copies = [send(t3, u3.at[0], (0, 1)), send(t3, u3.at[1], (0, -1))]
    g1[2, 3 : 3 + x1, PAD : PAD + y1, :] = jnp.concatenate([a1[...]] * 2, axis=-1)
    g2[1, 3 : 3 + x2, PAD : PAD + y2, :] = jnp.concatenate([a2[...]] * 4, axis=-1)
    smooth1, mixer1 = smooth_matrix(1), mix_matrix(1)
    S1, B1, T1 = pair_rows(smooth1), pair_rows(mixer1), pair_rows(product(smooth1, mixer1))
    smooth2, mixer2 = smooth_matrix(2), mix_matrix(2)
    S2, B2 = quad_rows(smooth2, 32), quad_rows(mixer2, 32)
    T2 = quad_rows(product(smooth2, mixer2), 32)
    smooth3, mixer3 = smooth_matrix(3), mix_matrix(3)
    S3, T3 = quad_rows(smooth3, 16), quad_rows(product(smooth3, mixer3), 16)
    T0_below = pair_rows(T0)
    T1_below = quad_rows(product(smooth1, mixer1), 32)
    T2_below = quad_rows(product(smooth2, mixer2), 16)

    wide, narrow = (2 * LANES, LANES), (LANES, LANES)
    down[...] = jnp.where(row_index(wide) // 2 == lane_index(wide), 0.125, 0.0).astype(BF16)
    last_down[...] = jnp.where(
        row_index(narrow) // 2 == lane_index(narrow) % 64, 0.125, 0.0
    ).astype(BF16)
    up[...] = children_matrix(2 * LANES, None)
    rise_fine[...] = children_matrix(2 * LANES, LANES)
    rise_second[...] = children_matrix(2 * LANES, 64)
    last_up[...] = children_matrix(LANES, None)
    last_rise[...] = children_matrix(LANES, 32)

    for copy in copies:
        copy.wait_recv()

    def smooth_beside(i):
        fields = mixed4(S0, [fx[i // 2, c, i % 2] for c in range(4)])
        for c in range(4):
            start = pl.multiple_of((i + x0 * (i // 2)) * y_rows + PAD, 8)
            g0[c, pl.ds(start, y0), :] = fields[c]

    steps(4, smooth_beside)
    for side in range(2):
        for first in (0, 5):
            fields = mixed4(S0, [p0[side, first + c] for c in range(4)])
            for c in range(4):
                p0[side, first + c] = fields[c]
    for slot in range(4):
        fields = mixed4(S0, [c0[slot, c : c + 1, :] for c in range(4)])
        for c in range(4):
            c0[slot, c : c + 1, :] = fields[c]

    @pl.when(mx == 0)
    def _():
        g0[:, 0 : 2 * y_rows] = jnp.zeros((4, 2 * y_rows, LANES), F32)
        c0[0:2] = jnp.zeros((2,) + c0.shape[1:], F32)
        a0[0] = jnp.zeros((y0, LANES), F32)

    @pl.when(mx == nx - 1)
    def _():
        g0[:, (x0 + 2) * y_rows :] = jnp.zeros((4, 2 * y_rows, LANES), F32)
        c0[2:4] = jnp.zeros((2,) + c0.shape[1:], F32)
        a0[x0 + 1] = jnp.zeros((y0, LANES), F32)

    for side, edge in ((0, 0), (1, ny - 1)):

        @pl.when(my == edge)
        def _(side=side):
            p0[side] = jnp.zeros(p0.shape[1:], F32)
            c0[side] = jnp.zeros(c0.shape[1:], F32)
            c0[2 + side] = jnp.zeros(c0.shape[1:], F32)

    for c in range(4):
        for side, row in ((0, PAD - 1), (1, PAD + y0)):
            left, right = c0[side, c : c + 1, :], c0[2 + side, c : c + 1, :]
            g0[c, y_rows + row : y_rows + row + 1, :] = left
            g0[c, (x0 + 2) * y_rows + row : (x0 + 2) * y_rows + row + 1, :] = right
            h0[side, c, PAD - 1 : PAD, :] = left
            h0[side, c, PAD + x0 : PAD + x0 + 1, :] = right
            h0[side, c, PAD : PAD + x0, :] = p0[side, c]
    steps(4, lambda i: relax_fine(1 + i + (x0 - 2) * (i // 2)))
    for side, own, halo in ((0, PAD, PAD - 1), (1, PAD + y0 - 1, PAD + y0)):
        near = [p0[side, c] for c in range(4)]
        change = mixed4(T0, [s0[side, 4] * near[c] for c in range(4)])
        for c in range(4):
            v0[c, fine_plane(own), :] += change[c]
        applied = []
        for c in range(4):
            beside = h0[side, c, PAD - 1 : PAD - 1 + x0, :] + h0[side, c, PAD + 1 : PAD + 1 + x0, :]
            beside += p0[side, 5 + c] + o0[side, c]
            applied.append(stencil(near[c], beside, p0[side, 4], LANES))
        change = mixed4(T0, applied)
        for c in range(4):
            v0[c, fine_plane(halo), :] = 2.0 * near[c] - change[c]

    steps(x1 - 2, lambda i: residual_fine(i + 1, 0, 8))
    steps(x1 - 2, lambda i: residual_fine(i + 1, y0 - 8, 8))
    steps(2, lambda i: residual_fine(i * (x1 - 1), 0, y0))

    for g in range(2):
        pieces = [
            r0[c, :, pl.ds(0, y1, stride=2), :] + r0[c, :, pl.ds(1, y1, stride=2), :]
            for c in (2 * g, 2 * g + 1)
        ]
        joined = jnp.concatenate([piece.reshape(x1 * y1, LANES) for piece in pieces], axis=-1)
        f1[g] = spread(joined, down[...]).reshape(x1, y1, LANES)
    fields = mixed2(S1, [f1[g] for g in range(2)])
    for g in range(2):
        g1[g, 3 : 3 + x1, PAD : PAD + y1, :] = fields[g]
    planes1 = [(0, 0), (0, 1), (0, 2), (1, 0), (1, 1), (1, 2), (2, 0), (2, 1)]
    cells1 = corner_cells(planes1, lambda c: 2 if c == 2 else 3)
    pack(g1, s1, planes1, 3, x1, y1)
    copies = exchange(g1, s1, p1, d1, c1, cells1, 3, x1, y1)

    def fill_beside(buffer, received):
        for side, row in ((0, PAD - y3), (1, PAD + y3)):
            inside = (my > 0) if side == 0 else (my < ny - 1)
            for x in range(x3):
                buffer[4 + x, row : row + y3, :] = jnp.where(
                    inside, received[side, x * y3 : (x + 1) * y3, :], 0.0
                )

    first_half = lane < 64
    block_steps = (2, -2, 1, -1)

    def send_block(buffer, packed, received):
        rows = slice(0, 2 * PAD)
        packed[...] = jnp.where(first_half, buffer[4, rows, :], buffer[5, rows, :])
        return [
            send(packed, received.at[n], (dx, 0)) for n, dx in enumerate(block_steps)
        ]

    def receive_block(buffer, received, copies):
        for copy in copies:
            copy.wait_recv()
        for n, dx in enumerate(block_steps):
            outside = (mx < dx) if dx > 0 else (mx >= nx + dx)
            block = jnp.where(outside, 0.0, received[n])
            turned = pltpu.roll(block, 64, 1)
            x = 4 - 2 * dx
            buffer[x, 0 : 2 * PAD, :] = jnp.where(first_half, block, turned)
            buffer[x + 1, 0 : 2 * PAD, :] = jnp.where(first_half, turned, block)

    for copy in coarse_copies:
        copy.wait_recv()
    fill_beside(k3, u3)
    coarse_copies = send_block(k3, b_k3, l_k3)

    def settle_fine(x):
        change = mixed4(T0, [fine_stencil(v0, a0[x + 1], c, x + 2) for c in range(4)])
        for c in range(4):
            value = fine_rows(v0, c, x + 2, PAD, y0) + fine_rows(g0, c, x + 2, PAD, y0)
            f0[c, x] = value - change[c]

    steps(x0, settle_fine)
    unpack(copies, g1, p1, c1, cells1, planes1, 3, x1, y1)

    def relax_second(step):
        x = step + 1
        row, rows = PAD - 2, y1 + 4
        coefficient = g1[2, x, row : row + rows, :]
        change = mixed2(T1, [stencil_of(g1, coefficient, c, x, row, rows, 64) for c in range(2)])
        for c in range(2):
            v1[c, x, row : row + rows, :] = 2.0 * g1[c, x, row : row + rows, :] - change[c]

    steps(x1 + 4, relax_second)

    def residual_second(i):
        total = [None] * 2
        for s in range(2):
            x = 2 * i + s
            coefficient = g1[2, x + 3, PAD : PAD + y1, :]
            applied = mixed2(
                B1, [stencil_of(v1, coefficient, c, x + 3, PAD, y1, 64) for c in range(2)]
            )
            for c in range(2):
                rest = f1[c, x] - applied[c]
                total[c] = rest if s == 0 else total[c] + rest
        for c in range(2):
            r1[c, i] = total[c]

    steps(x2, residual_second)

    pieces = [
        r1[c, :, pl.ds(0, y2, stride=2), :] + r1[c, :, pl.ds(1, y2, stride=2), :] for c in range(2)
    ]
    joined = jnp.concatenate([piece.reshape(x2 * y2, LANES) for piece in pieces], axis=-1)
    f2[...] = spread(joined, down[...]).reshape(x2, y2, LANES)
    g2[0, 3 : 3 + x2, PAD : PAD + y2, :] = mixed1(S2, f2[...], 32)
    planes2 = [(0, 0), (0, 1), (1, 0), (1, 1), (2, 0)]
    cells2 = corner_cells(planes2, lambda c: 3 if c == 1 else 4)
    pack(g2, s2, planes2, 3, x2, y2)
    copies = exchange(g2, s2, p2, d2, c2, cells2, 3, x2, y2)
    receive_block(k3, l_k3, coarse_copies)

    def settle_second(step):
        x = step + 2
        row, rows = PAD - 1, y1 + 2
        coefficient = g1[2, x, row : row + rows, :]
        change = mixed2(T1, [stencil_of(v1, coefficient, c, x, row, rows, 64) for c in range(2)])
        for c in range(2):
            value = v1[c, x, row : row + rows, :] + g1[c, x, row : row + rows, :] - change[c]
            x1_part[c, step, row : row + rows, :] = value

    steps(x1 + 2, settle_second)
    unpack(copies, g2, p2, c2, cells2, planes2, 3, x2, y2)

    def block_stencil(load, coefficient, x, xs, row, rows, segment):
        center = load(x, xs, row, rows)
        beside = load(x - 1, xs, row, rows) + load(x + 1, xs, row, rows)
        beside += load(x, xs, row - 1, rows) + load(x, xs, row + 1, rows)
        return center, stencil(center, beside, coefficient, segment)

    def from_g2(x, xs, row, rows):
        return g2[0, x : x + xs, row : row + rows, :]

    def from_v2(x, xs, row, rows):
        return v2[x : x + xs, row : row + rows, :]

    row, rows = PAD - 2, y2 + 4
    center, applied = block_stencil(
        from_g2, g2[1, 1 : x2 + 5, row : row + rows, :], 1, x2 + 4, row, rows, 32
    )
    v2[1 : x2 + 5, row : row + rows, :] = 2.0 * center - mixed1(T2, applied, 32)
    _, applied = block_stencil(
        from_v2, g2[1, 3 : 3 + x2, PAD : PAD + y2, :], 3, x2, PAD, y2, 32
    )
    rest = f2[...] - mixed1(B2, applied, 32)
    pairs = jnp.concatenate([rest[2 * i] + rest[2 * i + 1] for i in range(x3)], axis=0)
    r3[...] = spread(pairs, last_down[...]).reshape(x3, y2, LANES)

    forcing = r3[:, pl.ds(0, y3, stride=2), :] + r3[:, pl.ds(1, y3, stride=2), :]
    smoothed = mixed1(S3, forcing, 16)
    g3[4 : 4 + x3, PAD : PAD + y3, :] = smoothed
    for x in range(x3):
        s3[x * y3 : (x + 1) * y3, :] = smoothed[x]
        line[x : x + 1, :] = jnp.sum(smoothed[x], axis=0, keepdims=True)
    copies = [send(line, lines.at[k - 1], (0, k)) for k in range(1, ny)]
    copies += [send(s3, p3.at[0], (0, 1)), send(s3, p3.at[1], (0, -1))]
    row, rows = PAD - 1, y2 + 2
    center, applied = block_stencil(
        from_v2, g2[1, 2 : x2 + 4, row : row + rows, :], 2, x2 + 2, row, rows, 32
    )
    x2_part[:, row : row + rows, :] = (
        center + g2[0, 2 : x2 + 4, row : row + rows, :] - mixed1(T2, applied, 32)
    )
    for copy in copies:
        copy.wait_recv()
    total = line[...]
    for k in range(1, ny):
        total += lines[k - 1]
    total *= 4.0 / math.sqrt(ny * y3)
    for x in range(x3):
        g3[4 + x, 0:1, :] = total[x : x + 1, :]
    fill_beside(g3, p3)
    receive_block(g3, l_g3, send_block(g3, b_g3, l_g3))

    low, high = PAD - y3, PAD + 2 * y3
    cell = lax.broadcasted_iota(jnp.int32, (1, 3 * y3, LANES), 1) + (my - 1) * y3
    inside = (cell >= 0) & (cell < ny * y3)
    w3[:, low:high, :] = g3[:, low:high, :] + jnp.where(inside, g3[:, 0:1, :], 0.0)

    def from_w3(x, xs, row, rows):
        return w3[x : x + xs, row : row + rows, :]

    for sweep in range(1, 4):
        x, xs = sweep, 8 + x3 - 2 * sweep
        row, rows = low + sweep, high - low - 2 * sweep
        center, applied = block_stencil(
            from_w3, k3[x : x + xs, row : row + rows, :], x, xs, row, rows, 16
        )
        value = center + g3[x : x + xs, row : row + rows, :] - mixed1(T3, applied, 16)
        if sweep < 3:
            w3[x : x + xs, row : row + rows, :] = value
        else:
            b3[:, row : row + rows, :] = value

    below = b3[...]
    mixed = mixed1(T2_below, below, 16)
    flat = ((x3 + 2) * 2 * PAD, LANES)
    e2[...] = spread_stacked((below - mixed).reshape(flat), last_up[...]).reshape(e2.shape)
    m2[...] = spread_stacked(mixed.reshape(flat), last_rise[...]).reshape(m2.shape)
    q2[...] = spread_stacked(mixed.reshape(flat), last_up[...]).reshape(q2.shape)

    def raised(m, q, c, i, s, t, row, rows):
        other_y = q[c, i, row + 2 * t - 1 : row + 2 * t - 1 + rows, :]
        other_x = q[c, i + 2 * s - 1, row : row + rows, :]
        return m[c, i, row : row + rows, :] - other_y - other_x

    for x in range(-1, x2 + 1):
        i, s = x // 2 + 1, x % 2
        for t in range(2):
            row, rows = PAD - t, y3 + 1
            cells = pl.ds(PAD - t, rows, stride=2)
            value = raised(m2, q2, 0, i, s, t, row, rows)
            w2[x + 1, cells, :] = (
                x2_part[x + 1, cells, :]
                + e2[0, i, row : row + rows, :]
                - g2[1, x + 3, cells, :] * value
            )

    below = w2[...]
    mixed = mixed1(T1_below, below, 32)
    flat = ((x2 + 2) * (y2 + 2 * PAD), LANES)
    shape = (x2 + 2, y2 + 2 * PAD, LANES)
    for field, matrix, target in (
        (below - mixed, up, e1),
        (mixed, rise_second, m1),
        (mixed, up, q1),
    ):
        children = spread_stacked(field.reshape(flat), matrix[...])
        for c in range(2):
            target[c] = children[:, c * LANES : (c + 1) * LANES].reshape(shape)
    for x in range(-1, x1 + 1):
        i, s = x // 2 + 1, x % 2
        for t in range(2):
            row, rows = PAD - t, y2 + 1
            cells = pl.ds(PAD - t, rows, stride=2)
            coefficient = g1[2, x + 3, cells, :]
            for c in range(2):
                value = raised(m1, q1, c, i, s, t, row, rows)
                w1[c, x + 1, cells, :] = (
                    x1_part[c, x + 1, cells, :]
                    + e1[c, i, row : row + rows, :]
                    - coefficient * value
                )

    below = [w1[c] for c in range(2)]
    mixed = mixed2(T0_below, below)
    own = slice(1, x1 + 1), slice(PAD, PAD + y1)
    for g in range(2):
        inner = (x1 * y1, LANES)
        for field, matrix, target in (
            ((below[g] - mixed[g])[own].reshape(inner), up, e0),
            (mixed[g][own].reshape(inner), rise_fine, m0),
        ):
            children = spread_stacked(field, matrix[...])
            for c in range(2):
                part = children[:, c * LANES : (c + 1) * LANES]
                target[2 * g + c, 1 : x1 + 1, PAD : PAD + y1, :] = part.reshape(x1, y1, LANES)
        children = spread_stacked(
            mixed[g].reshape((x1 + 2) * (y1 + 2 * PAD), LANES), up[...]
        )
        for c in range(2):
            part = children[:, c * LANES : (c + 1) * LANES]
            q0[2 * g + c] = part.reshape(x1 + 2, y1 + 2 * PAD, LANES)

    def finish_fine(step):
        i = step + 1
        for t in range(2):
            cells = pl.ds(t, y1, stride=2)
            coefficient = [a0[2 * step + s + 1, pl.ds(t, y1, stride=2), :] for s in range(2)]
            for c in range(4):
                for s in range(2):
                    value = raised(m0, q0, c, i, s, t, PAD, y1)
                    x = 2 * step + s
                    out[c, x, cells, :] = (
                        f0[c, x, cells, :]
                        + e0[c, i, PAD : PAD + y1, :]
                        - coefficient[s] * value
                    )

    steps(x1, finish_fine)
    for copy in started:
        copy.wait_send()


def per_device(nx, ny, source, fine, second, third, coarse, mixers, smoothers):
    x0, y0 = source.shape[1:3]
    x1, y1 = second.shape[:2]
    x2, y2 = third.shape[:2]
    x3, y3 = coarse.shape[:2]

    def padded(groups, xs, ys, h):
        return pltpu.VMEM((groups, xs + 2 * h, ys + 2 * PAD, LANES), F32)

    def vmem(*shape):
        return pltpu.VMEM(shape, F32)

    def faces(planes, near, xs):
        rows = max(xs, 8)
        return [
            vmem(2, planes, rows, LANES),
            vmem(2, planes, rows, LANES),
            vmem(4, near, LANES),
            vmem(4, near, LANES),
        ]

    def three(groups, xs, ys):
        return [vmem(groups, xs + 2, ys + 2 * PAD, LANES)] * 3

    double = pltpu.VMEM((2 * LANES, 2 * LANES), BF16)
    tall = pltpu.VMEM((2 * LANES, LANES), BF16)
    scratch = (
        [vmem(2, 4, 2, y0, LANES), vmem(2, 4, x0, LANES), vmem(4, x0, y0, LANES), vmem(x0 + 2, y0, LANES)]
        + [vmem(4, (x0 + 4) * (y0 + 2 * PAD), LANES)] * 2
        + [vmem(2, 4, x0 + 2 * PAD, LANES)]
        + [vmem(4, x1, y0, LANES)]
        + three(4, x1, y1)
        + faces(9, 8, x0)
        + [vmem(*second.shape), vmem(2, x1, y1, LANES), padded(3, x1, y1, 3), padded(2, x1, y1, 3)]
        + [vmem(2, x2, y1, LANES), vmem(2, x1 + 2, y1 + 2 * PAD, LANES)]
        + three(2, x2, y2)
        + [vmem(2, x1 + 2, y1 + 2 * PAD, LANES)]
        + faces(8, 8, x1)
        + [vmem(*third.shape), vmem(x2, y2, LANES), padded(2, x2, y2, 3)]
        + [vmem(x2 + 6, y2 + 2 * PAD, LANES), vmem(x3, y2, LANES)]
        + [vmem(x2 + 2, y2 + 2 * PAD, LANES)]
        + [vmem(1, x3 + 2, 2 * PAD, LANES)] * 3
        + [vmem(x2 + 2, y2 + 2 * PAD, LANES)]
        + faces(5, 16, x2)
        + [vmem(*coarse.shape), vmem(x3, y2, LANES)]
        + [vmem(x3 + 8, 24, LANES)] * 3
        + [vmem(x3 + 2, 2 * PAD, LANES)]
        + [vmem(x3 * y3, LANES), vmem(2, x3 * y3, LANES)] * 2
        + [vmem(2 * PAD, LANES), vmem(4, 2 * PAD, LANES)] * 2
        + [vmem(x3, LANES), vmem(ny - 1, x3, LANES)]
        + [vmem(64, LANES)]
        + [tall, double, double, double, pltpu.VMEM((LANES, LANES), BF16), tall, tall]
    )
    copies = 8 * 3 + 4 + 2 * 2 + (ny - 1) + 4 * 2
    scratch += [
        pltpu.SMEM(mixers.shape, F32),
        pltpu.SMEM(smoothers.shape, F32),
        pltpu.SemaphoreType.DMA((copies,)),
        pltpu.SemaphoreType.DMA((copies,)),
        pltpu.SemaphoreType.DMA((10,)),
    ]
    anywhere = pl.BlockSpec(memory_space=pl.ANY)
    return pl.pallas_call(
        functools.partial(kernel, nx, ny),
        out_shape=pltpu.VMEM(source.shape, F32),
        in_specs=[anywhere] * 7,
        out_specs=pl.BlockSpec(memory_space=pltpu.VMEM),
        scratch_shapes=scratch,
        compiler_params=pltpu.CompilerParams(
            collective_id=0, has_side_effects=True, vmem_limit_bytes=56 * 1024 * 1024
        ),
    )(source, fine, second, third, coarse, mixers, smoothers)


def solution(mesh):
    field, cells = P(None, "gx", "gy", None), P("gx", "gy", None)
    return jax.shard_map(
        functools.partial(per_device, mesh.shape["gx"], mesh.shape["gy"]),
        mesh=mesh,
        in_specs=(field, cells, cells, cells, cells, P(), P()),
        out_specs=field,
        check_vma=False,
    )
```

```python
import functools
import math

import jax
import jax.numpy as jnp
from jax import lax
from jax.experimental import pallas as pl
from jax.experimental.pallas import tpu as pltpu
from jax.sharding import PartitionSpec as P

MESH = pl.DeviceIdType.MESH
F32 = jnp.float32
BF16 = jnp.bfloat16
LANES = 128
PAD = 8


def spread(field, matrix):
    high = field.astype(BF16)
    low = (field - high.astype(F32)).astype(BF16)
    return jnp.dot(high, matrix, preferred_element_type=F32) + jnp.dot(
        low, matrix, preferred_element_type=F32
    )


def spread_stacked(field, matrix):
    high = field.astype(BF16)
    low = (field - high.astype(F32)).astype(BF16)
    return jnp.dot(jnp.concatenate([high, low], axis=-1), matrix, preferred_element_type=F32)


def lane_index(shape):
    return lax.broadcasted_iota(jnp.int32, shape, len(shape) - 1)


def beside_z(field, segment):
    lane = lane_index((1, LANES)) % segment
    axis = field.ndim - 1
    before = jnp.where(lane == 0, 0.0, pltpu.roll(field, 1, axis))
    after = jnp.where(lane == segment - 1, 0.0, pltpu.roll(field, LANES - 1, axis))
    return before + after


def stencil(center, beside, coefficient, segment):
    total = beside + beside_z(center, segment)
    return coefficient * (6.0 * center - total) + center


def kernel(
    nx, ny,
    source, fine, second, third, coarse, mixers_in, smoothers_in, out,
    fx, o0, f0, a0, g0, v0, h0, r0, e0, m0, q0, s0, p0, d0, c0,
    a1, f1, g1, v1, r1, x1_part, e1, m1, q1, w1, s1, p1, d1, c1,
    a2, f2, g2, v2, r2, x2_part, e2, m2, q2, w2, s2, p2, d2, c2,
    a3, r3, g3, k3, w3, b3, s3, p3, t3, u3, b_k3, l_k3, b_g3, l_g3, line, lines,
    table, down, up, rise_fine, rise_second, last_down, last_up, last_rise,
    mixers, smoothers, send_sem, recv_sem, local_sem,
):
    mx, my = lax.axis_index("gx"), lax.axis_index("gy")

    def device(dx, dy):
        return (lax.rem(mx + (dx + nx), nx), lax.rem(my + (dy + ny), ny))

    barrier = pltpu.get_barrier_semaphore()
    peers = [(0, k) for k in range(1, ny)]
    peers += [(dx, dy) for dx in (-1, 1) for dy in (-1, 0, 1)] + [(-2, 0), (2, 0)]
    x0, y0 = f0.shape[1:3]
    x1, y1 = f1.shape[1:3]
    x2, y2 = f2.shape[:2]
    x3, y3 = a3.shape[:2]
    part_rows = x0 // 4
    parts = [(n * part_rows, part_rows) for n in range(4)]
    load_fine = pltpu.make_async_copy(fine, a0.at[pl.ds(1, x0)], local_sem.at[0])
    load_parts = [
        pltpu.make_async_copy(
            source.at[:, pl.ds(x, xs)], f0.at[:, pl.ds(x, xs)], local_sem.at[4 + n]
        )
        for n, (x, xs) in enumerate(parts)
    ]
    load_coarser = [
        pltpu.make_async_copy(second, a1, local_sem.at[1]),
        pltpu.make_async_copy(third, a2, local_sem.at[2]),
        pltpu.make_async_copy(coarse, a3, local_sem.at[3]),
    ]
    load_smoothers = pltpu.make_async_copy(smoothers_in, smoothers, local_sem.at[8])
    load_mixers = pltpu.make_async_copy(mixers_in, mixers, local_sem.at[9])
    for load in [load_smoothers] + load_parts + [load_fine, load_mixers] + load_coarser:
        load.start()
    for dx, dy in peers:
        pl.semaphore_signal(barrier, inc=1, device_id=device(dx, dy), device_id_type=MESH)

    def smooth_matrix(level):
        return [
            [smoothers[level, i, j] + (0.25 if i == j else 0.0) for j in range(4)]
            for i in range(4)
        ]

    def mix_matrix(level):
        return [
            [mixers[level, i, j] + (1.0 if i == j else 0.0) for j in range(4)] for i in range(4)
        ]

    def product(left, right):
        return [
            [sum(left[i][k] * right[k][j] for k in range(4)) for j in range(4)] for i in range(4)
        ]

    lane = lane_index((1, LANES))
    rows_used = [0]

    def keep(vector):
        row = rows_used[0]
        rows_used[0] += 1
        table[row : row + 1, :] = vector
        return row

    def pair_rows(matrix):
        return [
            [
                [
                    keep(
                        jnp.where(
                            lane < 64,
                            matrix[2 * g][2 * h + s],
                            matrix[2 * g + 1][2 * h + 1 - s],
                        )
                    )
                    for s in range(2)
                ]
                for h in range(2)
            ]
            for g in range(2)
        ]

    def quad_rows(matrix, segment):
        channel = (lane // segment) % 4
        rows = []
        for k in range(4):
            vector = jnp.zeros((1, LANES), F32)
            for i in range(4):
                vector = jnp.where(channel == i, matrix[i][(i - k) % 4], vector)
            rows.append(keep(vector))
        return rows


    def mixed4(matrix, fields):
        return [
            matrix[i][0] * fields[0]
            + matrix[i][1] * fields[1]
            + (matrix[i][2] * fields[2] + matrix[i][3] * fields[3])
            for i in range(4)
        ]

    def vector_of(row):
        return table[row : row + 1, :]

    def mixed2(rows, fields):
        turned = [pltpu.roll(field, 64, field.ndim - 1) for field in fields]
        return [
            vector_of(rows[g][0][0]) * fields[0]
            + vector_of(rows[g][0][1]) * turned[0]
            + (vector_of(rows[g][1][0]) * fields[1] + vector_of(rows[g][1][1]) * turned[1])
            for g in range(2)
        ]

    def mixed1(rows, field, segment):
        total = vector_of(rows[0]) * field
        for k in range(1, 4):
            total += vector_of(rows[k]) * pltpu.roll(field, k * segment, field.ndim - 1)
        return total

    def row_index(shape):
        return lax.broadcasted_iota(jnp.int32, shape, 0)

    def children_matrix(columns, segment):
        shape = (2 * LANES, columns)
        row, column = row_index(shape) % LANES, lane_index(shape)
        if segment is None:
            return jnp.where(row == column // 2, 1.0, 0.0).astype(BF16)
        odd = column % 2
        other = column // 2 + 2 * odd - 1
        place = column % segment
        valid = (place != 0) & (place != segment - 1)
        own = jnp.where(row == column // 2, 3.0, 0.0)
        return (own - jnp.where((row == other) & valid, 1.0, 0.0)).astype(BF16)

    started = []

    def send(src, dst, place):
        number = len(started)
        copy = pltpu.make_async_remote_copy(
            src_ref=src, dst_ref=dst, send_sem=send_sem.at[number], recv_sem=recv_sem.at[number],
            device_id=device(*place), device_id_type=MESH,
        )
        copy.start()
        started.append(copy)
        return copy

    def pack(g, s, planes, h, xs, ys):
        for p, (k, c) in enumerate(planes):
            s[0, p, 0:xs, :] = g[c, h : h + xs, PAD + k, :]
            s[1, p, 0:xs, :] = g[c, h : h + xs, PAD + ys - 1 - k, :]

    def corner_cells(planes, reach_of):
        return [
            (n, i) for n, (k, c) in enumerate(planes) for i in range(reach_of(c) - 1 - k)
        ]

    def send_corners(s, packed, corner, cells, xs):
        copies = []
        for side, dy in ((1, 1), (0, -1)):
            for dx in (1, -1):
                slot = (0 if dx > 0 else 1) * 2 + (0 if dy > 0 else 1)
                for r, (n, i) in enumerate(cells):
                    x = xs - 1 - i if dx > 0 else i
                    packed[slot, r : r + 1, :] = s[side, n, x : x + 1, :]
                copies.append(send(packed.at[slot], corner.at[slot], (dx, dy)))
        return copies

    def exchange(g, s, p, packed, corner, cells, h, xs, ys):
        own, held = pl.ds(PAD, ys), pl.ds(0, g.shape[0] - 1)
        copies = [
            send(g.at[held, pl.ds(xs, h), own], g.at[held, pl.ds(0, h), own], (1, 0)),
            send(g.at[held, pl.ds(h, h), own], g.at[held, pl.ds(xs + h, h), own], (-1, 0)),
        ]
        copies += send_corners(s, packed, corner, cells, xs)
        copies.append(send(s.at[1], p.at[0], (0, 1)))
        copies.append(send(s.at[0], p.at[1], (0, -1)))
        return copies

    def unpack(copies, g, p, corner, cells, planes, h, xs, ys):
        for copy in copies:
            copy.wait_recv()
        groups = g.shape[0]
        for n, (k, c) in enumerate(planes):
            g[c, h : h + xs, PAD - 1 - k, :] = p[0, n, 0:xs, :]
            g[c, h : h + xs, PAD + ys + k, :] = p[1, n, 0:xs, :]
        for r, (n, i) in enumerate(cells):
            k, c = planes[n]
            for from_dy in range(2):
                row = PAD - 1 - k if from_dy == 0 else PAD + ys + k
                g[c, h - 1 - i, row : row + 1, :] = corner[from_dy, r : r + 1, :]
                g[c, h + xs + i, row : row + 1, :] = corner[2 + from_dy, r : r + 1, :]

        @pl.when(mx == 0)
        def _():
            g[:, 0:h] = jnp.zeros((groups, h) + g.shape[2:], F32)

        @pl.when(mx == nx - 1)
        def _():
            g[:, h + xs :] = jnp.zeros((groups, h) + g.shape[2:], F32)

        @pl.when(my == 0)
        def _():
            g[:, :, 0:PAD] = jnp.zeros(g.shape[:2] + (PAD, LANES), F32)

        @pl.when(my == ny - 1)
        def _():
            g[:, :, PAD + ys :] = jnp.zeros(g.shape[:2] + (PAD, LANES), F32)

    def steps(count, body):
        def step(i, carry):
            body(i)
            return carry

        lax.fori_loop(0, count, step, 0)

    def stencil_of(field, coefficient, c, x, row, rows, segment):
        center = field[c, x, row : row + rows, :]
        beside = field[c, x - 1, row : row + rows, :] + field[c, x + 1, row : row + rows, :]
        beside += field[c, x, row - 1 : row - 1 + rows, :]
        beside += field[c, x, row + 1 : row + 1 + rows, :]
        return stencil(center, beside, coefficient, segment)

    y_rows = y0 + 2 * PAD

    def fine_rows(buffer, c, x, row, rows):
        start = x * y_rows + row
        if row % 8 == 0:
            start = pl.multiple_of(start, 8)
        return buffer[c, pl.ds(start, rows), :]

    def fine_plane(row):
        return pl.ds(2 * y_rows + row, x0, stride=y_rows)

    def fine_stencil(buffer, coefficient, c, x, first=0, count=y0):
        row = PAD + first
        center = fine_rows(buffer, c, x, row, count)
        beside = fine_rows(buffer, c, x - 1, row, count) + fine_rows(buffer, c, x + 1, row, count)
        beside += fine_rows(buffer, c, x, row - 1, count) + fine_rows(buffer, c, x, row + 1, count)
        return stencil(center, beside, coefficient, LANES)

    def smooth_fine(x):
        fields = mixed4(S0, [f0[c, x] for c in range(4)])
        for c in range(4):
            start = pl.multiple_of((x + 2) * y_rows + PAD, 8)
            g0[c, pl.ds(start, y0), :] = fields[c]

    pl.semaphore_wait(barrier, len(peers))
    copies = [
        send(source.at[:, pl.ds(x0 - 2, 2)], fx.at[0], (1, 0)),
        send(source.at[:, pl.ds(0, 2)], fx.at[1], (-1, 0)),
        send(fine.at[pl.ds(x0 - 1, 1)], a0.at[pl.ds(0, 1)], (1, 0)),
        send(fine.at[pl.ds(0, 1)], a0.at[pl.ds(x0 + 1, 1)], (-1, 0)),
    ]
    for load in load_parts:
        load.wait()
    load_fine.wait()
    for c in range(4):
        for k in range(2):
            n = c if k == 0 else 5 + c
            s0[0, n] = f0[c, :, k, :]
            s0[1, n] = f0[c, :, y0 - 1 - k, :]
    s0[0, 4] = a0[1 : x0 + 1, 0, :]
    s0[1, 4] = a0[1 : x0 + 1, y0 - 1, :]
    copies += send_corners(s0, d0, c0, [(c, 0) for c in range(4)], x0)
    copies.append(send(s0.at[1], p0.at[0], (0, 1)))
    copies.append(send(s0.at[0], p0.at[1], (0, -1)))

    load_smoothers.wait()
    S0 = smooth_matrix(0)
    steps(x0, smooth_fine)
    for side in range(2):
        fields = mixed4(S0, [s0[side, c] for c in range(4)])
        for c in range(4):
            o0[side, c] = fields[c]

    for c in range(4):
        for row in (PAD - 1, PAD + y0):
            g0[c, fine_plane(row), :] = jnp.zeros((x0, LANES), F32)
    load_mixers.wait()
    B0 = mix_matrix(0)
    T0 = product(S0, B0)

    def relax_fine(x):
        coefficient = a0[x - 1]
        change = mixed4(T0, [fine_stencil(g0, coefficient, c, x) for c in range(4)])
        for c in range(4):
            value = 2.0 * fine_rows(g0, c, x, PAD, y0) - change[c]
            v0[c, pl.ds(pl.multiple_of(x * y_rows + PAD, 8), y0), :] = value

    steps(x0 - 2, lambda i: relax_fine(i + 3))

    def residual_fine(i, first, count):
        total = [None] * 4
        window = slice(first, first + count)
        for s in range(2):
            x = 2 * i + s
            coefficient = a0[x + 1, window, :]
            applied = mixed4(
                B0, [fine_stencil(v0, coefficient, c, x + 2, first, count) for c in range(4)]
            )
            for c in range(4):
                rest = f0[c, x, window, :] - applied[c]
                total[c] = rest if s == 0 else total[c] + rest
        for c in range(4):
            r0[c, i, window, :] = total[c]

    steps(x1 - 2, lambda i: residual_fine(i + 1, 8, y0 - 16))
    for load in load_coarser:
        load.wait()
    third_cells = jnp.concatenate([a3[...]] * 8, axis=-1)
    k3[4 : 4 + x3, PAD : PAD + y3, :] = third_cells
    for x in range(x3):
        t3[x * y3 : (x + 1) * y3, :] = third_cells[x]
    coarse_copies = [send(t3, u3.at[0], (0, 1)), send(t3, u3.at[1], (0, -1))]
    g1[2, 3 : 3 + x1, PAD : PAD + y1, :] = jnp.concatenate([a1[...]] * 2, axis=-1)
    g2[1, 3 : 3 + x2, PAD : PAD + y2, :] = jnp.concatenate([a2[...]] * 4, axis=-1)
    early = []
    for g, xs, ys in ((g1, x1, y1), (g2, x2, y2)):
        last, own = g.shape[0] - 1, pl.ds(PAD, ys)
        early.append(
            [
                send(g.at[last, pl.ds(xs, 3), own], g.at[last, pl.ds(0, 3), own], (1, 0)),
                send(g.at[last, pl.ds(3, 3), own], g.at[last, pl.ds(xs + 3, 3), own], (-1, 0)),
            ]
        )
    smooth1, mixer1 = smooth_matrix(1), mix_matrix(1)
    S1, B1, T1 = pair_rows(smooth1), pair_rows(mixer1), pair_rows(product(smooth1, mixer1))
    smooth2, mixer2 = smooth_matrix(2), mix_matrix(2)
    S2, B2 = quad_rows(smooth2, 32), quad_rows(mixer2, 32)
    T2 = quad_rows(product(smooth2, mixer2), 32)
    smooth3, mixer3 = smooth_matrix(3), mix_matrix(3)
    S3, T3 = quad_rows(smooth3, 16), quad_rows(product(smooth3, mixer3), 16)
    T0_below = pair_rows(T0)
    T1_below = quad_rows(product(smooth1, mixer1), 32)
    T2_below = quad_rows(product(smooth2, mixer2), 16)

    wide, narrow = (2 * LANES, LANES), (LANES, LANES)
    down[...] = jnp.where(row_index(wide) // 2 == lane_index(wide), 0.125, 0.0).astype(BF16)
    last_down[...] = jnp.where(
        row_index(narrow) // 2 == lane_index(narrow) % 64, 0.125, 0.0
    ).astype(BF16)
    up[...] = children_matrix(2 * LANES, None)
    rise_fine[...] = children_matrix(2 * LANES, LANES)
    rise_second[...] = children_matrix(2 * LANES, 64)
    last_up[...] = children_matrix(LANES, None)
    last_rise[...] = children_matrix(LANES, 32)

    for copy in copies:
        copy.wait_recv()

    def smooth_beside(i):
        fields = mixed4(S0, [fx[i // 2, c, i % 2] for c in range(4)])
        for c in range(4):
            start = pl.multiple_of((i + x0 * (i // 2)) * y_rows + PAD, 8)
            g0[c, pl.ds(start, y0), :] = fields[c]

    steps(4, smooth_beside)
    for side in range(2):
        for first in (0, 5):
            fields = mixed4(S0, [p0[side, first + c] for c in range(4)])
            for c in range(4):
                p0[side, first + c] = fields[c]
    for slot in range(4):
        fields = mixed4(S0, [c0[slot, c : c + 1, :] for c in range(4)])
        for c in range(4):
            c0[slot, c : c + 1, :] = fields[c]

    @pl.when(mx == 0)
    def _():
        g0[:, 0 : 2 * y_rows] = jnp.zeros((4, 2 * y_rows, LANES), F32)
        c0[0:2] = jnp.zeros((2,) + c0.shape[1:], F32)
        a0[0] = jnp.zeros((y0, LANES), F32)

    @pl.when(mx == nx - 1)
    def _():
        g0[:, (x0 + 2) * y_rows :] = jnp.zeros((4, 2 * y_rows, LANES), F32)
        c0[2:4] = jnp.zeros((2,) + c0.shape[1:], F32)
        a0[x0 + 1] = jnp.zeros((y0, LANES), F32)

    for side, edge in ((0, 0), (1, ny - 1)):

        @pl.when(my == edge)
        def _(side=side):
            p0[side] = jnp.zeros(p0.shape[1:], F32)
            c0[side] = jnp.zeros(c0.shape[1:], F32)
            c0[2 + side] = jnp.zeros(c0.shape[1:], F32)

    for c in range(4):
        for side, row in ((0, PAD - 1), (1, PAD + y0)):
            left, right = c0[side, c : c + 1, :], c0[2 + side, c : c + 1, :]
            g0[c, y_rows + row : y_rows + row + 1, :] = left
            g0[c, (x0 + 2) * y_rows + row : (x0 + 2) * y_rows + row + 1, :] = right
            h0[side, c, PAD - 1 : PAD, :] = left
            h0[side, c, PAD + x0 : PAD + x0 + 1, :] = right
            h0[side, c, PAD : PAD + x0, :] = p0[side, c]
    steps(4, lambda i: relax_fine(1 + i + (x0 - 2) * (i // 2)))
    for side, own, halo in ((0, PAD, PAD - 1), (1, PAD + y0 - 1, PAD + y0)):
        near = [p0[side, c] for c in range(4)]
        change = mixed4(T0, [s0[side, 4] * near[c] for c in range(4)])
        for c in range(4):
            v0[c, fine_plane(own), :] += change[c]
        applied = []
        for c in range(4):
            beside = h0[side, c, PAD - 1 : PAD - 1 + x0, :] + h0[side, c, PAD + 1 : PAD + 1 + x0, :]
            beside += p0[side, 5 + c] + o0[side, c]
            applied.append(stencil(near[c], beside, p0[side, 4], LANES))
        change = mixed4(T0, applied)
        for c in range(4):
            v0[c, fine_plane(halo), :] = 2.0 * near[c] - change[c]

    steps(x1 - 2, lambda i: residual_fine(i + 1, 0, 8))
    steps(x1 - 2, lambda i: residual_fine(i + 1, y0 - 8, 8))
    steps(2, lambda i: residual_fine(i * (x1 - 1), 0, y0))

    for g in range(2):
        pieces = [
            r0[c, :, pl.ds(0, y1, stride=2), :] + r0[c, :, pl.ds(1, y1, stride=2), :]
            for c in (2 * g, 2 * g + 1)
        ]
        joined = jnp.concatenate([piece.reshape(x1 * y1, LANES) for piece in pieces], axis=-1)
        f1[g] = spread(joined, down[...]).reshape(x1, y1, LANES)
    fields = mixed2(S1, [f1[g] for g in range(2)])
    for g in range(2):
        g1[g, 3 : 3 + x1, PAD : PAD + y1, :] = fields[g]
    planes1 = [(0, 0), (0, 1), (0, 2), (1, 0), (1, 1), (1, 2), (2, 0), (2, 1)]
    cells1 = corner_cells(planes1, lambda c: 2 if c == 2 else 3)
    pack(g1, s1, planes1, 3, x1, y1)
    copies = exchange(g1, s1, p1, d1, c1, cells1, 3, x1, y1)

    def fill_beside(buffer, received):
        for side, row in ((0, PAD - y3), (1, PAD + y3)):
            inside = (my > 0) if side == 0 else (my < ny - 1)
            for x in range(x3):
                buffer[4 + x, row : row + y3, :] = jnp.where(
                    inside, received[side, x * y3 : (x + 1) * y3, :], 0.0
                )

    first_half = lane < 64
    block_steps = (2, -2, 1, -1)

    def send_block(buffer, packed, received):
        rows = slice(0, 2 * PAD)
        packed[...] = jnp.where(first_half, buffer[4, rows, :], buffer[5, rows, :])
        return [
            send(packed, received.at[n], (dx, 0)) for n, dx in enumerate(block_steps)
        ]

    def receive_block(buffer, received, copies):
        for copy in copies:
            copy.wait_recv()
        for n, dx in enumerate(block_steps):
            outside = (mx < dx) if dx > 0 else (mx >= nx + dx)
            block = jnp.where(outside, 0.0, received[n])
            turned = pltpu.roll(block, 64, 1)
            x = 4 - 2 * dx
            buffer[x, 0 : 2 * PAD, :] = jnp.where(first_half, block, turned)
            buffer[x + 1, 0 : 2 * PAD, :] = jnp.where(first_half, turned, block)

    for copy in coarse_copies:
        copy.wait_recv()
    fill_beside(k3, u3)
    coarse_copies = send_block(k3, b_k3, l_k3)

    def settle_fine(x):
        change = mixed4(T0, [fine_stencil(v0, a0[x + 1], c, x + 2) for c in range(4)])
        for c in range(4):
            value = fine_rows(v0, c, x + 2, PAD, y0) + fine_rows(g0, c, x + 2, PAD, y0)
            f0[c, x] = value - change[c]

    steps(x0, settle_fine)
    unpack(copies + early[0], g1, p1, c1, cells1, planes1, 3, x1, y1)

    def relax_second(step):
        x = step + 1
        row, rows = PAD - 2, y1 + 4
        coefficient = g1[2, x, row : row + rows, :]
        change = mixed2(T1, [stencil_of(g1, coefficient, c, x, row, rows, 64) for c in range(2)])
        for c in range(2):
            v1[c, x, row : row + rows, :] = 2.0 * g1[c, x, row : row + rows, :] - change[c]

    steps(x1 + 4, relax_second)

    def residual_second(i):
        total = [None] * 2
        for s in range(2):
            x = 2 * i + s
            coefficient = g1[2, x + 3, PAD : PAD + y1, :]
            applied = mixed2(
                B1, [stencil_of(v1, coefficient, c, x + 3, PAD, y1, 64) for c in range(2)]
            )
            for c in range(2):
                rest = f1[c, x] - applied[c]
                total[c] = rest if s == 0 else total[c] + rest
        for c in range(2):
            r1[c, i] = total[c]

    steps(x2, residual_second)

    pieces = [
        r1[c, :, pl.ds(0, y2, stride=2), :] + r1[c, :, pl.ds(1, y2, stride=2), :] for c in range(2)
    ]
    joined = jnp.concatenate([piece.reshape(x2 * y2, LANES) for piece in pieces], axis=-1)
    f2[...] = spread(joined, down[...]).reshape(x2, y2, LANES)
    g2[0, 3 : 3 + x2, PAD : PAD + y2, :] = mixed1(S2, f2[...], 32)
    planes2 = [(0, 0), (0, 1), (1, 0), (1, 1), (2, 0)]
    cells2 = corner_cells(planes2, lambda c: 3 if c == 1 else 4)
    pack(g2, s2, planes2, 3, x2, y2)
    copies = exchange(g2, s2, p2, d2, c2, cells2, 3, x2, y2)
    receive_block(k3, l_k3, coarse_copies)

    def settle_second(step):
        x = step + 2
        row, rows = PAD - 1, y1 + 2
        coefficient = g1[2, x, row : row + rows, :]
        change = mixed2(T1, [stencil_of(v1, coefficient, c, x, row, rows, 64) for c in range(2)])
        for c in range(2):
            value = v1[c, x, row : row + rows, :] + g1[c, x, row : row + rows, :] - change[c]
            x1_part[c, step, row : row + rows, :] = value

    steps(x1 + 2, settle_second)
    unpack(copies + early[1], g2, p2, c2, cells2, planes2, 3, x2, y2)

    def block_stencil(load, coefficient, x, xs, row, rows, segment):
        center = load(x, xs, row, rows)
        beside = load(x - 1, xs, row, rows) + load(x + 1, xs, row, rows)
        beside += load(x, xs, row - 1, rows) + load(x, xs, row + 1, rows)
        return center, stencil(center, beside, coefficient, segment)

    def from_g2(x, xs, row, rows):
        return g2[0, x : x + xs, row : row + rows, :]

    def from_v2(x, xs, row, rows):
        return v2[x : x + xs, row : row + rows, :]

    row, rows = PAD - 2, y2 + 4
    center, applied = block_stencil(
        from_g2, g2[1, 1 : x2 + 5, row : row + rows, :], 1, x2 + 4, row, rows, 32
    )
    v2[1 : x2 + 5, row : row + rows, :] = 2.0 * center - mixed1(T2, applied, 32)
    _, applied = block_stencil(
        from_v2, g2[1, 3 : 3 + x2, PAD : PAD + y2, :], 3, x2, PAD, y2, 32
    )
    rest = f2[...] - mixed1(B2, applied, 32)
    pairs = jnp.concatenate([rest[2 * i] + rest[2 * i + 1] for i in range(x3)], axis=0)
    r3[...] = spread(pairs, last_down[...]).reshape(x3, y2, LANES)

    forcing = r3[:, pl.ds(0, y3, stride=2), :] + r3[:, pl.ds(1, y3, stride=2), :]
    smoothed = mixed1(S3, forcing, 16)
    g3[4 : 4 + x3, PAD : PAD + y3, :] = smoothed
    for x in range(x3):
        s3[x * y3 : (x + 1) * y3, :] = smoothed[x]
        line[x : x + 1, :] = jnp.sum(smoothed[x], axis=0, keepdims=True)
    copies = [send(line, lines.at[k - 1], (0, k)) for k in range(1, ny)]
    copies += [send(s3, p3.at[0], (0, 1)), send(s3, p3.at[1], (0, -1))]
    row, rows = PAD - 1, y2 + 2
    center, applied = block_stencil(
        from_v2, g2[1, 2 : x2 + 4, row : row + rows, :], 2, x2 + 2, row, rows, 32
    )
    x2_part[:, row : row + rows, :] = (
        center + g2[0, 2 : x2 + 4, row : row + rows, :] - mixed1(T2, applied, 32)
    )
    for copy in copies:
        copy.wait_recv()
    total = line[...]
    for k in range(1, ny):
        total += lines[k - 1]
    total *= 4.0 / math.sqrt(ny * y3)
    for x in range(x3):
        g3[4 + x, 0:1, :] = total[x : x + 1, :]
    fill_beside(g3, p3)
    receive_block(g3, l_g3, send_block(g3, b_g3, l_g3))

    low, high = PAD - y3, PAD + 2 * y3
    cell = lax.broadcasted_iota(jnp.int32, (1, 3 * y3, LANES), 1) + (my - 1) * y3
    inside = (cell >= 0) & (cell < ny * y3)
    w3[:, low:high, :] = g3[:, low:high, :] + jnp.where(inside, g3[:, 0:1, :], 0.0)

    def from_w3(x, xs, row, rows):
        return w3[x : x + xs, row : row + rows, :]

    for sweep in range(1, 4):
        x, xs = sweep, 8 + x3 - 2 * sweep
        row, rows = low + sweep, high - low - 2 * sweep
        center, applied = block_stencil(
            from_w3, k3[x : x + xs, row : row + rows, :], x, xs, row, rows, 16
        )
        value = center + g3[x : x + xs, row : row + rows, :] - mixed1(T3, applied, 16)
        if sweep < 3:
            w3[x : x + xs, row : row + rows, :] = value
        else:
            b3[:, row : row + rows, :] = value

    below = b3[...]
    mixed = mixed1(T2_below, below, 16)
    flat = ((x3 + 2) * 2 * PAD, LANES)
    e2[...] = spread_stacked((below - mixed).reshape(flat), last_up[...]).reshape(e2.shape)
    m2[...] = spread_stacked(mixed.reshape(flat), last_rise[...]).reshape(m2.shape)
    q2[...] = spread_stacked(mixed.reshape(flat), last_up[...]).reshape(q2.shape)

    def raised(m, q, c, i, s, t, row, rows):
        other_y = q[c, i, row + 2 * t - 1 : row + 2 * t - 1 + rows, :]
        other_x = q[c, i + 2 * s - 1, row : row + rows, :]
        return m[c, i, row : row + rows, :] - other_y - other_x

    for x in range(-1, x2 + 1):
        i, s = x // 2 + 1, x % 2
        for t in range(2):
            row, rows = PAD - t, y3 + 1
            cells = pl.ds(PAD - t, rows, stride=2)
            value = raised(m2, q2, 0, i, s, t, row, rows)
            w2[x + 1, cells, :] = (
                x2_part[x + 1, cells, :]
                + e2[0, i, row : row + rows, :]
                - g2[1, x + 3, cells, :] * value
            )

    below = w2[...]
    mixed = mixed1(T1_below, below, 32)
    flat = ((x2 + 2) * (y2 + 2 * PAD), LANES)
    shape = (x2 + 2, y2 + 2 * PAD, LANES)
    for field, matrix, target in (
        (below - mixed, up, e1),
        (mixed, rise_second, m1),
        (mixed, up, q1),
    ):
        children = spread_stacked(field.reshape(flat), matrix[...])
        for c in range(2):
            target[c] = children[:, c * LANES : (c + 1) * LANES].reshape(shape)
    for x in range(-1, x1 + 1):
        i, s = x // 2 + 1, x % 2
        for t in range(2):
            row, rows = PAD - t, y2 + 1
            cells = pl.ds(PAD - t, rows, stride=2)
            coefficient = g1[2, x + 3, cells, :]
            for c in range(2):
                value = raised(m1, q1, c, i, s, t, row, rows)
                w1[c, x + 1, cells, :] = (
                    x1_part[c, x + 1, cells, :]
                    + e1[c, i, row : row + rows, :]
                    - coefficient * value
                )

    below = [w1[c] for c in range(2)]
    mixed = mixed2(T0_below, below)
    own = slice(1, x1 + 1), slice(PAD, PAD + y1)
    for g in range(2):
        inner = (x1 * y1, LANES)
        for field, matrix, target in (
            ((below[g] - mixed[g])[own].reshape(inner), up, e0),
            (mixed[g][own].reshape(inner), rise_fine, m0),
        ):
            children = spread_stacked(field, matrix[...])
            for c in range(2):
                part = children[:, c * LANES : (c + 1) * LANES]
                target[2 * g + c, 1 : x1 + 1, PAD : PAD + y1, :] = part.reshape(x1, y1, LANES)
        children = spread_stacked(
            mixed[g].reshape((x1 + 2) * (y1 + 2 * PAD), LANES), up[...]
        )
        for c in range(2):
            part = children[:, c * LANES : (c + 1) * LANES]
            q0[2 * g + c] = part.reshape(x1 + 2, y1 + 2 * PAD, LANES)

    def finish_fine(step):
        i = step + 1
        for t in range(2):
            cells = pl.ds(t, y1, stride=2)
            coefficient = [a0[2 * step + s + 1, pl.ds(t, y1, stride=2), :] for s in range(2)]
            for c in range(4):
                for s in range(2):
                    value = raised(m0, q0, c, i, s, t, PAD, y1)
                    x = 2 * step + s
                    out[c, x, cells, :] = (
                        f0[c, x, cells, :]
                        + e0[c, i, PAD : PAD + y1, :]
                        - coefficient[s] * value
                    )

    steps(x1, finish_fine)
    for copy in started:
        copy.wait_send()


def per_device(nx, ny, source, fine, second, third, coarse, mixers, smoothers):
    x0, y0 = source.shape[1:3]
    x1, y1 = second.shape[:2]
    x2, y2 = third.shape[:2]
    x3, y3 = coarse.shape[:2]

    def padded(groups, xs, ys, h):
        return pltpu.VMEM((groups, xs + 2 * h, ys + 2 * PAD, LANES), F32)

    def vmem(*shape):
        return pltpu.VMEM(shape, F32)

    def faces(planes, near, xs):
        rows = max(xs, 8)
        return [
            vmem(2, planes, rows, LANES),
            vmem(2, planes, rows, LANES),
            vmem(4, near, LANES),
            vmem(4, near, LANES),
        ]

    def three(groups, xs, ys):
        return [vmem(groups, xs + 2, ys + 2 * PAD, LANES)] * 3

    double = pltpu.VMEM((2 * LANES, 2 * LANES), BF16)
    tall = pltpu.VMEM((2 * LANES, LANES), BF16)
    scratch = (
        [vmem(2, 4, 2, y0, LANES), vmem(2, 4, x0, LANES), vmem(4, x0, y0, LANES), vmem(x0 + 2, y0, LANES)]
        + [vmem(4, (x0 + 4) * (y0 + 2 * PAD), LANES)] * 2
        + [vmem(2, 4, x0 + 2 * PAD, LANES)]
        + [vmem(4, x1, y0, LANES)]
        + three(4, x1, y1)
        + faces(9, 8, x0)
        + [vmem(*second.shape), vmem(2, x1, y1, LANES), padded(3, x1, y1, 3), padded(2, x1, y1, 3)]
        + [vmem(2, x2, y1, LANES), vmem(2, x1 + 2, y1 + 2 * PAD, LANES)]
        + three(2, x2, y2)
        + [vmem(2, x1 + 2, y1 + 2 * PAD, LANES)]
        + faces(8, 8, x1)
        + [vmem(*third.shape), vmem(x2, y2, LANES), padded(2, x2, y2, 3)]
        + [vmem(x2 + 6, y2 + 2 * PAD, LANES), vmem(x3, y2, LANES)]
        + [vmem(x2 + 2, y2 + 2 * PAD, LANES)]
        + [vmem(1, x3 + 2, 2 * PAD, LANES)] * 3
        + [vmem(x2 + 2, y2 + 2 * PAD, LANES)]
        + faces(5, 16, x2)
        + [vmem(*coarse.shape), vmem(x3, y2, LANES)]
        + [vmem(x3 + 8, 24, LANES)] * 3
        + [vmem(x3 + 2, 2 * PAD, LANES)]
        + [vmem(x3 * y3, LANES), vmem(2, x3 * y3, LANES)] * 2
        + [vmem(2 * PAD, LANES), vmem(4, 2 * PAD, LANES)] * 2
        + [vmem(x3, LANES), vmem(ny - 1, x3, LANES)]
        + [vmem(64, LANES)]
        + [tall, double, double, double, pltpu.VMEM((LANES, LANES), BF16), tall, tall]
    )
    copies = 8 * 3 + 4 + 4 + 2 * 2 + (ny - 1) + 4 * 2
    scratch += [
        pltpu.SMEM(mixers.shape, F32),
        pltpu.SMEM(smoothers.shape, F32),
        pltpu.SemaphoreType.DMA((copies,)),
        pltpu.SemaphoreType.DMA((copies,)),
        pltpu.SemaphoreType.DMA((10,)),
    ]
    anywhere = pl.BlockSpec(memory_space=pl.ANY)
    return pl.pallas_call(
        functools.partial(kernel, nx, ny),
        out_shape=pltpu.VMEM(source.shape, F32),
        in_specs=[anywhere] * 7,
        out_specs=pl.BlockSpec(memory_space=pltpu.VMEM),
        scratch_shapes=scratch,
        compiler_params=pltpu.CompilerParams(
            collective_id=0, has_side_effects=True, vmem_limit_bytes=56 * 1024 * 1024
        ),
    )(source, fine, second, third, coarse, mixers, smoothers)


def solution(mesh):
    field, cells = P(None, "gx", "gy", None), P("gx", "gy", None)
    return jax.shard_map(
        functools.partial(per_device, mesh.shape["gx"], mesh.shape["gy"]),
        mesh=mesh,
        in_specs=(field, cells, cells, cells, cells, P(), P()),
        out_specs=field,
        check_vma=False,
    )
```

```python
import functools
import math

import jax
import jax.numpy as jnp
from jax import lax
from jax.experimental import pallas as pl
from jax.experimental.pallas import tpu as pltpu
from jax.sharding import PartitionSpec as P

MESH = pl.DeviceIdType.MESH
F32 = jnp.float32
BF16 = jnp.bfloat16
LANES = 128
PAD = 8


def spread(field, matrix):
    high = field.astype(BF16)
    low = (field - high.astype(F32)).astype(BF16)
    return jnp.dot(high, matrix, preferred_element_type=F32) + jnp.dot(
        low, matrix, preferred_element_type=F32
    )


def spread_stacked(field, matrix):
    high = field.astype(BF16)
    low = (field - high.astype(F32)).astype(BF16)
    return jnp.dot(jnp.concatenate([high, low], axis=-1), matrix, preferred_element_type=F32)


def lane_index(shape):
    return lax.broadcasted_iota(jnp.int32, shape, len(shape) - 1)


def beside_z(field, segment):
    lane = lane_index((1, LANES)) % segment
    axis = field.ndim - 1
    before = jnp.where(lane == 0, 0.0, pltpu.roll(field, 1, axis))
    after = jnp.where(lane == segment - 1, 0.0, pltpu.roll(field, LANES - 1, axis))
    return before + after


def stencil(center, beside, coefficient, segment):
    total = beside + beside_z(center, segment)
    return coefficient * (6.0 * center - total) + center


def kernel(
    nx, ny,
    source, fine, second, third, coarse, mixers_in, smoothers_in, out,
    fx, o0, f0, a0, g0, v0, h0, r0, e0, m0, q0, s0, p0, d0, c0,
    a1, f1, g1, v1, r1, x1_part, e1, m1, q1, w1, s1, p1, d1, c1,
    a2, f2, g2, v2, r2, x2_part, e2, m2, q2, w2, s2, p2, d2, c2,
    a3, r3, g3, k3, w3, b3, s3, p3, t3, u3, b_k3, l_k3, b_g3, l_g3, line, lines,
    table, down, up, rise_fine, rise_second, last_down, last_up, last_rise,
    mixers, smoothers, send_sem, recv_sem, local_sem,
):
    mx, my = lax.axis_index("gx"), lax.axis_index("gy")

    def device(dx, dy):
        return (lax.rem(mx + (dx + nx), nx), lax.rem(my + (dy + ny), ny))

    barrier = pltpu.get_barrier_semaphore()
    peers = [(0, k) for k in range(1, ny)]
    peers += [(dx, dy) for dx in (-1, 1) for dy in (-1, 0, 1)] + [(-2, 0), (2, 0)]
    x0, y0 = f0.shape[1:3]
    x1, y1 = f1.shape[1:3]
    x2, y2 = f2.shape[:2]
    x3, y3 = a3.shape[:2]
    part_rows = x0 // 4
    parts = [(n * part_rows, part_rows) for n in range(4)]
    load_fine = pltpu.make_async_copy(fine, a0.at[pl.ds(1, x0)], local_sem.at[0])
    load_parts = [
        pltpu.make_async_copy(
            source.at[:, pl.ds(x, xs)], f0.at[:, pl.ds(x, xs)], local_sem.at[4 + n]
        )
        for n, (x, xs) in enumerate(parts)
    ]
    load_coarser = [
        pltpu.make_async_copy(second, a1, local_sem.at[1]),
        pltpu.make_async_copy(third, a2, local_sem.at[2]),
        pltpu.make_async_copy(coarse, a3, local_sem.at[3]),
    ]
    load_smoothers = pltpu.make_async_copy(smoothers_in, smoothers, local_sem.at[8])
    load_mixers = pltpu.make_async_copy(mixers_in, mixers, local_sem.at[9])
    for load in [load_smoothers] + load_parts + [load_fine, load_mixers] + load_coarser:
        load.start()
    for dx, dy in peers:
        pl.semaphore_signal(barrier, inc=1, device_id=device(dx, dy), device_id_type=MESH)

    def smooth_matrix(level):
        return [
            [smoothers[level, i, j] + (0.25 if i == j else 0.0) for j in range(4)]
            for i in range(4)
        ]

    def mix_matrix(level):
        return [
            [mixers[level, i, j] + (1.0 if i == j else 0.0) for j in range(4)] for i in range(4)
        ]

    def product(left, right):
        return [
            [sum(left[i][k] * right[k][j] for k in range(4)) for j in range(4)] for i in range(4)
        ]

    lane = lane_index((1, LANES))
    rows_used = [0]

    def keep(vector):
        row = rows_used[0]
        rows_used[0] += 1
        table[row : row + 1, :] = vector
        return row

    def pair_rows(matrix):
        return [
            [
                [
                    keep(
                        jnp.where(
                            lane < 64,
                            matrix[2 * g][2 * h + s],
                            matrix[2 * g + 1][2 * h + 1 - s],
                        )
                    )
                    for s in range(2)
                ]
                for h in range(2)
            ]
            for g in range(2)
        ]

    def quad_rows(matrix, segment):
        channel = (lane // segment) % 4
        rows = []
        for k in range(4):
            vector = jnp.zeros((1, LANES), F32)
            for i in range(4):
                vector = jnp.where(channel == i, matrix[i][(i - k) % 4], vector)
            rows.append(keep(vector))
        return rows


    def mixed4(matrix, fields):
        return [
            matrix[i][0] * fields[0]
            + matrix[i][1] * fields[1]
            + (matrix[i][2] * fields[2] + matrix[i][3] * fields[3])
            for i in range(4)
        ]

    def vector_of(row):
        return table[row : row + 1, :]

    def mixed2(rows, fields):
        turned = [pltpu.roll(field, 64, field.ndim - 1) for field in fields]
        return [
            vector_of(rows[g][0][0]) * fields[0]
            + vector_of(rows[g][0][1]) * turned[0]
            + (vector_of(rows[g][1][0]) * fields[1] + vector_of(rows[g][1][1]) * turned[1])
            for g in range(2)
        ]

    def mixed1(rows, field, segment):
        total = vector_of(rows[0]) * field
        for k in range(1, 4):
            total += vector_of(rows[k]) * pltpu.roll(field, k * segment, field.ndim - 1)
        return total

    def row_index(shape):
        return lax.broadcasted_iota(jnp.int32, shape, 0)

    def children_matrix(columns, segment):
        shape = (2 * LANES, columns)
        row, column = row_index(shape) % LANES, lane_index(shape)
        if segment is None:
            return jnp.where(row == column // 2, 1.0, 0.0).astype(BF16)
        odd = column % 2
        other = column // 2 + 2 * odd - 1
        place = column % segment
        valid = (place != 0) & (place != segment - 1)
        own = jnp.where(row == column // 2, 3.0, 0.0)
        return (own - jnp.where((row == other) & valid, 1.0, 0.0)).astype(BF16)

    started = []

    def send(src, dst, place):
        number = len(started)
        copy = pltpu.make_async_remote_copy(
            src_ref=src, dst_ref=dst, send_sem=send_sem.at[number], recv_sem=recv_sem.at[number],
            device_id=device(*place), device_id_type=MESH,
        )
        copy.start()
        started.append(copy)
        return copy

    def pack(g, s, planes, h, xs, ys):
        for p, (k, c) in enumerate(planes):
            s[0, p, 0:xs, :] = g[c, h : h + xs, PAD + k, :]
            s[1, p, 0:xs, :] = g[c, h : h + xs, PAD + ys - 1 - k, :]

    def corner_cells(planes, reach_of):
        return [
            (n, i) for n, (k, c) in enumerate(planes) for i in range(reach_of(c) - 1 - k)
        ]

    def send_corners(s, packed, corner, cells, xs):
        copies = []
        for side, dy in ((1, 1), (0, -1)):
            for dx in (1, -1):
                slot = (0 if dx > 0 else 1) * 2 + (0 if dy > 0 else 1)
                for r, (n, i) in enumerate(cells):
                    x = xs - 1 - i if dx > 0 else i
                    packed[slot, r : r + 1, :] = s[side, n, x : x + 1, :]
                copies.append(send(packed.at[slot], corner.at[slot], (dx, dy)))
        return copies

    def exchange(g, s, p, packed, corner, cells, h, xs, ys):
        own = pl.ds(PAD, ys)
        copies = [
            send(g.at[:, pl.ds(xs, h), own], g.at[:, pl.ds(0, h), own], (1, 0)),
            send(g.at[:, pl.ds(h, h), own], g.at[:, pl.ds(xs + h, h), own], (-1, 0)),
        ]
        copies += send_corners(s, packed, corner, cells, xs)
        copies.append(send(s.at[1], p.at[0], (0, 1)))
        copies.append(send(s.at[0], p.at[1], (0, -1)))
        return copies

    def unpack(copies, g, p, corner, cells, planes, h, xs, ys):
        for copy in copies:
            copy.wait_recv()
        groups = g.shape[0]
        for n, (k, c) in enumerate(planes):
            g[c, h : h + xs, PAD - 1 - k, :] = p[0, n, 0:xs, :]
            g[c, h : h + xs, PAD + ys + k, :] = p[1, n, 0:xs, :]
        for r, (n, i) in enumerate(cells):
            k, c = planes[n]
            for from_dy in range(2):
                row = PAD - 1 - k if from_dy == 0 else PAD + ys + k
                g[c, h - 1 - i, row : row + 1, :] = corner[from_dy, r : r + 1, :]
                g[c, h + xs + i, row : row + 1, :] = corner[2 + from_dy, r : r + 1, :]

        @pl.when(mx == 0)
        def _():
            g[:, 0:h] = jnp.zeros((groups, h) + g.shape[2:], F32)

        @pl.when(mx == nx - 1)
        def _():
            g[:, h + xs :] = jnp.zeros((groups, h) + g.shape[2:], F32)

        @pl.when(my == 0)
        def _():
            g[:, :, 0:PAD] = jnp.zeros(g.shape[:2] + (PAD, LANES), F32)

        @pl.when(my == ny - 1)
        def _():
            g[:, :, PAD + ys :] = jnp.zeros(g.shape[:2] + (PAD, LANES), F32)

    def steps(count, body):
        def step(i, carry):
            body(i)
            return carry

        lax.fori_loop(0, count, step, 0, unroll=2)

    def stencil_of(field, coefficient, c, x, row, rows, segment):
        center = field[c, x, row : row + rows, :]
        beside = field[c, x - 1, row : row + rows, :] + field[c, x + 1, row : row + rows, :]
        beside += field[c, x, row - 1 : row - 1 + rows, :]
        beside += field[c, x, row + 1 : row + 1 + rows, :]
        return stencil(center, beside, coefficient, segment)

    y_rows = y0 + 2 * PAD

    def fine_rows(buffer, c, x, row, rows):
        start = x * y_rows + row
        if row % 8 == 0:
            start = pl.multiple_of(start, 8)
        return buffer[c, pl.ds(start, rows), :]

    def fine_plane(row):
        return pl.ds(2 * y_rows + row, x0, stride=y_rows)

    def fine_stencil(buffer, coefficient, c, x, first=0, count=y0):
        row = PAD + first
        center = fine_rows(buffer, c, x, row, count)
        beside = fine_rows(buffer, c, x - 1, row, count) + fine_rows(buffer, c, x + 1, row, count)
        beside += fine_rows(buffer, c, x, row - 1, count) + fine_rows(buffer, c, x, row + 1, count)
        return stencil(center, beside, coefficient, LANES)

    def smooth_fine(x):
        fields = mixed4(S0, [f0[c, x] for c in range(4)])
        for c in range(4):
            start = pl.multiple_of((x + 2) * y_rows + PAD, 8)
            g0[c, pl.ds(start, y0), :] = fields[c]

    pl.semaphore_wait(barrier, len(peers))
    copies = [
        send(source.at[:, pl.ds(x0 - 2, 2)], fx.at[0], (1, 0)),
        send(source.at[:, pl.ds(0, 2)], fx.at[1], (-1, 0)),
        send(fine.at[pl.ds(x0 - 1, 1)], a0.at[pl.ds(0, 1)], (1, 0)),
        send(fine.at[pl.ds(0, 1)], a0.at[pl.ds(x0 + 1, 1)], (-1, 0)),
    ]
    for load in load_parts:
        load.wait()
    load_fine.wait()
    for c in range(4):
        for k in range(2):
            n = c if k == 0 else 5 + c
            s0[0, n] = f0[c, :, k, :]
            s0[1, n] = f0[c, :, y0 - 1 - k, :]
    s0[0, 4] = a0[1 : x0 + 1, 0, :]
    s0[1, 4] = a0[1 : x0 + 1, y0 - 1, :]
    copies += send_corners(s0, d0, c0, [(c, 0) for c in range(4)], x0)
    copies.append(send(s0.at[1], p0.at[0], (0, 1)))
    copies.append(send(s0.at[0], p0.at[1], (0, -1)))

    load_smoothers.wait()
    S0 = smooth_matrix(0)
    steps(x0, smooth_fine)
    for side in range(2):
        fields = mixed4(S0, [s0[side, c] for c in range(4)])
        for c in range(4):
            o0[side, c] = fields[c]

    for c in range(4):
        for row in (PAD - 1, PAD + y0):
            g0[c, fine_plane(row), :] = jnp.zeros((x0, LANES), F32)
    load_mixers.wait()
    B0 = mix_matrix(0)
    T0 = product(S0, B0)

    def relax_fine(x):
        coefficient = a0[x - 1]
        change = mixed4(T0, [fine_stencil(g0, coefficient, c, x) for c in range(4)])
        for c in range(4):
            value = 2.0 * fine_rows(g0, c, x, PAD, y0) - change[c]
            v0[c, pl.ds(pl.multiple_of(x * y_rows + PAD, 8), y0), :] = value

    steps(x0 - 2, lambda i: relax_fine(i + 3))

    def residual_fine(i, first, count):
        total = [None] * 4
        window = slice(first, first + count)
        for s in range(2):
            x = 2 * i + s
            coefficient = a0[x + 1, window, :]
            applied = mixed4(
                B0, [fine_stencil(v0, coefficient, c, x + 2, first, count) for c in range(4)]
            )
            for c in range(4):
                rest = f0[c, x, window, :] - applied[c]
                total[c] = rest if s == 0 else total[c] + rest
        for c in range(4):
            r0[c, i, window, :] = total[c]

    steps(x1 - 2, lambda i: residual_fine(i + 1, 8, y0 - 16))
    for load in load_coarser:
        load.wait()
    third_cells = jnp.concatenate([a3[...]] * 8, axis=-1)
    k3[4 : 4 + x3, PAD : PAD + y3, :] = third_cells
    for x in range(x3):
        t3[x * y3 : (x + 1) * y3, :] = third_cells[x]
    coarse_copies = [send(t3, u3.at[0], (0, 1)), send(t3, u3.at[1], (0, -1))]
    g1[2, 3 : 3 + x1, PAD : PAD + y1, :] = jnp.concatenate([a1[...]] * 2, axis=-1)
    g2[1, 3 : 3 + x2, PAD : PAD + y2, :] = jnp.concatenate([a2[...]] * 4, axis=-1)
    smooth1, mixer1 = smooth_matrix(1), mix_matrix(1)
    S1, B1, T1 = pair_rows(smooth1), pair_rows(mixer1), pair_rows(product(smooth1, mixer1))
    smooth2, mixer2 = smooth_matrix(2), mix_matrix(2)
    S2, B2 = quad_rows(smooth2, 32), quad_rows(mixer2, 32)
    T2 = quad_rows(product(smooth2, mixer2), 32)
    smooth3, mixer3 = smooth_matrix(3), mix_matrix(3)
    S3, T3 = quad_rows(smooth3, 16), quad_rows(product(smooth3, mixer3), 16)
    T0_below = pair_rows(T0)
    T1_below = quad_rows(product(smooth1, mixer1), 32)
    T2_below = quad_rows(product(smooth2, mixer2), 16)

    wide, narrow = (2 * LANES, LANES), (LANES, LANES)
    down[...] = jnp.where(row_index(wide) // 2 == lane_index(wide), 0.125, 0.0).astype(BF16)
    last_down[...] = jnp.where(
        row_index(narrow) // 2 == lane_index(narrow) % 64, 0.125, 0.0
    ).astype(BF16)
    up[...] = children_matrix(2 * LANES, None)
    rise_fine[...] = children_matrix(2 * LANES, LANES)
    rise_second[...] = children_matrix(2 * LANES, 64)
    last_up[...] = children_matrix(LANES, None)
    last_rise[...] = children_matrix(LANES, 32)

    for copy in copies:
        copy.wait_recv()

    def smooth_beside(i):
        fields = mixed4(S0, [fx[i // 2, c, i % 2] for c in range(4)])
        for c in range(4):
            start = pl.multiple_of((i + x0 * (i // 2)) * y_rows + PAD, 8)
            g0[c, pl.ds(start, y0), :] = fields[c]

    steps(4, smooth_beside)
    for side in range(2):
        for first in (0, 5):
            fields = mixed4(S0, [p0[side, first + c] for c in range(4)])
            for c in range(4):
                p0[side, first + c] = fields[c]
    for slot in range(4):
        fields = mixed4(S0, [c0[slot, c : c + 1, :] for c in range(4)])
        for c in range(4):
            c0[slot, c : c + 1, :] = fields[c]

    @pl.when(mx == 0)
    def _():
        g0[:, 0 : 2 * y_rows] = jnp.zeros((4, 2 * y_rows, LANES), F32)
        c0[0:2] = jnp.zeros((2,) + c0.shape[1:], F32)
        a0[0] = jnp.zeros((y0, LANES), F32)

    @pl.when(mx == nx - 1)
    def _():
        g0[:, (x0 + 2) * y_rows :] = jnp.zeros((4, 2 * y_rows, LANES), F32)
        c0[2:4] = jnp.zeros((2,) + c0.shape[1:], F32)
        a0[x0 + 1] = jnp.zeros((y0, LANES), F32)

    for side, edge in ((0, 0), (1, ny - 1)):

        @pl.when(my == edge)
        def _(side=side):
            p0[side] = jnp.zeros(p0.shape[1:], F32)
            c0[side] = jnp.zeros(c0.shape[1:], F32)
            c0[2 + side] = jnp.zeros(c0.shape[1:], F32)

    for c in range(4):
        for side, row in ((0, PAD - 1), (1, PAD + y0)):
            left, right = c0[side, c : c + 1, :], c0[2 + side, c : c + 1, :]
            g0[c, y_rows + row : y_rows + row + 1, :] = left
            g0[c, (x0 + 2) * y_rows + row : (x0 + 2) * y_rows + row + 1, :] = right
            h0[side, c, PAD - 1 : PAD, :] = left
            h0[side, c, PAD + x0 : PAD + x0 + 1, :] = right
            h0[side, c, PAD : PAD + x0, :] = p0[side, c]
    steps(4, lambda i: relax_fine(1 + i + (x0 - 2) * (i // 2)))
    for side, own, halo in ((0, PAD, PAD - 1), (1, PAD + y0 - 1, PAD + y0)):
        near = [p0[side, c] for c in range(4)]
        change = mixed4(T0, [s0[side, 4] * near[c] for c in range(4)])
        for c in range(4):
            v0[c, fine_plane(own), :] += change[c]
        applied = []
        for c in range(4):
            beside = h0[side, c, PAD - 1 : PAD - 1 + x0, :] + h0[side, c, PAD + 1 : PAD + 1 + x0, :]
            beside += p0[side, 5 + c] + o0[side, c]
            applied.append(stencil(near[c], beside, p0[side, 4], LANES))
        change = mixed4(T0, applied)
        for c in range(4):
            v0[c, fine_plane(halo), :] = 2.0 * near[c] - change[c]

    steps(x1 - 2, lambda i: residual_fine(i + 1, 0, 8))
    steps(x1 - 2, lambda i: residual_fine(i + 1, y0 - 8, 8))
    steps(2, lambda i: residual_fine(i * (x1 - 1), 0, y0))

    for g in range(2):
        pieces = [
            r0[c, :, pl.ds(0, y1, stride=2), :] + r0[c, :, pl.ds(1, y1, stride=2), :]
            for c in (2 * g, 2 * g + 1)
        ]
        joined = jnp.concatenate([piece.reshape(x1 * y1, LANES) for piece in pieces], axis=-1)
        f1[g] = spread(joined, down[...]).reshape(x1, y1, LANES)
    fields = mixed2(S1, [f1[g] for g in range(2)])
    for g in range(2):
        g1[g, 3 : 3 + x1, PAD : PAD + y1, :] = fields[g]
    planes1 = [(0, 0), (0, 1), (0, 2), (1, 0), (1, 1), (1, 2), (2, 0), (2, 1)]
    cells1 = corner_cells(planes1, lambda c: 2 if c == 2 else 3)
    pack(g1, s1, planes1, 3, x1, y1)
    copies = exchange(g1, s1, p1, d1, c1, cells1, 3, x1, y1)

    def fill_beside(buffer, received):
        for side, row in ((0, PAD - y3), (1, PAD + y3)):
            inside = (my > 0) if side == 0 else (my < ny - 1)
            for x in range(x3):
                buffer[4 + x, row : row + y3, :] = jnp.where(
                    inside, received[side, x * y3 : (x + 1) * y3, :], 0.0
                )

    first_half = lane < 64
    block_steps = (2, -2, 1, -1)

    def send_block(buffer, packed, received):
        rows = slice(0, 2 * PAD)
        packed[...] = jnp.where(first_half, buffer[4, rows, :], buffer[5, rows, :])
        return [
            send(packed, received.at[n], (dx, 0)) for n, dx in enumerate(block_steps)
        ]

    def receive_block(buffer, received, copies):
        for copy in copies:
            copy.wait_recv()
        for n, dx in enumerate(block_steps):
            outside = (mx < dx) if dx > 0 else (mx >= nx + dx)
            block = jnp.where(outside, 0.0, received[n])
            turned = pltpu.roll(block, 64, 1)
            x = 4 - 2 * dx
            buffer[x, 0 : 2 * PAD, :] = jnp.where(first_half, block, turned)
            buffer[x + 1, 0 : 2 * PAD, :] = jnp.where(first_half, turned, block)

    for copy in coarse_copies:
        copy.wait_recv()
    fill_beside(k3, u3)
    coarse_copies = send_block(k3, b_k3, l_k3)

    def settle_fine(x):
        change = mixed4(T0, [fine_stencil(v0, a0[x + 1], c, x + 2) for c in range(4)])
        for c in range(4):
            value = fine_rows(v0, c, x + 2, PAD, y0) + fine_rows(g0, c, x + 2, PAD, y0)
            f0[c, x] = value - change[c]

    steps(x0, settle_fine)
    unpack(copies, g1, p1, c1, cells1, planes1, 3, x1, y1)

    def relax_second(step):
        x = step + 1
        row, rows = PAD - 2, y1 + 4
        coefficient = g1[2, x, row : row + rows, :]
        change = mixed2(T1, [stencil_of(g1, coefficient, c, x, row, rows, 64) for c in range(2)])
        for c in range(2):
            v1[c, x, row : row + rows, :] = 2.0 * g1[c, x, row : row + rows, :] - change[c]

    steps(x1 + 4, relax_second)

    def residual_second(i):
        total = [None] * 2
        for s in range(2):
            x = 2 * i + s
            coefficient = g1[2, x + 3, PAD : PAD + y1, :]
            applied = mixed2(
                B1, [stencil_of(v1, coefficient, c, x + 3, PAD, y1, 64) for c in range(2)]
            )
            for c in range(2):
                rest = f1[c, x] - applied[c]
                total[c] = rest if s == 0 else total[c] + rest
        for c in range(2):
            r1[c, i] = total[c]

    steps(x2, residual_second)

    pieces = [
        r1[c, :, pl.ds(0, y2, stride=2), :] + r1[c, :, pl.ds(1, y2, stride=2), :] for c in range(2)
    ]
    joined = jnp.concatenate([piece.reshape(x2 * y2, LANES) for piece in pieces], axis=-1)
    f2[...] = spread(joined, down[...]).reshape(x2, y2, LANES)
    g2[0, 3 : 3 + x2, PAD : PAD + y2, :] = mixed1(S2, f2[...], 32)
    planes2 = [(0, 0), (0, 1), (1, 0), (1, 1), (2, 0)]
    cells2 = corner_cells(planes2, lambda c: 3 if c == 1 else 4)
    pack(g2, s2, planes2, 3, x2, y2)
    copies = exchange(g2, s2, p2, d2, c2, cells2, 3, x2, y2)
    receive_block(k3, l_k3, coarse_copies)

    def settle_second(step):
        x = step + 2
        row, rows = PAD - 1, y1 + 2
        coefficient = g1[2, x, row : row + rows, :]
        change = mixed2(T1, [stencil_of(v1, coefficient, c, x, row, rows, 64) for c in range(2)])
        for c in range(2):
            value = v1[c, x, row : row + rows, :] + g1[c, x, row : row + rows, :] - change[c]
            x1_part[c, step, row : row + rows, :] = value

    steps(x1 + 2, settle_second)
    unpack(copies, g2, p2, c2, cells2, planes2, 3, x2, y2)

    def block_stencil(load, coefficient, x, xs, row, rows, segment):
        center = load(x, xs, row, rows)
        beside = load(x - 1, xs, row, rows) + load(x + 1, xs, row, rows)
        beside += load(x, xs, row - 1, rows) + load(x, xs, row + 1, rows)
        return center, stencil(center, beside, coefficient, segment)

    def from_g2(x, xs, row, rows):
        return g2[0, x : x + xs, row : row + rows, :]

    def from_v2(x, xs, row, rows):
        return v2[x : x + xs, row : row + rows, :]

    row, rows = PAD - 2, y2 + 4
    center, applied = block_stencil(
        from_g2, g2[1, 1 : x2 + 5, row : row + rows, :], 1, x2 + 4, row, rows, 32
    )
    v2[1 : x2 + 5, row : row + rows, :] = 2.0 * center - mixed1(T2, applied, 32)
    _, applied = block_stencil(
        from_v2, g2[1, 3 : 3 + x2, PAD : PAD + y2, :], 3, x2, PAD, y2, 32
    )
    rest = f2[...] - mixed1(B2, applied, 32)
    pairs = jnp.concatenate([rest[2 * i] + rest[2 * i + 1] for i in range(x3)], axis=0)
    r3[...] = spread(pairs, last_down[...]).reshape(x3, y2, LANES)

    forcing = r3[:, pl.ds(0, y3, stride=2), :] + r3[:, pl.ds(1, y3, stride=2), :]
    smoothed = mixed1(S3, forcing, 16)
    g3[4 : 4 + x3, PAD : PAD + y3, :] = smoothed
    for x in range(x3):
        s3[x * y3 : (x + 1) * y3, :] = smoothed[x]
        line[x : x + 1, :] = jnp.sum(smoothed[x], axis=0, keepdims=True)
    copies = [send(line, lines.at[k - 1], (0, k)) for k in range(1, ny)]
    copies += [send(s3, p3.at[0], (0, 1)), send(s3, p3.at[1], (0, -1))]
    row, rows = PAD - 1, y2 + 2
    center, applied = block_stencil(
        from_v2, g2[1, 2 : x2 + 4, row : row + rows, :], 2, x2 + 2, row, rows, 32
    )
    x2_part[:, row : row + rows, :] = (
        center + g2[0, 2 : x2 + 4, row : row + rows, :] - mixed1(T2, applied, 32)
    )
    for copy in copies:
        copy.wait_recv()
    total = line[...]
    for k in range(1, ny):
        total += lines[k - 1]
    total *= 4.0 / math.sqrt(ny * y3)
    for x in range(x3):
        g3[4 + x, 0:1, :] = total[x : x + 1, :]
    fill_beside(g3, p3)
    receive_block(g3, l_g3, send_block(g3, b_g3, l_g3))

    low, high = PAD - y3, PAD + 2 * y3
    cell = lax.broadcasted_iota(jnp.int32, (1, 3 * y3, LANES), 1) + (my - 1) * y3
    inside = (cell >= 0) & (cell < ny * y3)
    w3[:, low:high, :] = g3[:, low:high, :] + jnp.where(inside, g3[:, 0:1, :], 0.0)

    def from_w3(x, xs, row, rows):
        return w3[x : x + xs, row : row + rows, :]

    for sweep in range(1, 4):
        x, xs = sweep, 8 + x3 - 2 * sweep
        row, rows = low + sweep, high - low - 2 * sweep
        center, applied = block_stencil(
            from_w3, k3[x : x + xs, row : row + rows, :], x, xs, row, rows, 16
        )
        value = center + g3[x : x + xs, row : row + rows, :] - mixed1(T3, applied, 16)
        if sweep < 3:
            w3[x : x + xs, row : row + rows, :] = value
        else:
            b3[:, row : row + rows, :] = value

    below = b3[...]
    mixed = mixed1(T2_below, below, 16)
    flat = ((x3 + 2) * 2 * PAD, LANES)
    e2[...] = spread_stacked((below - mixed).reshape(flat), last_up[...]).reshape(e2.shape)
    m2[...] = spread_stacked(mixed.reshape(flat), last_rise[...]).reshape(m2.shape)
    q2[...] = spread_stacked(mixed.reshape(flat), last_up[...]).reshape(q2.shape)

    def raised(m, q, c, i, s, t, row, rows):
        other_y = q[c, i, row + 2 * t - 1 : row + 2 * t - 1 + rows, :]
        other_x = q[c, i + 2 * s - 1, row : row + rows, :]
        return m[c, i, row : row + rows, :] - other_y - other_x

    for x in range(-1, x2 + 1):
        i, s = x // 2 + 1, x % 2
        for t in range(2):
            row, rows = PAD - t, y3 + 1
            cells = pl.ds(PAD - t, rows, stride=2)
            value = raised(m2, q2, 0, i, s, t, row, rows)
            w2[x + 1, cells, :] = (
                x2_part[x + 1, cells, :]
                + e2[0, i, row : row + rows, :]
                - g2[1, x + 3, cells, :] * value
            )

    below = w2[...]
    mixed = mixed1(T1_below, below, 32)
    flat = ((x2 + 2) * (y2 + 2 * PAD), LANES)
    shape = (x2 + 2, y2 + 2 * PAD, LANES)
    for field, matrix, target in (
        (below - mixed, up, e1),
        (mixed, rise_second, m1),
        (mixed, up, q1),
    ):
        children = spread_stacked(field.reshape(flat), matrix[...])
        for c in range(2):
            target[c] = children[:, c * LANES : (c + 1) * LANES].reshape(shape)
    for x in range(-1, x1 + 1):
        i, s = x // 2 + 1, x % 2
        for t in range(2):
            row, rows = PAD - t, y2 + 1
            cells = pl.ds(PAD - t, rows, stride=2)
            coefficient = g1[2, x + 3, cells, :]
            for c in range(2):
                value = raised(m1, q1, c, i, s, t, row, rows)
                w1[c, x + 1, cells, :] = (
                    x1_part[c, x + 1, cells, :]
                    + e1[c, i, row : row + rows, :]
                    - coefficient * value
                )

    below = [w1[c] for c in range(2)]
    mixed = mixed2(T0_below, below)
    own = slice(1, x1 + 1), slice(PAD, PAD + y1)
    for g in range(2):
        inner = (x1 * y1, LANES)
        for field, matrix, target in (
            ((below[g] - mixed[g])[own].reshape(inner), up, e0),
            (mixed[g][own].reshape(inner), rise_fine, m0),
        ):
            children = spread_stacked(field, matrix[...])
            for c in range(2):
                part = children[:, c * LANES : (c + 1) * LANES]
                target[2 * g + c, 1 : x1 + 1, PAD : PAD + y1, :] = part.reshape(x1, y1, LANES)
        children = spread_stacked(
            mixed[g].reshape((x1 + 2) * (y1 + 2 * PAD), LANES), up[...]
        )
        for c in range(2):
            part = children[:, c * LANES : (c + 1) * LANES]
            q0[2 * g + c] = part.reshape(x1 + 2, y1 + 2 * PAD, LANES)

    def finish_fine(step):
        i = step + 1
        for t in range(2):
            cells = pl.ds(t, y1, stride=2)
            coefficient = [a0[2 * step + s + 1, pl.ds(t, y1, stride=2), :] for s in range(2)]
            for c in range(4):
                for s in range(2):
                    value = raised(m0, q0, c, i, s, t, PAD, y1)
                    x = 2 * step + s
                    out[c, x, cells, :] = (
                        f0[c, x, cells, :]
                        + e0[c, i, PAD : PAD + y1, :]
                        - coefficient[s] * value
                    )

    steps(x1, finish_fine)
    for copy in started:
        copy.wait_send()


def per_device(nx, ny, source, fine, second, third, coarse, mixers, smoothers):
    x0, y0 = source.shape[1:3]
    x1, y1 = second.shape[:2]
    x2, y2 = third.shape[:2]
    x3, y3 = coarse.shape[:2]

    def padded(groups, xs, ys, h):
        return pltpu.VMEM((groups, xs + 2 * h, ys + 2 * PAD, LANES), F32)

    def vmem(*shape):
        return pltpu.VMEM(shape, F32)

    def faces(planes, near, xs):
        rows = max(xs, 8)
        return [
            vmem(2, planes, rows, LANES),
            vmem(2, planes, rows, LANES),
            vmem(4, near, LANES),
            vmem(4, near, LANES),
        ]

    def three(groups, xs, ys):
        return [vmem(groups, xs + 2, ys + 2 * PAD, LANES)] * 3

    double = pltpu.VMEM((2 * LANES, 2 * LANES), BF16)
    tall = pltpu.VMEM((2 * LANES, LANES), BF16)
    scratch = (
        [vmem(2, 4, 2, y0, LANES), vmem(2, 4, x0, LANES), vmem(4, x0, y0, LANES), vmem(x0 + 2, y0, LANES)]
        + [vmem(4, (x0 + 4) * (y0 + 2 * PAD), LANES)] * 2
        + [vmem(2, 4, x0 + 2 * PAD, LANES)]
        + [vmem(4, x1, y0, LANES)]
        + three(4, x1, y1)
        + faces(9, 8, x0)
        + [vmem(*second.shape), vmem(2, x1, y1, LANES), padded(3, x1, y1, 3), padded(2, x1, y1, 3)]
        + [vmem(2, x2, y1, LANES), vmem(2, x1 + 2, y1 + 2 * PAD, LANES)]
        + three(2, x2, y2)
        + [vmem(2, x1 + 2, y1 + 2 * PAD, LANES)]
        + faces(8, 8, x1)
        + [vmem(*third.shape), vmem(x2, y2, LANES), padded(2, x2, y2, 3)]
        + [vmem(x2 + 6, y2 + 2 * PAD, LANES), vmem(x3, y2, LANES)]
        + [vmem(x2 + 2, y2 + 2 * PAD, LANES)]
        + [vmem(1, x3 + 2, 2 * PAD, LANES)] * 3
        + [vmem(x2 + 2, y2 + 2 * PAD, LANES)]
        + faces(5, 16, x2)
        + [vmem(*coarse.shape), vmem(x3, y2, LANES)]
        + [vmem(x3 + 8, 24, LANES)] * 3
        + [vmem(x3 + 2, 2 * PAD, LANES)]
        + [vmem(x3 * y3, LANES), vmem(2, x3 * y3, LANES)] * 2
        + [vmem(2 * PAD, LANES), vmem(4, 2 * PAD, LANES)] * 2
        + [vmem(x3, LANES), vmem(ny - 1, x3, LANES)]
        + [vmem(64, LANES)]
        + [tall, double, double, double, pltpu.VMEM((LANES, LANES), BF16), tall, tall]
    )
    copies = 8 * 3 + 4 + 2 * 2 + (ny - 1) + 4 * 2
    scratch += [
        pltpu.SMEM(mixers.shape, F32),
        pltpu.SMEM(smoothers.shape, F32),
        pltpu.SemaphoreType.DMA((copies,)),
        pltpu.SemaphoreType.DMA((copies,)),
        pltpu.SemaphoreType.DMA((10,)),
    ]
    anywhere = pl.BlockSpec(memory_space=pl.ANY)
    return pl.pallas_call(
        functools.partial(kernel, nx, ny),
        out_shape=pltpu.VMEM(source.shape, F32),
        in_specs=[anywhere] * 7,
        out_specs=pl.BlockSpec(memory_space=pltpu.VMEM),
        scratch_shapes=scratch,
        compiler_params=pltpu.CompilerParams(
            collective_id=0, has_side_effects=True, vmem_limit_bytes=56 * 1024 * 1024
        ),
    )(source, fine, second, third, coarse, mixers, smoothers)


def solution(mesh):
    field, cells = P(None, "gx", "gy", None), P("gx", "gy", None)
    return jax.shard_map(
        functools.partial(per_device, mesh.shape["gx"], mesh.shape["gy"]),
        mesh=mesh,
        in_specs=(field, cells, cells, cells, cells, P(), P()),
        out_specs=field,
        check_vma=False,
    )
```
